512 devices in a mesh: img: 32 (over x_lo, z), blk: 16 (over x_hi, y, core).
Axes of the slice: x: 4 (x_hi: 2, x_lo: 2; x = x_hi * 2 + x_lo), y: 4, z: 16, core: 2. Of those that a mesh axis runs over, the one named last changes fastest.
Arguments:
- images: bfloat16 [32768, 4096], P(('img', 'blk')), may hold values from -16 to 16
- references: bfloat16 [256, 4096], P('blk'), may hold values from -1 to 1
- precision: float32 [32768], P(('img', 'blk')), may hold values from 0.05 to 0.5
- candidates: int32 [32768, 2], P(('img', 'blk')), may hold values from 0 to 255, as said below
Outputs:
- class_average: float32 [256, 4096], P('blk', 'img')
- log_evidence: float32 [32768], P(('img', 'blk'))
The draws below stay inside these ranges and needn't reach their ends.
Inputs may be any that keep to these rules, and one draw needn't show every extreme that they name: The 2 candidates of an image differ. Classes b * 16 to (b + 1) * 16 - 1 form owner block b. Among the 128 candidate entries of the images of one device, exactly 16 name classes of one owner block, chosen per device, and the other entries are spread over the other owner blocks as evenly as they divide.
All inputs are finite; a program needn't handle non-finite values.
Results may differ from the reference program's by a relative error of at most 0.0028.
Values may be sent and summed in bfloat16 or wider, within the bound.
A program may use at most 64 MiB of HBM per device.

```python
import math
import jax
import jax.numpy as jnp
from jax import lax

CYCLES = 32
ORDERS = 64
TURNS = 36
PICKS = 2
CLASS_DEV = 16
IMAGE_DEV = 64
FEATS = 4096
CLASSES = 256
IMAGES = 32768


def reference_bank(key):
    bank_key = jax.random.fold_in(key, 11)
    spread = 16.0 / math.sqrt(FEATS)
    values = jnp.clip(jax.random.normal(bank_key, (CLASSES, FEATS), jnp.float32), -4.0, 4.0) * spread
    return values.astype(jnp.bfloat16).astype(jnp.float32)


def candidate_table(key):
    table_key = jax.random.fold_in(key, 13)
    subkeys = jax.random.split(table_key, 4)
    group_count = IMAGES // IMAGE_DEV
    pair_count = IMAGE_DEV * PICKS
    owner_count = CLASSES // CLASS_DEV
    slot_count = 2 * pair_count // owner_count
    busiest = jax.random.randint(subkeys[0], (group_count, 1), 0, owner_count)
    ranking = jax.vmap(lambda one_key: jax.random.permutation(one_key, pair_count))(jax.random.split(subkeys[1], group_count))
    others = (ranking - slot_count) % max(owner_count - 1, 1)
    others = others + (others >= busiest).astype(jnp.int32)
    owner_ids = jnp.where(ranking < slot_count, busiest, others).reshape(group_count, IMAGE_DEV, 2)
    local_ids = jax.random.randint(subkeys[2], (group_count, IMAGE_DEV, 2), 0, CLASS_DEV)
    bumps = jax.random.randint(subkeys[3], (group_count, IMAGE_DEV), 1, CLASS_DEV)
    second = jnp.where(owner_ids[..., 0] == owner_ids[..., 1], (local_ids[..., 0] + bumps) % CLASS_DEV, local_ids[..., 1])
    local_ids = jnp.stack([local_ids[..., 0], second], axis=-1)
    return (owner_ids * CLASS_DEV + local_ids).reshape(IMAGES, PICKS).astype(jnp.int32)


def draw_references(key, part):
    return reference_bank(key).astype(jnp.bfloat16)


def draw_candidates(key, part):
    return candidate_table(key)


def draw_precision(key, part):
    key = jax.random.fold_in(key, 3)
    values = jnp.exp(jax.random.uniform(key, (IMAGES,), jnp.float32, math.log(0.05), math.log(0.5)))
    return values.astype(jnp.float32)


def draw_images(key, part):
    key = jax.random.fold_in(key, 5)
    subkeys = jax.random.split(key, 7)
    values = jnp.clip(jax.random.normal(subkeys[6], (IMAGES, FEATS), jnp.float32), -6.0, 6.0)
    return jnp.clip(values, -16.0, 16.0).astype(jnp.bfloat16)


def setup_inputs(seed: int = 0) -> dict:
    key_of = jax.random.split(jax.random.key(seed), 5)
    return {
        "images": draw_images(jax.random.fold_in(key_of[4], 71), 0),
        "references": draw_references(jax.random.fold_in(key_of[4], 71), 0),
        "precision": draw_precision(jax.random.fold_in(key_of[4], 71), 0),
        "candidates": draw_candidates(jax.random.fold_in(key_of[4], 71), 0),
    }


highest = lax.Precision.HIGHEST


def rotation_table():
    orders = jnp.arange(ORDERS, dtype=jnp.int32)
    turn_ids = jnp.arange(TURNS, dtype=jnp.int32)
    phases = (turn_ids[:, None] * orders[None, :]) % TURNS
    angles = phases.astype(jnp.float32) * (2.0 * math.pi / TURNS)
    return jnp.stack([jnp.cos(angles), -jnp.sin(angles)], axis=2).reshape(TURNS, 2 * ORDERS)


def align(image_rows, posterior, turn_table):
    block_rows = image_rows.shape[0]
    spectrum = jnp.dot(turn_table.T, posterior.reshape(TURNS, -1), precision=highest)
    spectrum = spectrum.reshape(ORDERS, 2, PICKS, block_rows)
    real_part = jnp.transpose(spectrum[:, 0], (2, 1, 0))[..., None]
    imag_part = jnp.transpose(spectrum[:, 1], (2, 1, 0))[..., None]
    pieces = image_rows.reshape(block_rows, ORDERS, 2, CYCLES)
    real_in = pieces[:, None, :, 0, :]
    imag_in = pieces[:, None, :, 1, :]
    real_out = real_in * real_part - imag_in * imag_part
    imag_out = real_in * imag_part + imag_in * real_part
    return jnp.stack([real_out, imag_out], axis=3).reshape(block_rows * PICKS, FEATS)


def reference(images, references, precision, candidates):
    turn_table = rotation_table()
    ref_rows = references.astype(jnp.float32)
    pieces = ref_rows.reshape(CLASSES, ORDERS, 2, CYCLES)
    swapped = jnp.stack([-pieces[:, :, 1, :], pieces[:, :, 0, :]], axis=2)
    stacked = jnp.stack([pieces, swapped]).reshape(2, CLASSES, ORDERS, 2 * CYCLES)
    squares = jnp.sum(ref_rows * ref_rows, axis=1)
    group_count = IMAGES // IMAGE_DEV

    def one_block(loop_state, inputs):
        class_sum, class_weight = loop_state
        block_rows, block_prec, block_picks = inputs
        image_rows = block_rows.astype(jnp.float32)
        spectra = image_rows.reshape(IMAGE_DEV, ORDERS, 2 * CYCLES)
        harmonic = jnp.einsum("hcmk,imk->mhci", stacked, spectra, precision=highest)
        turned = jnp.dot(turn_table, harmonic.reshape(2 * ORDERS, -1), precision=highest)
        turned = turned.reshape(TURNS, CLASSES, IMAGE_DEV)
        scores = block_prec[None, None, :] * (turned - 0.5 * squares[None, :, None])
        row_peak = jnp.max(scores, axis=(0, 1))
        evidence = row_peak + jnp.log(jnp.sum(jnp.exp(scores - row_peak[None, None, :]), axis=(0, 1)))
        index_table = jnp.broadcast_to(block_picks.T[None], (TURNS, PICKS, IMAGE_DEV))
        chosen = jnp.take_along_axis(scores, index_table, axis=1)
        pick_peak = jnp.max(chosen, axis=(0, 1))
        unnorm = jnp.exp(chosen - pick_peak[None, None, :])
        posterior = unnorm / jnp.sum(unnorm, axis=(0, 1))[None, None, :]
        weight_share = jnp.sum(posterior, axis=0)
        rounded = align(image_rows, posterior, turn_table).astype(jnp.bfloat16)
        rounded = lax.optimization_barrier(rounded)
        flat_picks = block_picks.reshape(-1)
        class_sum = class_sum + jax.ops.segment_sum(rounded.astype(jnp.float32), flat_picks, num_segments=CLASSES)
        class_weight = class_weight + jax.ops.segment_sum(weight_share.T.reshape(-1), flat_picks, num_segments=CLASSES)
        return (class_sum, class_weight), evidence

    start = (jnp.zeros((CLASSES, FEATS), jnp.float32), jnp.zeros((CLASSES,), jnp.float32))
    inputs = (images.reshape(group_count, IMAGE_DEV, FEATS), precision.reshape(group_count, IMAGE_DEV), candidates.reshape(group_count, IMAGE_DEV, PICKS))
    (class_sum, class_weight), evidence = lax.scan(one_block, start, inputs)
    class_average = class_sum / (1.0 + class_weight)[:, None]
    return class_average, evidence.reshape(IMAGES)
```

```python
import math

import jax
import jax.numpy as jnp
import ml_dtypes
import numpy as np
from jax import lax
from jax.experimental import pallas as pl
from jax.experimental.pallas import tpu as pltpu
from jax.sharding import PartitionSpec as P

CYCLES = 32
ORDERS = 64
TURNS = 36
FEATS = 4096
LANES = 128
MESH = pl.DeviceIdType.MESH
F32 = jnp.float32
BF16 = jnp.bfloat16


def spread_table():
    feats = np.arange(FEATS)
    order = feats // (2 * CYCLES)
    turns = np.arange(TURNS)
    angle = 2.0 * math.pi / TURNS * ((turns[:, None] * order[None, :]) % TURNS)
    out = np.zeros((16, 128, 512), np.float32)
    for part, values in enumerate((np.cos(angle), -np.sin(angle))):
        values = values.astype(np.float32).reshape(TURNS, 16, 256).transpose(1, 0, 2)
        high = values.astype(ml_dtypes.bfloat16).astype(np.float32)
        low = values - high
        cols = slice(part * 256, part * 256 + 256)
        out[:, 0:36, cols] = high
        out[:, 40:76, cols] = high
        out[:, 80:116, cols] = low
    return out.astype(ml_dtypes.bfloat16)


def weighted(pairs):
    total = None
    for coef, value in pairs:
        if abs(coef) < 1e-12:
            continue
        if abs(coef - 1.0) < 1e-12:
            term = value
        elif abs(coef + 1.0) < 1e-12:
            term = -value
        else:
            term = value * np.float32(coef)
        total = term if total is None else total + term
    return total


def turns_of(a, b):
    def cos(k, s):
        return math.cos(2.0 * math.pi * (k * s % 36) / 36.0)

    def sin(k, s):
        return math.sin(2.0 * math.pi * (k * s % 36) / 36.0)

    even_c, odd_c, even_s, odd_s = {}, {}, {}, {}
    for s in range(5):
        p = weighted([(cos(k, s), a[k]) for k in range(0, 19, 4)])
        q = weighted([(cos(k, s), a[k]) for k in range(2, 19, 4)])
        even_c[s], even_c[9 - s] = p + q, p - q
    for s in range(9):
        odd_c[s] = weighted([(cos(k, s), a[k]) for k in range(1, 18, 2)])
    for s in range(1, 5):
        p = weighted([(sin(k, s), b[k]) for k in range(4, 17, 4)])
        q = weighted([(sin(k, s), b[k]) for k in range(2, 17, 4)])
        even_s[s], even_s[9 - s] = p + q, q - p
    for s in range(1, 10):
        odd_s[s] = weighted([(sin(k, s), b[k]) for k in range(1, 18, 2)])
    x = [None] * 36
    for s in range(10):
        if s < 9:
            c_lo, c_hi = even_c[s] + odd_c[s], even_c[s] - odd_c[s]
        else:
            c_lo = c_hi = even_c[9]
        if s == 0:
            x[0], x[18] = c_lo, c_hi
        elif s == 9:
            x[9], x[27] = c_lo - odd_s[9], c_lo + odd_s[9]
        else:
            s_lo, s_hi = even_s[s] + odd_s[s], odd_s[s] - even_s[s]
            x[s], x[36 - s] = c_lo - s_lo, c_lo + s_lo
            x[18 - s], x[18 + s] = c_hi - s_hi, c_hi + s_hi
    return x


def tree(op, values):
    values = list(values)
    while len(values) > 1:
        nxt = [op(values[i], values[i + 1]) for i in range(0, len(values) - 1, 2)]
        if len(values) % 2:
            nxt.append(values[-1])
        values = nxt
    return values[0]


def add(p, q):
    return p + q


def dot_nt(a, b, **kw):
    return lax.dot_general(a, b, (((1,), (1,)), ((), ())), preferred_element_type=F32, **kw)


def dot_nn(a, b):
    return jnp.dot(a, b, preferred_element_type=F32)


def kernel(
    images, refs, aux, table, avg_out, evid_out,
    G, IM, IMS, FI, F, AUXS, CHX, CHS, PT, PP, TE, OH, SA, RA, SB, RB, TA, R2A, TB, R2B,
    UZ, SZ, RZ, W0, RW0, W1, RW1, W2, RW2, LS, LR,
    loc, ags, agr, sibs, sibr, s1s, s1r, s2s, s2r, zs, zr, ws, wr,
):
    img, blk = lax.axis_index("img"), lax.axis_index("blk")
    z, x_lo = img % 16, img // 16
    core, y, x_hi = blk % 2, (blk // 2) % 4, blk // 8
    x = x_hi * 2 + x_lo
    q_me = x_hi * 4 + y

    def dev(x_, y_, z_, c_):
        return ((x_ % 2) * 16 + z_, (x_ // 2) * 8 + y_ * 2 + c_)

    sib = dev(x, y, z, 1 - core)
    y_up, y_dn = (y + 1) % 4, (y + 3) % 4
    up, down = dev(x, y_up, z, core), dev(x, y_dn, z, core)
    x_opp, x_same = 3 - x, x_hi * 2 + 1 - x_lo
    opp, same = dev(x_opp, y, z, core), dev(x_same, y, z, core)

    def at_y(d):
        return dev(x, (y + d) % 4, z, core)

    def at_x(d):
        return dev((x + d) % 4, y, z, core)

    def at_z(d):
        return dev(x, y, (z + d) % 16, core)

    sent = []

    def send(src, dst, ssem, rsem, to):
        copy = pltpu.make_async_remote_copy(
            src_ref=src, dst_ref=dst, send_sem=ssem, recv_sem=rsem, device_id=to, device_id_type=MESH
        )
        copy.start()
        sent.append(copy)

    def arrived(dst, rsem):
        pltpu.make_async_copy(dst, dst, rsem).wait()

    mine_rows = pl.ds(pl.multiple_of(core * 64, 64), 64)
    own_im = pltpu.make_async_copy(images, IM.at[mine_rows], loc.at[0])
    own_im.start()
    own_g = pltpu.make_async_copy(refs, G.at[pl.ds(pl.multiple_of(q_me * 16, 16), 16)], loc.at[1])
    own_g.start()
    own_t = pltpu.make_async_copy(table, TE, loc.at[2])
    own_t.start()

    barrier = pltpu.get_barrier_semaphore()
    partners = [sib] + [at_y(d) for d in range(1, 4)] + [at_x(d) for d in range(1, 4)]
    partners += [at_z(d) for d in range(1, 16)]
    for to in partners:
        pl.semaphore_signal(barrier, inc=1, device_id=to, device_id_type=MESH)
    pl.semaphore_wait(barrier, len(partners))

    def piece(q, h):
        return G.at[pl.ds(pl.multiple_of(q * 16, 16), 16), pl.ds(pl.multiple_of(h * 2048, 2048), 2048)]

    def own_piece(h):
        return refs.at[:, pl.ds(pl.multiple_of(h * 2048, 2048), 2048)]

    h = x_lo
    col, far = x_hi * 4, (1 - x_hi) * 4
    y_far = (y + 2) % 4

    def give(n, q, hh, to, src=None):
        send(piece(q, hh) if src is None else src, piece(q, hh), ags.at[n], agr.at[q, hh], to)

    def got(q, hh):
        arrived(piece(q, hh), agr.at[q, hh])

    give(0, q_me, 0, up, own_piece(0))
    give(1, q_me, 1, down, own_piece(1))
    give(2, q_me, h, opp, own_piece(h))
    give(3, q_me, 1, up, own_piece(1))
    give(4, q_me, 0, down, own_piece(0))
    send(images, IM.at[mine_rows], sibs.at[0], sibr.at[0], sib)
    send(aux, AUXS, sibs.at[1], sibr.at[1], sib)
    own_im.wait()
    arrived(IM.at[pl.ds(pl.multiple_of((1 - core) * 64, 64), 64)], sibr.at[0])
    arrived(AUXS, sibr.at[1])

    row = lax.broadcasted_iota(jnp.int32, (128, 128), 0)
    lane = lax.broadcasted_iota(jnp.int32, (128, 128), 1)

    def swap(src, dst):
        first = dst % 64 < 32
        return jnp.where(first & (src == dst + 32), 1.0, jnp.where((~first) & (src == dst - 32), -1.0, 0.0))

    eye = jnp.where(row == lane, 1.0, 0.0)
    rows_of = jnp.concatenate([eye, swap(lane, row)], axis=0).astype(BF16)
    cols_of = swap(row, lane).astype(BF16)

    def prepare(first, count, half):
        def step(n, carry):
            t = first + n
            block = IM[:, pl.ds(pl.multiple_of(t * 128, 128), 128)]
            both = dot_nt(rows_of, block)
            j = t - 18 * half
            sign = jnp.where(j < 9, 1.0, -1.0).astype(F32)
            FI[j, half * 128 : half * 128 + 128, 0:128] = both[0:128].astype(BF16)
            FI[j, half * 128 : half * 128 + 128, 128:256] = (both[128:256] * sign).astype(BF16)
            IMS[:, pl.ds(pl.multiple_of(t * 128, 128), 128)] = dot_nn(block, cols_of).astype(BF16)
            return carry

        lax.fori_loop(0, count, step, 0)

    prepare(0, 6, 0)
    got(col + y_dn, 0)
    give(5, col + y_dn, 0, up)
    got(col + y_up, 1)
    give(6, col + y_up, 1, down)
    prepare(6, 6, 0)
    got(col + y_dn, 1)
    got(col + y_up, 0)
    give(7, col + y_dn, h, opp)
    give(8, col + y_up, h, opp)
    got(far + y, 1 - h)
    give(9, far + y, 1 - h, same)
    prepare(12, 6, 0)
    got(col + y_far, 0)
    got(col + y_far, 1)
    give(10, col + y_far, h, opp)
    prepare(18, 7, 1)
    got(far + y_dn, 1 - h)
    give(11, far + y_dn, 1 - h, same)
    got(far + y_up, 1 - h)
    give(12, far + y_up, 1 - h, same)
    prepare(25, 7, 1)
    got(far + y_far, 1 - h)
    give(13, far + y_far, 1 - h, same)

    right = lax.broadcasted_iota(jnp.int32, (8, 128), 1) >= 64
    auxc = jnp.where(right == (core == 1), aux[...], AUXS[...])
    precision = auxc[0:1, :]
    class_id = ((row // 16) * 32 + core * 16 + row % 16).astype(F32)
    picks = [auxc[1:2, :] == class_id, auxc[2:3, :] == class_id]
    for k in range(2):
        OH[:, k * 128 : k * 128 + 128] = jnp.where(picks[k], 1.0, 0.0).astype(BF16)
    PT[...] = jnp.zeros_like(PT)

    for d in (0, 1, 2, 3):
        got(far + (y + d) % 4, h)
    own_g.wait()

    low = (lax.broadcasted_iota(jnp.int32, (128, 256), 1) % 128) < 64
    for j in range(18):
        left = G[:, j * 128 : j * 128 + 128]
        if j < 14:
            tile = jnp.concatenate([left, G[:, (18 + j) * 128 : (18 + j) * 128 + 128]], axis=1)
            keep, right_side = low, FI[j]
        else:
            tile, keep, right_side = left, low[:, 0:128], FI[j, 0:128, :]
        zero = jnp.zeros_like(tile)
        stacked = jnp.concatenate([jnp.where(keep, tile, zero), jnp.where(keep, zero, tile)], axis=0)
        out = dot_nn(stacked, right_side)
        even, odd = out[0:128], out[128:256]
        k_even, k_odd = (2 * j if j <= 9 else 36 - 2 * j), (2 * j + 1 if j <= 8 else 35 - 2 * j)
        if j <= 9:
            F[k_even] = even[:, 0:128]
        else:
            F[k_even] += even[:, 0:128]
        if 0 < k_even < 18:
            if j <= 9:
                F[18 + k_even] = even[:, 128:256]
            else:
                F[18 + k_even] += even[:, 128:256]
        if j <= 8:
            F[k_odd] = odd[:, 0:128]
            F[18 + k_odd] = odd[:, 128:256]
        else:
            F[k_odd] += odd[:, 0:128]
            F[18 + k_odd] += odd[:, 128:256]

    square = jnp.zeros((128, 128), F32)
    for t in range(32):
        value = G[:, t * 128 : t * 128 + 128].astype(F32)
        square = square + value * value
    F[36] = jnp.broadcast_to(0.5 * jnp.sum(square, axis=1, keepdims=True), (128, 128))

    even_row = lax.broadcasted_iota(jnp.int32, (8, 128), 0) % 2 == 0

    def choose(kk, carry):
        f = F[kk]
        parts = []
        for k in range(2):
            kept = jnp.where(picks[k], f, 0.0)
            total = tree(add, [kept[n * 8 : n * 8 + 8] for n in range(16)])
            parts.append(total + pltpu.roll(total, 1, 0))
        both = jnp.where(even_row, parts[0], parts[1])
        both = both + pltpu.roll(both, 2, 0)
        CHX[kk] = both + pltpu.roll(both, 4, 0)
        return carry

    lax.fori_loop(0, 37, choose, 0)
    send(CHX, CHS, sibs.at[2], sibr.at[2], sib)
    arrived(CHS, sibr.at[2])

    coefs = [CHX[k] + CHS[k] for k in range(37)]
    turned = turns_of(coefs[0:19], [None] + coefs[19:36])
    scores = [precision * (v - coefs[36]) for v in turned]
    peak = tree(jnp.maximum, scores)
    peak = jnp.maximum(peak, jnp.where(even_row, pltpu.roll(peak, 7, 0), pltpu.roll(peak, 1, 0)))
    exps = [jnp.exp(v - peak) for v in scores]
    total = tree(add, exps)
    total = total + jnp.where(even_row, pltpu.roll(total, 7, 0), pltpu.roll(total, 1, 0))
    posterior = [v / total for v in exps]
    share = tree(add, posterior)
    for s in range(TURNS):
        high = posterior[s].astype(BF16).astype(F32)
        rest = posterior[s] - high
        for k in range(2):
            PT[k, s : s + 1, :] = high[k : k + 1]
            PT[k, 40 + s : 41 + s, :] = rest[k : k + 1]
            PT[k, 80 + s : 81 + s, :] = high[k : k + 1]
    for k in range(2):
        PP[k * 128 : k * 128 + 128, :] = PT[k].T.astype(BF16)
    own_t.wait()

    onehot = OH[...]

    def sums(x_half, second):
        def step(v, carry):
            u = x_half * 8 + second * 4 + v
            lanes = pl.ds(pl.multiple_of(u * 256, 256), 256)
            out_lanes = pl.ds(pl.multiple_of(v * 256, 256), 256)
            factor = dot_nn(PP[...], TE[u])
            straight, turned_in = IM[:, lanes].astype(F32), IMS[:, lanes].astype(F32)
            rows = [
                (
                    straight * factor[k * 128 : k * 128 + 128, 0:256]
                    - turned_in * factor[k * 128 : k * 128 + 128, 256:512]
                ).astype(BF16)
                for k in range(2)
            ]
            out = dot_nn(onehot, jnp.concatenate(rows, axis=0)).astype(BF16)
            for q in range(8):
                block = out[q * 16 : q * 16 + 16]
                if second:
                    SB[(q // 4) * 2 + x_half, q % 4, :, out_lanes] = block
                else:
                    SA[x_half, q % 4, q // 4, :, out_lanes] = block
            return carry

        lax.fori_loop(0, 4, step, 0)

    for x_half in range(2):
        sums(x_half, 0)
        for d in range(1, 4):
            n = x_half * 3 + d - 1
            send(SA.at[x_half, (y + d) % 4], RA.at[d - 1, x_half], s1s.at[n], s1r.at[n], at_y(d))
    for x_half in range(2):
        sums(x_half, 1)
    for d in range(1, 4):
        n = 5 + d
        send(SB.at[(x + d) % 4], RB.at[d - 1], s1s.at[n], s1r.at[n], at_x(d))

    shares = jnp.concatenate(
        [jnp.broadcast_to(share[0:1], (8, 128)), jnp.broadcast_to(share[1:2], (8, 128))], axis=1
    )
    W0[...] = dot_nt(shares, onehot.astype(F32), precision=lax.Precision.HIGHEST)
    for d in range(1, 16):
        send(W0, RW0.at[d - 1], ws.at[d - 1], wr.at[d - 1], at_z(d))

    def block_scores(n, carry):
        run_peak, run_total = carry
        rows = pl.ds(pl.multiple_of(n * 8, 8), 8)
        f = [F[k, rows, :] for k in range(37)]
        turned = turns_of(f[0:19], [None] + f[19:36])
        scores = [precision * (v - f[36]) for v in turned]
        new_peak = jnp.maximum(run_peak, tree(jnp.maximum, scores))
        total = tree(add, [jnp.exp(v - new_peak) for v in scores])
        return new_peak, run_total * jnp.exp(run_peak - new_peak) + total

    start = (jnp.full((8, 128), -jnp.inf, F32), jnp.zeros((8, 128), F32))
    run_peak, run_total = lax.fori_loop(0, 16, block_scores, start)
    peak = jnp.max(run_peak, axis=0, keepdims=True)
    total = jnp.sum(run_total * jnp.exp(run_peak - peak), axis=0, keepdims=True)
    LS[0:8] = jnp.broadcast_to(peak, (8, 128))
    LS[8:16] = jnp.broadcast_to(total, (8, 128))
    send(LS, LR, sibs.at[3], sibr.at[3], sib)

    for d in range(1, 16):
        arrived(RW0.at[d - 1], wr.at[d - 1])
    W1[...] = tree(add, [W0[...]] + [RW0[d] for d in range(15)])
    for d in range(1, 4):
        send(W1, RW1.at[d - 1], ws.at[14 + d], wr.at[14 + d], at_y(d))

    for d in range(1, 4):
        for x_half in range(2):
            arrived(RA.at[d - 1, x_half], s1r.at[x_half * 3 + d - 1])
    for x_half in range(2):
        for x_top in range(2):
            total = SA[x_half, y, x_top].astype(F32)
            for d in range(3):
                total = total + RA[d, x_half, x_top].astype(F32)
            TA[x_top * 2 + x_half] = total
    for d in range(1, 4):
        send(TA.at[(x + d) % 4], R2A.at[d - 1], s2s.at[d - 1], s2r.at[d - 1], at_x(d))
    for d in range(1, 4):
        arrived(RB.at[d - 1], s1r.at[5 + d])
    for y_to in range(4):
        total = SB[x, y_to].astype(F32)
        for d in range(3):
            total = total + RB[d, y_to].astype(F32)
        TB[y_to] = total
    for d in range(1, 4):
        send(TB.at[(y + d) % 4], R2B.at[d - 1], s2s.at[2 + d], s2r.at[2 + d], at_y(d))

    for d in range(1, 4):
        arrived(RW1.at[d - 1], wr.at[14 + d])
    W2[...] = tree(add, [W1[...]] + [RW1[d] for d in range(3)])
    for d in range(1, 4):
        send(W2, RW2.at[d - 1], ws.at[17 + d], wr.at[17 + d], at_x(d))

    arrived(LR, sibr.at[3])
    peak = jnp.maximum(LS[0:8], LR[0:8])
    total = LS[8:16] * jnp.exp(LS[0:8] - peak) + LR[8:16] * jnp.exp(LR[0:8] - peak)
    evidence = peak + jnp.log(total)
    evid_out[...] = jnp.where(core == 0, evidence[0:1, 0:64], evidence[0:1, 64:128])

    for d in range(1, 4):
        arrived(R2A.at[d - 1], s2r.at[d - 1])
    total = TA[x] + R2A[0] + R2A[1] + R2A[2]
    for n in range(8):
        UZ[n] = total[:, n * 128 : n * 128 + 128]
    for d in range(1, 4):
        arrived(R2B.at[d - 1], s2r.at[2 + d])
    total = TB[y] + R2B[0] + R2B[1] + R2B[2]
    for n in range(8):
        UZ[8 + n] = total[:, n * 128 : n * 128 + 128]
    SZ[...] = UZ[...].astype(BF16)
    for d in range(1, 16):
        send(SZ.at[(z + d) % 16], RZ.at[d - 1], zs.at[d - 1], zr.at[d - 1], at_z(d))

    for d in range(1, 4):
        arrived(RW2.at[d - 1], wr.at[17 + d])
    weight = tree(add, [W2[...]] + [RW2[d] for d in range(3)])
    pick = lane[0:16] == row[0:16] + q_me * 16
    weight = jnp.sum(jnp.where(pick, jnp.broadcast_to(weight[0:1], (16, 128)), 0.0), axis=1, keepdims=True)
    for d in range(1, 16):
        arrived(RZ.at[d - 1], zr.at[d - 1])
    total = tree(add, [UZ[z]] + [RZ[d].astype(F32) for d in range(15)])
    avg_out[...] = total / (1.0 + weight)
    for copy in sent:
        copy.wait_send()


def body(images, references, precision, candidates):
    rows = jnp.concatenate(
        [precision.reshape(1, 64), candidates.T.astype(F32), jnp.zeros((5, 64), F32)], axis=0
    )
    aux = jnp.concatenate([rows, rows], axis=1)
    table = jnp.asarray(spread_table())
    anywhere = pl.BlockSpec(memory_space=pl.ANY)
    vmem = pl.BlockSpec(memory_space=pltpu.VMEM)
    dma = pltpu.SemaphoreType.DMA
    scratch = [
        pltpu.VMEM((128, 4096), BF16),
        pltpu.VMEM((128, 4096), BF16),
        pltpu.VMEM((128, 4096), BF16),
        pltpu.VMEM((18, 256, 256), BF16),
        pltpu.VMEM((37, 128, 128), F32),
        pltpu.VMEM((8, 128), F32),
        pltpu.VMEM((37, 8, 128), F32),
        pltpu.VMEM((37, 8, 128), F32),
        pltpu.VMEM((2, 128, 128), F32),
        pltpu.VMEM((256, 128), BF16),
        pltpu.VMEM((16, 128, 512), BF16),
        pltpu.VMEM((128, 256), BF16),
        pltpu.VMEM((2, 4, 2, 16, 1024), BF16),
        pltpu.VMEM((3, 2, 2, 16, 1024), BF16),
        pltpu.VMEM((4, 4, 16, 1024), BF16),
        pltpu.VMEM((3, 4, 16, 1024), BF16),
        pltpu.VMEM((4, 16, 1024), F32),
        pltpu.VMEM((3, 16, 1024), F32),
        pltpu.VMEM((4, 16, 1024), F32),
        pltpu.VMEM((3, 16, 1024), F32),
        pltpu.VMEM((16, 16, 128), F32),
        pltpu.VMEM((16, 16, 128), BF16),
        pltpu.VMEM((15, 16, 128), BF16),
        pltpu.VMEM((8, 128), F32),
        pltpu.VMEM((15, 8, 128), F32),
        pltpu.VMEM((8, 128), F32),
        pltpu.VMEM((3, 8, 128), F32),
        pltpu.VMEM((8, 128), F32),
        pltpu.VMEM((3, 8, 128), F32),
        pltpu.VMEM((16, 128), F32),
        pltpu.VMEM((16, 128), F32),
        dma((3,)),
        dma((14,)),
        dma((8, 2)),
        dma((4,)),
        dma((4,)),
        dma((9,)),
        dma((9,)),
        dma((6,)),
        dma((6,)),
        dma((15,)),
        dma((15,)),
        dma((21,)),
        dma((21,)),
    ]
    average, evidence = pl.pallas_call(
        kernel,
        out_shape=(jax.ShapeDtypeStruct((16, 128), F32), jax.ShapeDtypeStruct((1, 64), F32)),
        in_specs=[anywhere, anywhere, vmem, anywhere],
        out_specs=(vmem, vmem),
        scratch_shapes=scratch,
        compiler_params=pltpu.CompilerParams(
            collective_id=0, has_side_effects=True, vmem_limit_bytes=40 * 1024 * 1024
        ),
    )(images, references, aux, table)
    return average, evidence.reshape(64)


def solution(mesh):
    in_specs = (P(("img", "blk"), None), P("blk", None), P(("img", "blk")), P(("img", "blk"), None))
    out_specs = (P("blk", "img"), P(("img", "blk")))
    return jax.shard_map(body, mesh=mesh, in_specs=in_specs, out_specs=out_specs, check_vma=False)
```

```python
import math

import jax
import jax.numpy as jnp
import ml_dtypes
import numpy as np
from jax import lax
from jax.experimental import pallas as pl
from jax.experimental.pallas import tpu as pltpu
from jax.sharding import PartitionSpec as P

CYCLES = 32
ORDERS = 64
TURNS = 36
FEATS = 4096
LANES = 128
MESH = pl.DeviceIdType.MESH
F32 = jnp.float32
BF16 = jnp.bfloat16


def spread_table():
    feats = np.arange(FEATS)
    order = feats // (2 * CYCLES)
    turns = np.arange(TURNS)
    angle = 2.0 * math.pi / TURNS * ((turns[:, None] * order[None, :]) % TURNS)
    out = np.zeros((16, 128, 512), np.float32)
    for part, values in enumerate((np.cos(angle), -np.sin(angle))):
        values = values.astype(np.float32).reshape(TURNS, 16, 256).transpose(1, 0, 2)
        high = values.astype(ml_dtypes.bfloat16).astype(np.float32)
        low = values - high
        cols = slice(part * 256, part * 256 + 256)
        out[:, 0:36, cols] = high
        out[:, 40:76, cols] = high
        out[:, 80:116, cols] = low
    return out.astype(ml_dtypes.bfloat16)


def weighted(pairs):
    total = None
    for coef, value in pairs:
        if abs(coef) < 1e-12:
            continue
        if abs(coef - 1.0) < 1e-12:
            term = value
        elif abs(coef + 1.0) < 1e-12:
            term = -value
        else:
            term = value * np.float32(coef)
        total = term if total is None else total + term
    return total


def turns_of(a, b):
    def cos(k, s):
        return math.cos(2.0 * math.pi * (k * s % 36) / 36.0)

    def sin(k, s):
        return math.sin(2.0 * math.pi * (k * s % 36) / 36.0)

    even_c, odd_c, even_s, odd_s = {}, {}, {}, {}
    for s in range(5):
        p = weighted([(cos(k, s), a[k]) for k in range(0, 19, 4)])
        q = weighted([(cos(k, s), a[k]) for k in range(2, 19, 4)])
        even_c[s], even_c[9 - s] = p + q, p - q
    for s in range(9):
        odd_c[s] = weighted([(cos(k, s), a[k]) for k in range(1, 18, 2)])
    for s in range(1, 5):
        p = weighted([(sin(k, s), b[k]) for k in range(4, 17, 4)])
        q = weighted([(sin(k, s), b[k]) for k in range(2, 17, 4)])
        even_s[s], even_s[9 - s] = p + q, q - p
    for s in range(1, 10):
        odd_s[s] = weighted([(sin(k, s), b[k]) for k in range(1, 18, 2)])
    x = [None] * 36
    for s in range(10):
        if s < 9:
            c_lo, c_hi = even_c[s] + odd_c[s], even_c[s] - odd_c[s]
        else:
            c_lo = c_hi = even_c[9]
        if s == 0:
            x[0], x[18] = c_lo, c_hi
        elif s == 9:
            x[9], x[27] = c_lo - odd_s[9], c_lo + odd_s[9]
        else:
            s_lo, s_hi = even_s[s] + odd_s[s], odd_s[s] - even_s[s]
            x[s], x[36 - s] = c_lo - s_lo, c_lo + s_lo
            x[18 - s], x[18 + s] = c_hi - s_hi, c_hi + s_hi
    return x


def tree(op, values):
    values = list(values)
    while len(values) > 1:
        nxt = [op(values[i], values[i + 1]) for i in range(0, len(values) - 1, 2)]
        if len(values) % 2:
            nxt.append(values[-1])
        values = nxt
    return values[0]


def add(p, q):
    return p + q


def dot_nt(a, b, **kw):
    return lax.dot_general(a, b, (((1,), (1,)), ((), ())), preferred_element_type=F32, **kw)


def dot_nn(a, b):
    return jnp.dot(a, b, preferred_element_type=F32)


def kernel(
    images, refs, prec, cand, table, avg_out, evid_out,
    G, IM, IMS, FI, F, PIN, CIN, AUX, AUXS, CHX, CHS, PT, PP, TE, OH, SA, RA, SB, RB, TA, R2A, TB, R2B,
    UZ, SZ, RZ, W0, RW0, W1, RW1, W2, RW2, LS, LR,
    loc, tok, ags, agr, sibs, sibr, s1s, s1r, s2s, s2r, zs, zr, ws, wr,
):
    img, blk = lax.axis_index("img"), lax.axis_index("blk")
    z, x_lo = img % 16, img // 16
    core, y, x_hi = blk % 2, (blk // 2) % 4, blk // 8
    x = x_hi * 2 + x_lo
    q_me = x_hi * 4 + y

    def dev(x_, y_, z_, c_):
        return ((x_ % 2) * 16 + z_, (x_ // 2) * 8 + y_ * 2 + c_)

    sib = dev(x, y, z, 1 - core)
    x_opp, x_same = 3 - x, x_hi * 2 + 1 - x_lo
    same = dev(x_same, y, z, core)

    def at_y(d):
        return dev(x, (y + d) % 4, z, core)

    def at_x(d):
        return dev((x + d) % 4, y, z, core)

    def at_z(d):
        return dev(x, y, (z + d) % 16, core)

    sent = []

    def send(src, dst, ssem, rsem, to):
        copy = pltpu.make_async_remote_copy(
            src_ref=src, dst_ref=dst, send_sem=ssem, recv_sem=rsem, device_id=to, device_id_type=MESH
        )
        copy.start()
        sent.append(copy)

    def arrived(dst, rsem):
        pltpu.make_async_copy(dst, dst, rsem).wait()

    mine_rows = pl.ds(pl.multiple_of(core * 64, 64), 64)
    own_p = pltpu.make_async_copy(prec, PIN, loc.at[3])
    own_p.start()
    own_c = pltpu.make_async_copy(cand, CIN, loc.at[4])
    own_c.start()
    own_g = pltpu.make_async_copy(refs, G.at[pl.ds(pl.multiple_of(q_me * 16, 16), 16)], loc.at[1])
    own_g.start()
    own_im = pltpu.make_async_copy(images, IM.at[mine_rows], loc.at[0])
    own_im.start()
    own_t = pltpu.make_async_copy(table, TE, loc.at[2])
    own_t.start()

    barrier = pltpu.get_barrier_semaphore()
    partners = [dev(x_opp, (y + d) % 4, z, core) for d in range(1, 4)]
    partners += [at_y(d) for d in range(1, 4)] + [at_x(d) for d in range(1, 4)]
    partners += [at_z(1), at_z(15), sib]
    for to in partners:
        pl.semaphore_signal(barrier, inc=1, device_id=to, device_id_type=MESH)
    own_p.wait()
    own_c.wait()
    mine = jnp.concatenate([PIN[...], CIN[...].astype(F32)], axis=0)
    AUX[0:3, :] = jnp.concatenate([mine, mine], axis=1)
    AUX[3:8, :] = jnp.zeros((5, 128), F32)
    pl.semaphore_wait(barrier, len(partners))

    def token(n):
        for d in (1 << n, 16 - (1 << n)):
            pl.semaphore_signal(tok.at[n], inc=1, device_id=at_z(d), device_id_type=MESH)

    def rows_at(q):
        return pl.ds(pl.multiple_of(q * 16, 16), 16)

    def piece(q, hh):
        return G.at[rows_at(q), pl.ds(pl.multiple_of(hh * 2048, 2048), 2048)]

    h = x_lo
    col, far = x_hi * 4, (1 - x_hi) * 4
    order = (0, 1, 3, 2)

    def near_q(d):
        return col + (y + d) % 4

    def far_q(d):
        return far + (y + d) % 4

    send(AUX, AUXS, sibs.at[1], sibr.at[1], sib)
    send(images, IM.at[mine_rows], sibs.at[0], sibr.at[0], sib)
    own_half = refs.at[:, pl.ds(pl.multiple_of(h * 2048, 2048), 2048)]
    for n, d in enumerate(order):
        send(own_half, piece(q_me, h), ags.at[n], agr.at[q_me, h], dev(x_opp, (y + d) % 4, z, core))
    for n, d in enumerate((1, 3, 2)):
        send(refs, G.at[rows_at(q_me)], ags.at[4 + n], agr.at[q_me, 0], at_y(d))
    token(0)
    own_im.wait()
    arrived(IM.at[pl.ds(pl.multiple_of((1 - core) * 64, 64), 64)], sibr.at[0])
    arrived(AUXS, sibr.at[1])

    row = lax.broadcasted_iota(jnp.int32, (128, 128), 0)
    lane = lax.broadcasted_iota(jnp.int32, (128, 128), 1)

    def swap(src, dst):
        first = dst % 64 < 32
        return jnp.where(first & (src == dst + 32), 1.0, jnp.where((~first) & (src == dst - 32), -1.0, 0.0))

    eye = jnp.where(row == lane, 1.0, 0.0)
    rows_of = jnp.concatenate([eye, swap(lane, row)], axis=0).astype(BF16)
    cols_of = swap(row, lane).astype(BF16)

    def prepare(first, count, half):
        def step(n, carry):
            t = first + n
            block = IM[:, pl.ds(pl.multiple_of(t * 128, 128), 128)]
            both = dot_nt(rows_of, block)
            j = t - 18 * half
            sign = jnp.where(j < 9, 1.0, -1.0).astype(F32)
            FI[j, half * 128 : half * 128 + 128, 0:128] = both[0:128].astype(BF16)
            FI[j, half * 128 : half * 128 + 128, 128:256] = (both[128:256] * sign).astype(BF16)
            IMS[:, pl.ds(pl.multiple_of(t * 128, 128), 128)] = dot_nn(block, cols_of).astype(BF16)
            return carry

        lax.fori_loop(0, count, step, 0, unroll=2)

    def forward(n):
        q = far_q(order[n])
        arrived(piece(q, 1 - h), agr.at[q, 1 - h])
        send(piece(q, 1 - h), piece(q, 1 - h), ags.at[7 + n], agr.at[q, 1 - h], same)

    prepare(0, 8, 0)
    forward(0)
    prepare(8, 4, 0)
    forward(1)
    prepare(12, 4, 0)
    forward(2)
    pl.semaphore_wait(tok.at[0], 2)
    token(1)
    prepare(16, 2, 0)
    prepare(18, 4, 1)
    forward(3)

    right = lax.broadcasted_iota(jnp.int32, (8, 128), 1) >= 64
    auxc = jnp.where(right == (core == 1), AUX[...], AUXS[...])
    precision = auxc[0:1, :]
    class_id = ((row // 16) * 32 + core * 16 + row % 16).astype(F32)
    picks = [auxc[1:2, :] == class_id, auxc[2:3, :] == class_id]
    for k in range(2):
        OH[:, k * 128 : k * 128 + 128] = jnp.where(picks[k], 1.0, 0.0).astype(BF16)
    PT[...] = jnp.zeros_like(PT)

    prepare(22, 10, 1)
    own_g.wait()
    for d in (1, 3, 2):
        q = near_q(d)
        arrived(G.at[rows_at(q)], agr.at[q, 0])

    low = (lax.broadcasted_iota(jnp.int32, (64, 256), 1) % 128) < 64

    def harmonics(first):
        rows = pl.ds(pl.multiple_of(first * 16, 64), 64)
        for j in range(18):
            left = G[rows, j * 128 : j * 128 + 128]
            if j < 14:
                tile = jnp.concatenate([left, G[rows, (18 + j) * 128 : (18 + j) * 128 + 128]], axis=1)
                keep, right_side = low, FI[j]
            else:
                tile, keep, right_side = left, low[:, 0:128], FI[j, 0:128, :]
            zero = jnp.zeros_like(tile)
            stacked = jnp.concatenate([jnp.where(keep, tile, zero), jnp.where(keep, zero, tile)], axis=0)
            out = dot_nn(stacked, right_side)
            even, odd = out[0:64], out[64:128]
            k_even, k_odd = (2 * j if j <= 9 else 36 - 2 * j), (2 * j + 1 if j <= 8 else 35 - 2 * j)
            if j <= 9:
                F[k_even, rows, :] = even[:, 0:128]
            else:
                F[k_even, rows, :] += even[:, 0:128]
            if 0 < k_even < 18:
                if j <= 9:
                    F[18 + k_even, rows, :] = even[:, 128:256]
                else:
                    F[18 + k_even, rows, :] += even[:, 128:256]
            if j <= 8:
                F[k_odd, rows, :] = odd[:, 0:128]
                F[18 + k_odd, rows, :] = odd[:, 128:256]
            else:
                F[k_odd, rows, :] += odd[:, 0:128]
                F[18 + k_odd, rows, :] += odd[:, 128:256]
        square = jnp.zeros((64, 128), F32)
        for t in range(32):
            value = G[rows, t * 128 : t * 128 + 128].astype(F32)
            square = square + value * value
        F[36, rows, :] = jnp.broadcast_to(0.5 * jnp.sum(square, axis=1, keepdims=True), (64, 128))

    even_row = lax.broadcasted_iota(jnp.int32, (8, 128), 0) % 2 == 0

    def choose(first, more):
        rows = pl.ds(pl.multiple_of(first * 16, 64), 64)
        ids = (((row[0:64] // 16) + first) * 32 + core * 16 + row[0:64] % 16).astype(F32)
        keep = [auxc[k : k + 1, :] == ids for k in (1, 2)]

        def step(kk, carry):
            f = F[kk, rows, :]
            parts = []
            for k in range(2):
                kept = jnp.where(keep[k], f, 0.0)
                total = tree(add, [kept[n * 8 : n * 8 + 8] for n in range(8)])
                parts.append(total + pltpu.roll(total, 1, 0))
            both = jnp.where(even_row, parts[0], parts[1])
            both = both + pltpu.roll(both, 2, 0)
            both = both + pltpu.roll(both, 4, 0)
            CHX[kk] = CHX[kk] + both if more else both
            return carry

        lax.fori_loop(0, 36, step, 0, unroll=4)
        step(36, 0)

    harmonics(col)
    choose(col, False)
    pl.semaphore_wait(tok.at[1], 2)
    token(2)
    for d in order:
        arrived(piece(far_q(d), h), agr.at[far_q(d), h])
    harmonics(far)
    choose(far, True)
    send(CHX, CHS, sibs.at[2], sibr.at[2], sib)
    arrived(CHS, sibr.at[2])

    coefs = [CHX[k] + CHS[k] for k in range(37)]
    turned = turns_of(coefs[0:19], [None] + coefs[19:36])
    scores = [precision * (v - coefs[36]) for v in turned]
    peak = tree(jnp.maximum, scores)
    peak = jnp.maximum(peak, jnp.where(even_row, pltpu.roll(peak, 7, 0), pltpu.roll(peak, 1, 0)))
    exps = [jnp.exp(v - peak) for v in scores]
    total = tree(add, exps)
    total = total + jnp.where(even_row, pltpu.roll(total, 7, 0), pltpu.roll(total, 1, 0))
    posterior = [v / total for v in exps]
    share = tree(add, posterior)
    for s in range(TURNS):
        high = posterior[s].astype(BF16).astype(F32)
        rest = posterior[s] - high
        for k in range(2):
            PT[k, s : s + 1, :] = high[k : k + 1]
            PT[k, 40 + s : 41 + s, :] = rest[k : k + 1]
            PT[k, 80 + s : 81 + s, :] = high[k : k + 1]
    for k in range(2):
        PP[k * 128 : k * 128 + 128, :] = PT[k].T.astype(BF16)
    own_t.wait()

    onehot = OH[...]

    def sums(x_half, second):
        def step(v, carry):
            u = x_half * 8 + second * 4 + v
            lanes = pl.ds(pl.multiple_of(u * 256, 256), 256)
            out_lanes = pl.ds(pl.multiple_of(v * 256, 256), 256)
            factor = dot_nn(PP[...], TE[u])
            straight, turned_in = IM[:, lanes].astype(F32), IMS[:, lanes].astype(F32)
            rows = [
                (
                    straight * factor[k * 128 : k * 128 + 128, 0:256]
                    - turned_in * factor[k * 128 : k * 128 + 128, 256:512]
                ).astype(BF16)
                for k in range(2)
            ]
            out = dot_nn(onehot, jnp.concatenate(rows, axis=0)).astype(BF16)
            for q in range(8):
                block = out[q * 16 : q * 16 + 16]
                if second:
                    SB[(q // 4) * 2 + x_half, q % 4, :, out_lanes] = block
                else:
                    SA[x_half, q % 4, q // 4, :, out_lanes] = block
            return carry

        lax.fori_loop(0, 4, step, 0, unroll=True)

    for x_half in range(2):
        sums(x_half, 0)
        for d in range(1, 4):
            n = x_half * 3 + d - 1
            send(SA.at[x_half, (y + d) % 4], RA.at[d - 1, x_half], s1s.at[n], s1r.at[n], at_y(d))
    for x_half in range(2):
        sums(x_half, 1)
    for d in range(1, 4):
        n = 5 + d
        send(SB.at[(x + d) % 4], RB.at[d - 1], s1s.at[n], s1r.at[n], at_x(d))

    shares = jnp.concatenate(
        [jnp.broadcast_to(share[0:1], (8, 128)), jnp.broadcast_to(share[1:2], (8, 128))], axis=1
    )
    W0[...] = dot_nt(shares, onehot.astype(F32), precision=lax.Precision.HIGHEST)
    pl.semaphore_wait(tok.at[2], 2)
    for d in range(1, 16):
        send(W0, RW0.at[d - 1], ws.at[d - 1], wr.at[d - 1], at_z(d))

    def block_scores(n, carry):
        run_peak, run_total = carry
        rows = pl.ds(pl.multiple_of(n * 8, 8), 8)
        f = [F[k, rows, :] for k in range(37)]
        turned = turns_of(f[0:19], [None] + f[19:36])
        scores = [precision * (v - f[36]) for v in turned]
        new_peak = jnp.maximum(run_peak, tree(jnp.maximum, scores))
        total = tree(add, [jnp.exp(v - new_peak) for v in scores])
        return new_peak, run_total * jnp.exp(run_peak - new_peak) + total

    start = (jnp.full((8, 128), -jnp.inf, F32), jnp.zeros((8, 128), F32))
    run_peak, run_total = lax.fori_loop(0, 16, block_scores, start)
    peak = jnp.max(run_peak, axis=0, keepdims=True)
    total = jnp.sum(run_total * jnp.exp(run_peak - peak), axis=0, keepdims=True)
    LS[0:8] = jnp.broadcast_to(peak, (8, 128))
    LS[8:16] = jnp.broadcast_to(total, (8, 128))
    send(LS, LR, sibs.at[3], sibr.at[3], sib)

    for d in range(1, 16):
        arrived(RW0.at[d - 1], wr.at[d - 1])
    W1[...] = tree(add, [W0[...]] + [RW0[d] for d in range(15)])
    for d in range(1, 4):
        send(W1, RW1.at[d - 1], ws.at[14 + d], wr.at[14 + d], at_y(d))

    for d in range(1, 4):
        for x_half in range(2):
            arrived(RA.at[d - 1, x_half], s1r.at[x_half * 3 + d - 1])
    for x_half in range(2):
        for x_top in range(2):
            total = SA[x_half, y, x_top].astype(F32)
            for d in range(3):
                total = total + RA[d, x_half, x_top].astype(F32)
            TA[x_top * 2 + x_half] = total
    for d in range(1, 4):
        send(TA.at[(x + d) % 4], R2A.at[d - 1], s2s.at[d - 1], s2r.at[d - 1], at_x(d))
    for d in range(1, 4):
        arrived(RB.at[d - 1], s1r.at[5 + d])
    for y_to in range(4):
        total = SB[x, y_to].astype(F32)
        for d in range(3):
            total = total + RB[d, y_to].astype(F32)
        TB[y_to] = total
    for d in range(1, 4):
        send(TB.at[(y + d) % 4], R2B.at[d - 1], s2s.at[2 + d], s2r.at[2 + d], at_y(d))

    for d in range(1, 4):
        arrived(RW1.at[d - 1], wr.at[14 + d])
    W2[...] = tree(add, [W1[...]] + [RW1[d] for d in range(3)])
    for d in range(1, 4):
        send(W2, RW2.at[d - 1], ws.at[17 + d], wr.at[17 + d], at_x(d))

    arrived(LR, sibr.at[3])
    peak = jnp.maximum(LS[0:8], LR[0:8])
    total = LS[8:16] * jnp.exp(LS[0:8] - peak) + LR[8:16] * jnp.exp(LR[0:8] - peak)
    evidence = peak + jnp.log(total)
    evid_out[...] = jnp.where(core == 0, evidence[0:1, 0:64], evidence[0:1, 64:128])

    for d in range(1, 4):
        arrived(R2A.at[d - 1], s2r.at[d - 1])
    total = TA[x] + R2A[0] + R2A[1] + R2A[2]
    for n in range(8):
        UZ[n] = total[:, n * 128 : n * 128 + 128]
    for d in range(1, 4):
        arrived(R2B.at[d - 1], s2r.at[2 + d])
    total = TB[y] + R2B[0] + R2B[1] + R2B[2]
    for n in range(8):
        UZ[8 + n] = total[:, n * 128 : n * 128 + 128]
    SZ[...] = UZ[...].astype(BF16)
    for d in range(1, 16):
        send(SZ.at[(z + d) % 16], RZ.at[d - 1], zs.at[d - 1], zr.at[d - 1], at_z(d))

    for d in range(1, 4):
        arrived(RW2.at[d - 1], wr.at[17 + d])
    weight = tree(add, [W2[...]] + [RW2[d] for d in range(3)])
    pick = lane[0:16] == row[0:16] + q_me * 16
    weight = jnp.sum(jnp.where(pick, jnp.broadcast_to(weight[0:1], (16, 128)), 0.0), axis=1, keepdims=True)
    for d in range(1, 16):
        arrived(RZ.at[d - 1], zr.at[d - 1])
    total = tree(add, [UZ[z]] + [RZ[d].astype(F32) for d in range(15)])
    avg_out[...] = total / (1.0 + weight)
    for copy in sent:
        copy.wait_send()


def body(images, references, precision, candidates):
    table = jnp.asarray(spread_table())
    anywhere = pl.BlockSpec(memory_space=pltpu.HBM)
    vmem = pl.BlockSpec(memory_space=pltpu.VMEM)
    dma = pltpu.SemaphoreType.DMA
    scratch = [
        pltpu.VMEM((128, 4096), BF16),
        pltpu.VMEM((128, 4096), BF16),
        pltpu.VMEM((128, 4096), BF16),
        pltpu.VMEM((18, 256, 256), BF16),
        pltpu.VMEM((37, 128, 128), F32),
        pltpu.VMEM((1, 64), F32),
        pltpu.VMEM((2, 64), jnp.int32),
        pltpu.VMEM((8, 128), F32),
        pltpu.VMEM((8, 128), F32),
        pltpu.VMEM((37, 8, 128), F32),
        pltpu.VMEM((37, 8, 128), F32),
        pltpu.VMEM((2, 128, 128), F32),
        pltpu.VMEM((256, 128), BF16),
        pltpu.VMEM((16, 128, 512), BF16),
        pltpu.VMEM((128, 256), BF16),
        pltpu.VMEM((2, 4, 2, 16, 1024), BF16),
        pltpu.VMEM((3, 2, 2, 16, 1024), BF16),
        pltpu.VMEM((4, 4, 16, 1024), BF16),
        pltpu.VMEM((3, 4, 16, 1024), BF16),
        pltpu.VMEM((4, 16, 1024), F32),
        pltpu.VMEM((3, 16, 1024), F32),
        pltpu.VMEM((4, 16, 1024), F32),
        pltpu.VMEM((3, 16, 1024), F32),
        pltpu.VMEM((16, 16, 128), F32),
        pltpu.VMEM((16, 16, 128), BF16),
        pltpu.VMEM((15, 16, 128), BF16),
        pltpu.VMEM((8, 128), F32),
        pltpu.VMEM((15, 8, 128), F32),
        pltpu.VMEM((8, 128), F32),
        pltpu.VMEM((3, 8, 128), F32),
        pltpu.VMEM((8, 128), F32),
        pltpu.VMEM((3, 8, 128), F32),
        pltpu.VMEM((16, 128), F32),
        pltpu.VMEM((16, 128), F32),
        dma((5,)),
        pltpu.SemaphoreType.REGULAR((3,)),
        dma((11,)),
        dma((8, 2)),
        dma((4,)),
        dma((4,)),
        dma((9,)),
        dma((9,)),
        dma((6,)),
        dma((6,)),
        dma((15,)),
        dma((15,)),
        dma((21,)),
        dma((21,)),
    ]
    average, evidence = pl.pallas_call(
        kernel,
        out_shape=(jax.ShapeDtypeStruct((16, 128), F32), jax.ShapeDtypeStruct((1, 64), F32)),
        in_specs=[anywhere] * 5,
        out_specs=(vmem, vmem),
        scratch_shapes=scratch,
        compiler_params=pltpu.CompilerParams(
            collective_id=0, has_side_effects=True, vmem_limit_bytes=60 * 1024 * 1024
        ),
    )(images, references, precision.reshape(1, 64), candidates.T, table)
    return average, evidence.reshape(64)


def solution(mesh):
    in_specs = (P(("img", "blk"), None), P("blk", None), P(("img", "blk")), P(("img", "blk"), None))
    out_specs = (P("blk", "img"), P(("img", "blk")))
    return jax.shard_map(body, mesh=mesh, in_specs=in_specs, out_specs=out_specs, check_vma=False)
```

```python
import math

import jax
import jax.numpy as jnp
import ml_dtypes
import numpy as np
from jax import lax
from jax.experimental import pallas as pl
from jax.experimental.pallas import tpu as pltpu
from jax.sharding import PartitionSpec as P

CYCLES = 32
ORDERS = 64
TURNS = 36
FEATS = 4096
LANES = 128
MESH = pl.DeviceIdType.MESH
F32 = jnp.float32
BF16 = jnp.bfloat16


def spread_table():
    feats = np.arange(FEATS)
    order = feats // (2 * CYCLES)
    turns = np.arange(TURNS)
    angle = 2.0 * math.pi / TURNS * ((turns[:, None] * order[None, :]) % TURNS)
    out = np.zeros((16, 128, 512), np.float32)
    for part, values in enumerate((np.cos(angle), -np.sin(angle))):
        values = values.astype(np.float32).reshape(TURNS, 16, 256).transpose(1, 0, 2)
        high = values.astype(ml_dtypes.bfloat16).astype(np.float32)
        low = values - high
        cols = slice(part * 256, part * 256 + 256)
        out[:, 0:36, cols] = high
        out[:, 40:76, cols] = high
        out[:, 80:116, cols] = low
    return out.astype(ml_dtypes.bfloat16)


def weighted(pairs):
    total = None
    for coef, value in pairs:
        if abs(coef) < 1e-12:
            continue
        if abs(coef - 1.0) < 1e-12:
            term = value
        elif abs(coef + 1.0) < 1e-12:
            term = -value
        else:
            term = value * np.float32(coef)
        total = term if total is None else total + term
    return total


def turns_of(a, b):
    def cos(k, s):
        return math.cos(2.0 * math.pi * (k * s % 36) / 36.0)

    def sin(k, s):
        return math.sin(2.0 * math.pi * (k * s % 36) / 36.0)

    even_c, odd_c, even_s, odd_s = {}, {}, {}, {}
    for s in range(5):
        p = weighted([(cos(k, s), a[k]) for k in range(0, 19, 4)])
        q = weighted([(cos(k, s), a[k]) for k in range(2, 19, 4)])
        even_c[s], even_c[9 - s] = p + q, p - q
    for s in range(9):
        odd_c[s] = weighted([(cos(k, s), a[k]) for k in range(1, 18, 2)])
    for s in range(1, 5):
        p = weighted([(sin(k, s), b[k]) for k in range(4, 17, 4)])
        q = weighted([(sin(k, s), b[k]) for k in range(2, 17, 4)])
        even_s[s], even_s[9 - s] = p + q, q - p
    for s in range(1, 10):
        odd_s[s] = weighted([(sin(k, s), b[k]) for k in range(1, 18, 2)])
    x = [None] * 36
    for s in range(10):
        if s < 9:
            c_lo, c_hi = even_c[s] + odd_c[s], even_c[s] - odd_c[s]
        else:
            c_lo = c_hi = even_c[9]
        if s == 0:
            x[0], x[18] = c_lo, c_hi
        elif s == 9:
            x[9], x[27] = c_lo - odd_s[9], c_lo + odd_s[9]
        else:
            s_lo, s_hi = even_s[s] + odd_s[s], odd_s[s] - even_s[s]
            x[s], x[36 - s] = c_lo - s_lo, c_lo + s_lo
            x[18 - s], x[18 + s] = c_hi - s_hi, c_hi + s_hi
    return x


def tree(op, values):
    values = list(values)
    while len(values) > 1:
        nxt = [op(values[i], values[i + 1]) for i in range(0, len(values) - 1, 2)]
        if len(values) % 2:
            nxt.append(values[-1])
        values = nxt
    return values[0]


def add(p, q):
    return p + q


def dot_nt(a, b, **kw):
    return lax.dot_general(a, b, (((1,), (1,)), ((), ())), preferred_element_type=F32, **kw)


def dot_nn(a, b):
    return jnp.dot(a, b, preferred_element_type=F32)


def kernel(
    images, refs, prec, cand, table, avg_out, evid_out,
    G, IM, IMS, FI, F, PIN, CIN, AUX, AUXS, CHX, CHS, PT, PP, TE, OH, SA, RA, SB, RB, TA, R2A, TB, R2B,
    UZ, SZ, RZ, W0, RW0, W1, RW1, W2, RW2, LS, LR,
    loc, tok, ags, agr, sibs, sibr, s1s, s1r, s2s, s2r, zs, zr, ws, wr,
):
    img, blk = lax.axis_index("img"), lax.axis_index("blk")
    z, x_lo = img % 16, img // 16
    core, y, x_hi = blk % 2, (blk // 2) % 4, blk // 8
    x = x_hi * 2 + x_lo
    q_me = x_hi * 4 + y

    def dev(x_, y_, z_, c_):
        return ((x_ % 2) * 16 + z_, (x_ // 2) * 8 + y_ * 2 + c_)

    sib = dev(x, y, z, 1 - core)
    x_opp, x_same = 3 - x, x_hi * 2 + 1 - x_lo
    same = dev(x_same, y, z, core)

    def at_y(d):
        return dev(x, (y + d) % 4, z, core)

    def at_x(d):
        return dev((x + d) % 4, y, z, core)

    def at_z(d):
        return dev(x, y, (z + d) % 16, core)

    sent = []
    far_first = sorted(range(1, 16), key=lambda d: -min(d, 16 - d))

    def send(src, dst, ssem, rsem, to):
        copy = pltpu.make_async_remote_copy(
            src_ref=src, dst_ref=dst, send_sem=ssem, recv_sem=rsem, device_id=to, device_id_type=MESH
        )
        copy.start()
        sent.append(copy)

    def arrived(dst, rsem):
        pltpu.make_async_copy(dst, dst, rsem).wait()

    mine_rows = pl.ds(pl.multiple_of(core * 64, 64), 64)
    own_p = pltpu.make_async_copy(prec, PIN, loc.at[3])
    own_p.start()
    own_c = pltpu.make_async_copy(cand, CIN, loc.at[4])
    own_c.start()
    own_g = pltpu.make_async_copy(refs, G.at[pl.ds(pl.multiple_of(q_me * 16, 16), 16)], loc.at[1])
    own_g.start()
    own_im = pltpu.make_async_copy(images, IM.at[mine_rows], loc.at[0])
    own_im.start()
    own_t = pltpu.make_async_copy(table, TE, loc.at[2])
    own_t.start()

    barrier = pltpu.get_barrier_semaphore()
    partners = [dev(x_opp, (y + d) % 4, z, core) for d in range(1, 4)]
    partners += [at_y(d) for d in range(1, 4)] + [at_x(d) for d in range(1, 4)]
    partners += [at_z(1), at_z(15), sib]
    for to in partners:
        pl.semaphore_signal(barrier, inc=1, device_id=to, device_id_type=MESH)
    own_p.wait()
    own_c.wait()
    mine = jnp.concatenate([PIN[...], CIN[...].astype(F32)], axis=0)
    AUX[0:3, :] = jnp.concatenate([mine, mine], axis=1)
    AUX[3:8, :] = jnp.zeros((5, 128), F32)
    pl.semaphore_wait(barrier, len(partners))

    def token(n):
        for d in (1 << n, 16 - (1 << n)):
            pl.semaphore_signal(tok.at[n], inc=1, device_id=at_z(d), device_id_type=MESH)

    def rows_at(q):
        return pl.ds(pl.multiple_of(q * 16, 16), 16)

    def piece(q, hh):
        return G.at[rows_at(q), pl.ds(pl.multiple_of(hh * 2048, 2048), 2048)]

    h = x_lo
    col, far = x_hi * 4, (1 - x_hi) * 4
    order = (0, 1, 3, 2)

    def near_q(d):
        return col + (y + d) % 4

    def far_q(d):
        return far + (y + d) % 4

    send(AUX, AUXS, sibs.at[1], sibr.at[1], sib)
    send(images, IM.at[mine_rows], sibs.at[0], sibr.at[0], sib)
    own_half = refs.at[:, pl.ds(pl.multiple_of(h * 2048, 2048), 2048)]
    for n, d in enumerate(order):
        send(own_half, piece(q_me, h), ags.at[n], agr.at[q_me, h], dev(x_opp, (y + d) % 4, z, core))
    for n, d in enumerate((1, 3, 2)):
        send(refs, G.at[rows_at(q_me)], ags.at[4 + n], agr.at[q_me, 0], at_y(d))
    token(0)
    own_im.wait()
    arrived(IM.at[pl.ds(pl.multiple_of((1 - core) * 64, 64), 64)], sibr.at[0])
    arrived(AUXS, sibr.at[1])

    row = lax.broadcasted_iota(jnp.int32, (128, 128), 0)
    lane = lax.broadcasted_iota(jnp.int32, (128, 128), 1)

    def swap(src, dst):
        first = dst % 64 < 32
        return jnp.where(first & (src == dst + 32), 1.0, jnp.where((~first) & (src == dst - 32), -1.0, 0.0))

    eye = jnp.where(row == lane, 1.0, 0.0)
    rows_of = jnp.concatenate([eye, swap(lane, row)], axis=0).astype(BF16)
    cols_of = swap(row, lane).astype(BF16)

    def prepare(first, count, half):
        def step(n, carry):
            t = first + n
            block = IM[:, pl.ds(pl.multiple_of(t * 128, 128), 128)]
            both = dot_nt(rows_of, block)
            j = t - 18 * half
            sign = jnp.where(j < 9, 1.0, -1.0).astype(F32)
            FI[j, half * 128 : half * 128 + 128, 0:128] = both[0:128].astype(BF16)
            FI[j, half * 128 : half * 128 + 128, 128:256] = (both[128:256] * sign).astype(BF16)
            IMS[:, pl.ds(pl.multiple_of(t * 128, 128), 128)] = dot_nn(block, cols_of).astype(BF16)
            return carry

        lax.fori_loop(0, count, step, 0, unroll=2)

    def forward(n):
        q = far_q(order[n])
        arrived(piece(q, 1 - h), agr.at[q, 1 - h])
        send(piece(q, 1 - h), piece(q, 1 - h), ags.at[7 + n], agr.at[q, 1 - h], same)

    prepare(0, 8, 0)
    forward(0)
    prepare(8, 4, 0)
    forward(1)
    prepare(12, 4, 0)
    forward(2)
    pl.semaphore_wait(tok.at[0], 2)
    token(1)
    prepare(16, 2, 0)
    prepare(18, 4, 1)
    forward(3)

    right = lax.broadcasted_iota(jnp.int32, (8, 128), 1) >= 64
    auxc = jnp.where(right == (core == 1), AUX[...], AUXS[...])
    precision = auxc[0:1, :]
    class_id = ((row // 16) * 32 + core * 16 + row % 16).astype(F32)
    picks = [auxc[1:2, :] == class_id, auxc[2:3, :] == class_id]
    for k in range(2):
        OH[:, k * 128 : k * 128 + 128] = jnp.where(picks[k], 1.0, 0.0).astype(BF16)
    PT[...] = jnp.zeros_like(PT)

    prepare(22, 10, 1)
    own_g.wait()
    for d in (1, 3, 2):
        q = near_q(d)
        arrived(G.at[rows_at(q)], agr.at[q, 0])

    low = (lax.broadcasted_iota(jnp.int32, (64, 256), 1) % 128) < 64

    def harmonics(first):
        rows = pl.ds(pl.multiple_of(first * 16, 64), 64)
        for j in range(18):
            left = G[rows, j * 128 : j * 128 + 128]
            if j < 14:
                tile = jnp.concatenate([left, G[rows, (18 + j) * 128 : (18 + j) * 128 + 128]], axis=1)
                keep, right_side = low, FI[j]
            else:
                tile, keep, right_side = left, low[:, 0:128], FI[j, 0:128, :]
            zero = jnp.zeros_like(tile)
            stacked = jnp.concatenate([jnp.where(keep, tile, zero), jnp.where(keep, zero, tile)], axis=0)
            out = dot_nn(stacked, right_side)
            even, odd = out[0:64], out[64:128]
            k_even, k_odd = (2 * j if j <= 9 else 36 - 2 * j), (2 * j + 1 if j <= 8 else 35 - 2 * j)
            if j <= 9:
                F[k_even, rows, :] = even[:, 0:128]
            else:
                F[k_even, rows, :] += even[:, 0:128]
            if 0 < k_even < 18:
                if j <= 9:
                    F[18 + k_even, rows, :] = even[:, 128:256]
                else:
                    F[18 + k_even, rows, :] += even[:, 128:256]
            if j <= 8:
                F[k_odd, rows, :] = odd[:, 0:128]
                F[18 + k_odd, rows, :] = odd[:, 128:256]
            else:
                F[k_odd, rows, :] += odd[:, 0:128]
                F[18 + k_odd, rows, :] += odd[:, 128:256]
        square = jnp.zeros((64, 128), F32)
        for t in range(32):
            value = G[rows, t * 128 : t * 128 + 128].astype(F32)
            square = square + value * value
        F[36, rows, :] = jnp.broadcast_to(0.5 * jnp.sum(square, axis=1, keepdims=True), (64, 128))

    even_row = lax.broadcasted_iota(jnp.int32, (8, 128), 0) % 2 == 0

    def choose(first, more):
        rows = pl.ds(pl.multiple_of(first * 16, 64), 64)
        ids = (((row[0:64] // 16) + first) * 32 + core * 16 + row[0:64] % 16).astype(F32)
        keep = [auxc[k : k + 1, :] == ids for k in (1, 2)]

        def step(kk, carry):
            f = F[kk, rows, :]
            parts = []
            for k in range(2):
                kept = jnp.where(keep[k], f, 0.0)
                total = tree(add, [kept[n * 8 : n * 8 + 8] for n in range(8)])
                parts.append(total + pltpu.roll(total, 1, 0))
            both = jnp.where(even_row, parts[0], parts[1])
            both = both + pltpu.roll(both, 2, 0)
            both = both + pltpu.roll(both, 4, 0)
            CHX[kk] = CHX[kk] + both if more else both
            return carry

        lax.fori_loop(0, 36, step, 0, unroll=4)
        step(36, 0)

    harmonics(col)
    choose(col, False)
    pl.semaphore_wait(tok.at[1], 2)
    token(2)
    for d in order:
        arrived(piece(far_q(d), h), agr.at[far_q(d), h])
    harmonics(far)
    choose(far, True)
    send(CHX, CHS, sibs.at[2], sibr.at[2], sib)
    arrived(CHS, sibr.at[2])

    coefs = [CHX[k] + CHS[k] for k in range(37)]
    turned = turns_of(coefs[0:19], [None] + coefs[19:36])
    scores = [precision * (v - coefs[36]) for v in turned]
    peak = tree(jnp.maximum, scores)
    peak = jnp.maximum(peak, jnp.where(even_row, pltpu.roll(peak, 7, 0), pltpu.roll(peak, 1, 0)))
    exps = [jnp.exp(v - peak) for v in scores]
    total = tree(add, exps)
    total = total + jnp.where(even_row, pltpu.roll(total, 7, 0), pltpu.roll(total, 1, 0))
    posterior = [v / total for v in exps]
    share = tree(add, posterior)
    for s in range(TURNS):
        high = posterior[s].astype(BF16).astype(F32)
        rest = posterior[s] - high
        for k in range(2):
            PT[k, s : s + 1, :] = high[k : k + 1]
            PT[k, 40 + s : 41 + s, :] = rest[k : k + 1]
            PT[k, 80 + s : 81 + s, :] = high[k : k + 1]
    for k in range(2):
        PP[k * 128 : k * 128 + 128, :] = PT[k].T.astype(BF16)
    own_t.wait()

    onehot = OH[...]

    def sums(x_half, second):
        def step(v, carry):
            u = x_half * 8 + second * 4 + v
            lanes = pl.ds(pl.multiple_of(u * 256, 256), 256)
            out_lanes = pl.ds(pl.multiple_of(v * 256, 256), 256)
            factor = dot_nn(PP[...], TE[u])
            straight, turned_in = IM[:, lanes].astype(F32), IMS[:, lanes].astype(F32)
            rows = [
                (
                    straight * factor[k * 128 : k * 128 + 128, 0:256]
                    - turned_in * factor[k * 128 : k * 128 + 128, 256:512]
                ).astype(BF16)
                for k in range(2)
            ]
            out = dot_nn(onehot, jnp.concatenate(rows, axis=0)).astype(BF16)
            for q in range(8):
                block = out[q * 16 : q * 16 + 16]
                if second:
                    SB[(q // 4) * 2 + x_half, q % 4, :, out_lanes] = block
                else:
                    SA[x_half, q % 4, q // 4, :, out_lanes] = block
            return carry

        lax.fori_loop(0, 4, step, 0, unroll=True)

    other = 1 - x_lo
    for pos, x_half in enumerate((other, x_lo)):
        sums(x_half, 0)
        for d in (2, 1, 3):
            n = pos * 3 + d - 1
            send(SA.at[x_half, (y + d) % 4], RA.at[d - 1, x_half], s1s.at[n], s1r.at[n], at_y(d))
        sums(x_half, 1)
        for d in ((1, 3), (2,))[pos]:
            send(SB.at[(x + d) % 4], RB.at[d - 1], s1s.at[5 + d], s1r.at[5 + d], at_x(d))
    shares = jnp.concatenate(
        [jnp.broadcast_to(share[0:1], (8, 128)), jnp.broadcast_to(share[1:2], (8, 128))], axis=1
    )
    W0[...] = dot_nt(shares, onehot.astype(F32), precision=lax.Precision.HIGHEST)
    pl.semaphore_wait(tok.at[2], 2)
    for d in far_first:
        send(W0, RW0.at[d - 1], ws.at[d - 1], wr.at[d - 1], at_z(d))

    def block_scores(n, carry):
        run_peak, run_total = carry
        rows = pl.ds(pl.multiple_of(n * 8, 8), 8)
        f = [F[k, rows, :] for k in range(37)]
        turned = turns_of(f[0:19], [None] + f[19:36])
        scores = [precision * (v - f[36]) for v in turned]
        new_peak = jnp.maximum(run_peak, tree(jnp.maximum, scores))
        total = tree(add, [jnp.exp(v - new_peak) for v in scores])
        return new_peak, run_total * jnp.exp(run_peak - new_peak) + total

    start = (jnp.full((8, 128), -jnp.inf, F32), jnp.zeros((8, 128), F32))
    run_peak, run_total = lax.fori_loop(0, 16, block_scores, start)
    peak = jnp.max(run_peak, axis=0, keepdims=True)
    total = jnp.sum(run_total * jnp.exp(run_peak - peak), axis=0, keepdims=True)
    LS[0:8] = jnp.broadcast_to(peak, (8, 128))
    LS[8:16] = jnp.broadcast_to(total, (8, 128))
    send(LS, LR, sibs.at[3], sibr.at[3], sib)

    for pos, x_half in enumerate((other, x_lo)):
        for d in range(1, 4):
            arrived(RA.at[d - 1, x_half], s1r.at[pos * 3 + d - 1])
    for x_half in range(2):
        for x_top in range(2):
            total = SA[x_half, y, x_top].astype(F32)
            for d in range(3):
                total = total + RA[d, x_half, x_top].astype(F32)
            TA[x_top * 2 + x_half] = total
    for d in range(1, 4):
        send(TA.at[(x + d) % 4], R2A.at[d - 1], s2s.at[d - 1], s2r.at[d - 1], at_x(d))
    for d in range(1, 4):
        arrived(RB.at[d - 1], s1r.at[5 + d])
    for y_to in range(4):
        total = SB[x, y_to].astype(F32)
        for d in range(3):
            total = total + RB[d, y_to].astype(F32)
        TB[y_to] = total
    for d in range(1, 4):
        send(TB.at[(y + d) % 4], R2B.at[d - 1], s2s.at[2 + d], s2r.at[2 + d], at_y(d))

    arrived(LR, sibr.at[3])
    peak = jnp.maximum(LS[0:8], LR[0:8])
    total = LS[8:16] * jnp.exp(LS[0:8] - peak) + LR[8:16] * jnp.exp(LR[0:8] - peak)
    evidence = peak + jnp.log(total)
    evid_out[...] = jnp.where(core == 0, evidence[0:1, 0:64], evidence[0:1, 64:128])

    for d in range(1, 16):
        arrived(RW0.at[d - 1], wr.at[d - 1])
    W1[...] = tree(add, [W0[...]] + [RW0[d] for d in range(15)])
    for d in range(1, 4):
        send(W1, RW1.at[d - 1], ws.at[14 + d], wr.at[14 + d], at_y(d))

    for d in range(1, 4):
        arrived(R2A.at[d - 1], s2r.at[d - 1])
    total = TA[x] + R2A[0] + R2A[1] + R2A[2]
    for n in range(8):
        UZ[n] = total[:, n * 128 : n * 128 + 128]
    for d in range(1, 4):
        arrived(R2B.at[d - 1], s2r.at[2 + d])
    total = TB[y] + R2B[0] + R2B[1] + R2B[2]
    for n in range(8):
        UZ[8 + n] = total[:, n * 128 : n * 128 + 128]
    SZ[...] = UZ[...].astype(BF16)
    for d in far_first:
        send(SZ.at[(z + d) % 16], RZ.at[d - 1], zs.at[d - 1], zr.at[d - 1], at_z(d))

    for d in range(1, 4):
        arrived(RW1.at[d - 1], wr.at[14 + d])
    W2[...] = tree(add, [W1[...]] + [RW1[d] for d in range(3)])
    for d in range(1, 4):
        send(W2, RW2.at[d - 1], ws.at[17 + d], wr.at[17 + d], at_x(d))

    for d in range(1, 4):
        arrived(RW2.at[d - 1], wr.at[17 + d])
    weight = tree(add, [W2[...]] + [RW2[d] for d in range(3)])
    pick = lane[0:16] == row[0:16] + q_me * 16
    weight = jnp.sum(jnp.where(pick, jnp.broadcast_to(weight[0:1], (16, 128)), 0.0), axis=1, keepdims=True)
    for d in range(1, 16):
        arrived(RZ.at[d - 1], zr.at[d - 1])
    total = tree(add, [UZ[z]] + [RZ[d].astype(F32) for d in range(15)])
    avg_out[...] = total / (1.0 + weight)
    for copy in sent:
        copy.wait_send()


def body(images, references, precision, candidates):
    table = jnp.asarray(spread_table())
    anywhere = pl.BlockSpec(memory_space=pltpu.HBM)
    vmem = pl.BlockSpec(memory_space=pltpu.VMEM)
    dma = pltpu.SemaphoreType.DMA
    scratch = [
        pltpu.VMEM((128, 4096), BF16),
        pltpu.VMEM((128, 4096), BF16),
        pltpu.VMEM((128, 4096), BF16),
        pltpu.VMEM((18, 256, 256), BF16),
        pltpu.VMEM((37, 128, 128), F32),
        pltpu.VMEM((1, 64), F32),
        pltpu.VMEM((2, 64), jnp.int32),
        pltpu.VMEM((8, 128), F32),
        pltpu.VMEM((8, 128), F32),
        pltpu.VMEM((37, 8, 128), F32),
        pltpu.VMEM((37, 8, 128), F32),
        pltpu.VMEM((2, 128, 128), F32),
        pltpu.VMEM((256, 128), BF16),
        pltpu.VMEM((16, 128, 512), BF16),
        pltpu.VMEM((128, 256), BF16),
        pltpu.VMEM((2, 4, 2, 16, 1024), BF16),
        pltpu.VMEM((3, 2, 2, 16, 1024), BF16),
        pltpu.VMEM((4, 4, 16, 1024), BF16),
        pltpu.VMEM((3, 4, 16, 1024), BF16),
        pltpu.VMEM((4, 16, 1024), F32),
        pltpu.VMEM((3, 16, 1024), F32),
        pltpu.VMEM((4, 16, 1024), F32),
        pltpu.VMEM((3, 16, 1024), F32),
        pltpu.VMEM((16, 16, 128), F32),
        pltpu.VMEM((16, 16, 128), BF16),
        pltpu.VMEM((15, 16, 128), BF16),
        pltpu.VMEM((8, 128), F32),
        pltpu.VMEM((15, 8, 128), F32),
        pltpu.VMEM((8, 128), F32),
        pltpu.VMEM((3, 8, 128), F32),
        pltpu.VMEM((8, 128), F32),
        pltpu.VMEM((3, 8, 128), F32),
        pltpu.VMEM((16, 128), F32),
        pltpu.VMEM((16, 128), F32),
        dma((5,)),
        pltpu.SemaphoreType.REGULAR((3,)),
        dma((11,)),
        dma((8, 2)),
        dma((4,)),
        dma((4,)),
        dma((9,)),
        dma((9,)),
        dma((6,)),
        dma((6,)),
        dma((15,)),
        dma((15,)),
        dma((21,)),
        dma((21,)),
    ]
    average, evidence = pl.pallas_call(
        kernel,
        out_shape=(jax.ShapeDtypeStruct((16, 128), F32), jax.ShapeDtypeStruct((1, 64), F32)),
        in_specs=[anywhere] * 5,
        out_specs=(vmem, vmem),
        scratch_shapes=scratch,
        compiler_params=pltpu.CompilerParams(
            collective_id=0, has_side_effects=True, vmem_limit_bytes=60 * 1024 * 1024
        ),
    )(images, references, precision.reshape(1, 64), candidates.T, table)
    return average, evidence.reshape(64)


def solution(mesh):
    in_specs = (P(("img", "blk"), None), P("blk", None), P(("img", "blk")), P(("img", "blk"), None))
    out_specs = (P("blk", "img"), P(("img", "blk")))
    return jax.shard_map(body, mesh=mesh, in_specs=in_specs, out_specs=out_specs, check_vma=False)
```

```python
import math

import jax
import jax.numpy as jnp
import ml_dtypes
import numpy as np
from jax import lax
from jax.experimental import pallas as pl
from jax.experimental.pallas import tpu as pltpu
from jax.sharding import PartitionSpec as P

CYCLES = 32
ORDERS = 64
TURNS = 36
FEATS = 4096
LANES = 128
MESH = pl.DeviceIdType.MESH
F32 = jnp.float32
BF16 = jnp.bfloat16


def spread_table():
    feats = np.arange(FEATS)
    order = feats // (2 * CYCLES)
    turns = np.arange(TURNS)
    angle = 2.0 * math.pi / TURNS * ((turns[:, None] * order[None, :]) % TURNS)
    out = np.zeros((16, 128, 512), np.float32)
    for part, values in enumerate((np.cos(angle), -np.sin(angle))):
        values = values.astype(np.float32).reshape(TURNS, 16, 256).transpose(1, 0, 2)
        high = values.astype(ml_dtypes.bfloat16).astype(np.float32)
        low = values - high
        cols = slice(part * 256, part * 256 + 256)
        out[:, 0:36, cols] = high
        out[:, 40:76, cols] = high
        out[:, 80:116, cols] = low
    return out.astype(ml_dtypes.bfloat16)


def weighted(pairs):
    total = None
    for coef, value in pairs:
        if abs(coef) < 1e-12:
            continue
        if abs(coef - 1.0) < 1e-12:
            term = value
        elif abs(coef + 1.0) < 1e-12:
            term = -value
        else:
            term = value * np.float32(coef)
        total = term if total is None else total + term
    return total


def turns_of(a, b):
    def cos(k, s):
        return math.cos(2.0 * math.pi * (k * s % 36) / 36.0)

    def sin(k, s):
        return math.sin(2.0 * math.pi * (k * s % 36) / 36.0)

    even_c, odd_c, even_s, odd_s = {}, {}, {}, {}
    for s in range(5):
        p = weighted([(cos(k, s), a[k]) for k in range(0, 19, 4)])
        q = weighted([(cos(k, s), a[k]) for k in range(2, 19, 4)])
        even_c[s], even_c[9 - s] = p + q, p - q
    for s in range(9):
        odd_c[s] = weighted([(cos(k, s), a[k]) for k in range(1, 18, 2)])
    for s in range(1, 5):
        p = weighted([(sin(k, s), b[k]) for k in range(4, 17, 4)])
        q = weighted([(sin(k, s), b[k]) for k in range(2, 17, 4)])
        even_s[s], even_s[9 - s] = p + q, q - p
    for s in range(1, 10):
        odd_s[s] = weighted([(sin(k, s), b[k]) for k in range(1, 18, 2)])
    x = [None] * 36
    for s in range(10):
        if s < 9:
            c_lo, c_hi = even_c[s] + odd_c[s], even_c[s] - odd_c[s]
        else:
            c_lo = c_hi = even_c[9]
        if s == 0:
            x[0], x[18] = c_lo, c_hi
        elif s == 9:
            x[9], x[27] = c_lo - odd_s[9], c_lo + odd_s[9]
        else:
            s_lo, s_hi = even_s[s] + odd_s[s], odd_s[s] - even_s[s]
            x[s], x[36 - s] = c_lo - s_lo, c_lo + s_lo
            x[18 - s], x[18 + s] = c_hi - s_hi, c_hi + s_hi
    return x


def tree(op, values):
    values = list(values)
    while len(values) > 1:
        nxt = [op(values[i], values[i + 1]) for i in range(0, len(values) - 1, 2)]
        if len(values) % 2:
            nxt.append(values[-1])
        values = nxt
    return values[0]


def add(p, q):
    return p + q


def dot_nt(a, b, **kw):
    return lax.dot_general(a, b, (((1,), (1,)), ((), ())), preferred_element_type=F32, **kw)


def dot_nn(a, b):
    return jnp.dot(a, b, preferred_element_type=F32)


def kernel(
    images, refs, prec, cand, table, avg_out, evid_out,
    G, IM, IMS, FI, F, PIN, CIN, AUX, AUXS, CHX, CHS, PT, PP, TE, OH, SA, RA, SB, RB, TA, R2A, TB, R2B,
    UZ, SZ, RZ, W0, RW0, W1, RW1, W2, RW2, LS, LR,
    loc, tok, ags, agr, sibs, sibr, s1s, s1r, s2s, s2r, zs, zr, ws, wr,
):
    img, blk = lax.axis_index("img"), lax.axis_index("blk")
    z, x_lo = img % 16, img // 16
    core, y, x_hi = blk % 2, (blk // 2) % 4, blk // 8
    x = x_hi * 2 + x_lo
    q_me = x_hi * 4 + y

    def dev(x_, y_, z_, c_):
        return ((x_ % 2) * 16 + z_, (x_ // 2) * 8 + y_ * 2 + c_)

    sib = dev(x, y, z, 1 - core)
    x_opp, x_same = 3 - x, x_hi * 2 + 1 - x_lo
    zb = z % 2
    z_pair, z_other = (z + 1 - 2 * zb) % 16, (z + 15 + 2 * zb) % 16
    same, pair, other_z = dev(x_same, y, z, core), dev(x, y, z_pair, core), dev(x, y, z_other, core)
    diagonal = dev(x_same, y, z_pair, core)

    def at_y(d):
        return dev(x, (y + d) % 4, z, core)

    def at_x(d):
        return dev((x + d) % 4, y, z, core)

    def at_z(d):
        return dev(x, y, (z + d) % 16, core)

    sent = []
    far_first = sorted(range(1, 16), key=lambda d: -min(d, 16 - d))

    def send(src, dst, ssem, rsem, to):
        copy = pltpu.make_async_remote_copy(
            src_ref=src, dst_ref=dst, send_sem=ssem, recv_sem=rsem, device_id=to, device_id_type=MESH
        )
        copy.start()
        sent.append(copy)

    def arrived(dst, rsem):
        pltpu.make_async_copy(dst, dst, rsem).wait()

    mine_rows = pl.ds(pl.multiple_of(core * 64, 64), 64)
    own_p = pltpu.make_async_copy(prec, PIN, loc.at[3])
    own_p.start()
    own_c = pltpu.make_async_copy(cand, CIN, loc.at[4])
    own_c.start()
    own_g = pltpu.make_async_copy(refs, G.at[pl.ds(pl.multiple_of(q_me * 16, 16), 16)], loc.at[1])
    own_g.start()
    own_im = pltpu.make_async_copy(images, IM.at[mine_rows], loc.at[0])
    own_im.start()
    own_t = pltpu.make_async_copy(table, TE, loc.at[2])
    own_t.start()

    barrier = pltpu.get_barrier_semaphore()
    partners = [dev(x_opp, (y + d) % 4, z, core) for d in range(1, 4)]
    partners += [at_y(d) for d in range(1, 4)] + [at_x(d) for d in range(1, 4)]
    partners += [diagonal, pair, other_z, sib]
    for to in partners:
        pl.semaphore_signal(barrier, inc=1, device_id=to, device_id_type=MESH)
    own_p.wait()
    own_c.wait()
    mine = jnp.concatenate([PIN[...], CIN[...].astype(F32)], axis=0)
    AUX[0:3, :] = jnp.concatenate([mine, mine], axis=1)
    AUX[3:8, :] = jnp.zeros((5, 128), F32)
    pl.semaphore_wait(barrier, len(partners))

    def token(n):
        for d in (1 << n, 16 - (1 << n)):
            pl.semaphore_signal(tok.at[n], inc=1, device_id=at_z(d), device_id_type=MESH)

    def rows_at(q):
        return pl.ds(pl.multiple_of(q * 16, 16), 16)

    def half(q, n):
        return G.at[rows_at(q), pl.ds(pl.multiple_of(n * 2048, 2048), 2048)]

    def quarter(q, n):
        return G.at[rows_at(q), pl.ds(pl.multiple_of(n * 1024, 1024), 1024)]

    mine_f, same_f = 2 * x_lo + zb, 2 * (1 - x_lo) + zb
    pair_f, diagonal_f = 2 * x_lo + 1 - zb, 2 * (1 - x_lo) + 1 - zb
    col, far = x_hi * 4, (1 - x_hi) * 4
    order = (0, 1, 3, 2)

    def near_q(d):
        return col + (y + d) % 4

    def far_q(d):
        return far + (y + d) % 4

    send(AUX, AUXS, sibs.at[1], sibr.at[1], sib)
    send(images, IM.at[mine_rows], sibs.at[0], sibr.at[0], sib)
    opp_quarter = refs.at[:, pl.ds(pl.multiple_of(same_f * 1024, 1024), 1024)]
    own_half = refs.at[:, pl.ds(pl.multiple_of(zb * 2048, 2048), 2048)]
    for n, d in enumerate(order):
        to = dev(x_opp, (y + d) % 4, z, core)
        send(opp_quarter, quarter(q_me, same_f), ags.at[n], agr.at[q_me, same_f], to)
    for n, d in enumerate((1, 3, 2)):
        send(own_half, half(q_me, zb), ags.at[4 + n], agr.at[q_me, zb], at_y(d))
    token(0)
    own_im.wait()
    arrived(IM.at[pl.ds(pl.multiple_of((1 - core) * 64, 64), 64)], sibr.at[0])
    arrived(AUXS, sibr.at[1])

    row = lax.broadcasted_iota(jnp.int32, (128, 128), 0)
    lane = lax.broadcasted_iota(jnp.int32, (128, 128), 1)

    def swap(src, dst):
        first = dst % 64 < 32
        return jnp.where(first & (src == dst + 32), 1.0, jnp.where((~first) & (src == dst - 32), -1.0, 0.0))

    eye = jnp.where(row == lane, 1.0, 0.0)
    rows_of = jnp.concatenate([eye, swap(lane, row)], axis=0).astype(BF16)
    cols_of = swap(row, lane).astype(BF16)

    def prepare(first, count, half):
        def step(n, carry):
            t = first + n
            block = IM[:, pl.ds(pl.multiple_of(t * 128, 128), 128)]
            both = dot_nt(rows_of, block)
            j = t - 18 * half
            sign = jnp.where(j < 9, 1.0, -1.0).astype(F32)
            FI[j, half * 128 : half * 128 + 128, 0:128] = both[0:128].astype(BF16)
            FI[j, half * 128 : half * 128 + 128, 128:256] = (both[128:256] * sign).astype(BF16)
            IMS[:, pl.ds(pl.multiple_of(t * 128, 128), 128)] = dot_nn(block, cols_of).astype(BF16)
            return carry

        lax.fori_loop(0, count, step, 0, unroll=2)

    def hand_far(n):
        q = far_q(order[n])
        part, sem = quarter(q, mine_f), agr.at[q, mine_f]
        arrived(part, sem)
        for m, to in enumerate((diagonal, same, pair)):
            send(part, part, ags.at[10 + 3 * n + m], sem, to)

    def hand_near(n):
        q = near_q((1, 3, 2)[n])
        part, sem = half(q, zb), agr.at[q, zb]
        arrived(part, sem)
        send(part, part, ags.at[7 + n], sem, other_z)

    prepare(0, 4, 0)
    hand_far(0)
    prepare(4, 2, 0)
    hand_far(1)
    hand_far(2)
    hand_near(0)
    hand_near(1)
    prepare(6, 2, 0)
    hand_far(3)
    hand_near(2)
    pl.semaphore_wait(tok.at[0], 2)
    token(1)
    prepare(8, 10, 0)
    prepare(18, 14, 1)

    right = lax.broadcasted_iota(jnp.int32, (8, 128), 1) >= 64
    auxc = jnp.where(right == (core == 1), AUX[...], AUXS[...])
    precision = auxc[0:1, :]
    class_id = ((row // 16) * 32 + core * 16 + row % 16).astype(F32)
    picks = [auxc[1:2, :] == class_id, auxc[2:3, :] == class_id]
    for k in range(2):
        OH[:, k * 128 : k * 128 + 128] = jnp.where(picks[k], 1.0, 0.0).astype(BF16)
    PT[...] = jnp.zeros_like(PT)

    own_g.wait()
    for d in (1, 3, 2):
        q = near_q(d)
        arrived(half(q, 1 - zb), agr.at[q, 1 - zb])

    low = (lax.broadcasted_iota(jnp.int32, (64, 256), 1) % 128) < 64

    def harmonics(first):
        rows = pl.ds(pl.multiple_of(first * 16, 64), 64)
        for j in range(18):
            left = G[rows, j * 128 : j * 128 + 128]
            if j < 14:
                tile = jnp.concatenate([left, G[rows, (18 + j) * 128 : (18 + j) * 128 + 128]], axis=1)
                keep, right_side = low, FI[j]
            else:
                tile, keep, right_side = left, low[:, 0:128], FI[j, 0:128, :]
            zero = jnp.zeros_like(tile)
            stacked = jnp.concatenate([jnp.where(keep, tile, zero), jnp.where(keep, zero, tile)], axis=0)
            out = dot_nn(stacked, right_side)
            even, odd = out[0:64], out[64:128]
            k_even, k_odd = (2 * j if j <= 9 else 36 - 2 * j), (2 * j + 1 if j <= 8 else 35 - 2 * j)
            if j <= 9:
                F[k_even, rows, :] = even[:, 0:128]
            else:
                F[k_even, rows, :] += even[:, 0:128]
            if 0 < k_even < 18:
                if j <= 9:
                    F[18 + k_even, rows, :] = even[:, 128:256]
                else:
                    F[18 + k_even, rows, :] += even[:, 128:256]
            if j <= 8:
                F[k_odd, rows, :] = odd[:, 0:128]
                F[18 + k_odd, rows, :] = odd[:, 128:256]
            else:
                F[k_odd, rows, :] += odd[:, 0:128]
                F[18 + k_odd, rows, :] += odd[:, 128:256]
        square = jnp.zeros((64, 128), F32)
        for t in range(32):
            value = G[rows, t * 128 : t * 128 + 128].astype(F32)
            square = square + value * value
        F[36, rows, :] = jnp.broadcast_to(0.5 * jnp.sum(square, axis=1, keepdims=True), (64, 128))

    even_row = lax.broadcasted_iota(jnp.int32, (8, 128), 0) % 2 == 0

    def choose(first, more):
        rows = pl.ds(pl.multiple_of(first * 16, 64), 64)
        ids = (((row[0:64] // 16) + first) * 32 + core * 16 + row[0:64] % 16).astype(F32)
        keep = [auxc[k : k + 1, :] == ids for k in (1, 2)]

        def step(kk, carry):
            f = F[kk, rows, :]
            parts = []
            for k in range(2):
                kept = jnp.where(keep[k], f, 0.0)
                total = tree(add, [kept[n * 8 : n * 8 + 8] for n in range(8)])
                parts.append(total + pltpu.roll(total, 1, 0))
            both = jnp.where(even_row, parts[0], parts[1])
            both = both + pltpu.roll(both, 2, 0)
            both = both + pltpu.roll(both, 4, 0)
            CHX[kk] = CHX[kk] + both if more else both
            return carry

        lax.fori_loop(0, 36, step, 0, unroll=4)
        step(36, 0)

    harmonics(col)
    choose(col, False)
    pl.semaphore_wait(tok.at[1], 2)
    token(2)
    for d in order:
        for f in (same_f, pair_f, diagonal_f):
            arrived(quarter(far_q(d), f), agr.at[far_q(d), f])
    harmonics(far)
    choose(far, True)
    send(CHX, CHS, sibs.at[2], sibr.at[2], sib)
    arrived(CHS, sibr.at[2])

    coefs = [CHX[k] + CHS[k] for k in range(37)]
    turned = turns_of(coefs[0:19], [None] + coefs[19:36])
    scores = [precision * (v - coefs[36]) for v in turned]
    peak = tree(jnp.maximum, scores)
    peak = jnp.maximum(peak, jnp.where(even_row, pltpu.roll(peak, 7, 0), pltpu.roll(peak, 1, 0)))
    exps = [jnp.exp(v - peak) for v in scores]
    total = tree(add, exps)
    total = total + jnp.where(even_row, pltpu.roll(total, 7, 0), pltpu.roll(total, 1, 0))
    posterior = [v / total for v in exps]
    share = tree(add, posterior)
    for s in range(TURNS):
        high = posterior[s].astype(BF16).astype(F32)
        rest = posterior[s] - high
        for k in range(2):
            PT[k, s : s + 1, :] = high[k : k + 1]
            PT[k, 40 + s : 41 + s, :] = rest[k : k + 1]
            PT[k, 80 + s : 81 + s, :] = high[k : k + 1]
    for k in range(2):
        PP[k * 128 : k * 128 + 128, :] = PT[k].T.astype(BF16)
    own_t.wait()

    onehot = OH[...]

    def sums(x_half, second):
        def step(v, carry):
            u = x_half * 8 + second * 4 + v
            lanes = pl.ds(pl.multiple_of(u * 256, 256), 256)
            out_lanes = pl.ds(pl.multiple_of(v * 256, 256), 256)
            factor = dot_nn(PP[...], TE[u])
            straight, turned_in = IM[:, lanes].astype(F32), IMS[:, lanes].astype(F32)
            rows = [
                (
                    straight * factor[k * 128 : k * 128 + 128, 0:256]
                    - turned_in * factor[k * 128 : k * 128 + 128, 256:512]
                ).astype(BF16)
                for k in range(2)
            ]
            out = dot_nn(onehot, jnp.concatenate(rows, axis=0)).astype(BF16)
            for q in range(8):
                block = out[q * 16 : q * 16 + 16]
                if second:
                    SB[(q // 4) * 2 + x_half, q % 4, :, out_lanes] = block
                else:
                    SA[x_half, q % 4, q // 4, :, out_lanes] = block
            return carry

        lax.fori_loop(0, 4, step, 0, unroll=True)

    other = 1 - x_lo
    for pos, x_half in enumerate((other, x_lo)):
        sums(x_half, 0)
        for d in (2, 1, 3):
            n = pos * 3 + d - 1
            send(SA.at[x_half, (y + d) % 4], RA.at[d - 1, x_half], s1s.at[n], s1r.at[n], at_y(d))
        sums(x_half, 1)
        for d in ((1, 3), (2,))[pos]:
            send(SB.at[(x + d) % 4], RB.at[d - 1], s1s.at[5 + d], s1r.at[5 + d], at_x(d))
    shares = jnp.concatenate(
        [jnp.broadcast_to(share[0:1], (8, 128)), jnp.broadcast_to(share[1:2], (8, 128))], axis=1
    )
    W0[...] = dot_nt(shares, onehot.astype(F32), precision=lax.Precision.HIGHEST)
    pl.semaphore_wait(tok.at[2], 2)
    for d in far_first:
        send(W0, RW0.at[d - 1], ws.at[d - 1], wr.at[d - 1], at_z(d))

    def block_scores(n, carry):
        run_peak, run_total = carry
        rows = pl.ds(pl.multiple_of(n * 8, 8), 8)
        f = [F[k, rows, :] for k in range(37)]
        turned = turns_of(f[0:19], [None] + f[19:36])
        scores = [precision * (v - f[36]) for v in turned]
        new_peak = jnp.maximum(run_peak, tree(jnp.maximum, scores))
        total = tree(add, [jnp.exp(v - new_peak) for v in scores])
        return new_peak, run_total * jnp.exp(run_peak - new_peak) + total

    start = (jnp.full((8, 128), -jnp.inf, F32), jnp.zeros((8, 128), F32))
    run_peak, run_total = lax.fori_loop(0, 16, block_scores, start)
    peak = jnp.max(run_peak, axis=0, keepdims=True)
    total = jnp.sum(run_total * jnp.exp(run_peak - peak), axis=0, keepdims=True)
    LS[0:8] = jnp.broadcast_to(peak, (8, 128))
    LS[8:16] = jnp.broadcast_to(total, (8, 128))
    send(LS, LR, sibs.at[3], sibr.at[3], sib)

    for pos, x_half in enumerate((other, x_lo)):
        for d in range(1, 4):
            arrived(RA.at[d - 1, x_half], s1r.at[pos * 3 + d - 1])
    for x_half in range(2):
        for x_top in range(2):
            total = SA[x_half, y, x_top].astype(F32)
            for d in range(3):
                total = total + RA[d, x_half, x_top].astype(F32)
            TA[x_top * 2 + x_half] = total
    for d in range(1, 4):
        send(TA.at[(x + d) % 4], R2A.at[d - 1], s2s.at[d - 1], s2r.at[d - 1], at_x(d))
    for d in range(1, 4):
        arrived(RB.at[d - 1], s1r.at[5 + d])
    for y_to in range(4):
        total = SB[x, y_to].astype(F32)
        for d in range(3):
            total = total + RB[d, y_to].astype(F32)
        TB[y_to] = total
    for d in range(1, 4):
        send(TB.at[(y + d) % 4], R2B.at[d - 1], s2s.at[2 + d], s2r.at[2 + d], at_y(d))

    arrived(LR, sibr.at[3])
    peak = jnp.maximum(LS[0:8], LR[0:8])
    total = LS[8:16] * jnp.exp(LS[0:8] - peak) + LR[8:16] * jnp.exp(LR[0:8] - peak)
    evidence = peak + jnp.log(total)
    evid_out[...] = jnp.where(core == 0, evidence[0:1, 0:64], evidence[0:1, 64:128])

    for d in range(1, 16):
        arrived(RW0.at[d - 1], wr.at[d - 1])
    W1[...] = tree(add, [W0[...]] + [RW0[d] for d in range(15)])
    for d in range(1, 4):
        send(W1, RW1.at[d - 1], ws.at[14 + d], wr.at[14 + d], at_y(d))

    for d in range(1, 4):
        arrived(R2A.at[d - 1], s2r.at[d - 1])
    total = TA[x] + R2A[0] + R2A[1] + R2A[2]
    for n in range(8):
        UZ[n] = total[:, n * 128 : n * 128 + 128]
    for d in range(1, 4):
        arrived(R2B.at[d - 1], s2r.at[2 + d])
    total = TB[y] + R2B[0] + R2B[1] + R2B[2]
    for n in range(8):
        UZ[8 + n] = total[:, n * 128 : n * 128 + 128]
    SZ[...] = UZ[...].astype(BF16)
    for d in far_first:
        send(SZ.at[(z + d) % 16], RZ.at[d - 1], zs.at[d - 1], zr.at[d - 1], at_z(d))

    for d in range(1, 4):
        arrived(RW1.at[d - 1], wr.at[14 + d])
    W2[...] = tree(add, [W1[...]] + [RW1[d] for d in range(3)])
    for d in range(1, 4):
        send(W2, RW2.at[d - 1], ws.at[17 + d], wr.at[17 + d], at_x(d))

    for d in range(1, 4):
        arrived(RW2.at[d - 1], wr.at[17 + d])
    weight = tree(add, [W2[...]] + [RW2[d] for d in range(3)])
    pick = lane[0:16] == row[0:16] + q_me * 16
    weight = jnp.sum(jnp.where(pick, jnp.broadcast_to(weight[0:1], (16, 128)), 0.0), axis=1, keepdims=True)
    for d in range(1, 16):
        arrived(RZ.at[d - 1], zr.at[d - 1])
    total = tree(add, [UZ[z]] + [RZ[d].astype(F32) for d in range(15)])
    avg_out[...] = total / (1.0 + weight)
    for copy in sent:
        copy.wait_send()


def body(images, references, precision, candidates):
    table = jnp.asarray(spread_table())
    anywhere = pl.BlockSpec(memory_space=pltpu.HBM)
    vmem = pl.BlockSpec(memory_space=pltpu.VMEM)
    dma = pltpu.SemaphoreType.DMA
    scratch = [
        pltpu.VMEM((128, 4096), BF16),
        pltpu.VMEM((128, 4096), BF16),
        pltpu.VMEM((128, 4096), BF16),
        pltpu.VMEM((18, 256, 256), BF16),
        pltpu.VMEM((37, 128, 128), F32),
        pltpu.VMEM((1, 64), F32),
        pltpu.VMEM((2, 64), jnp.int32),
        pltpu.VMEM((8, 128), F32),
        pltpu.VMEM((8, 128), F32),
        pltpu.VMEM((37, 8, 128), F32),
        pltpu.VMEM((37, 8, 128), F32),
        pltpu.VMEM((2, 128, 128), F32),
        pltpu.VMEM((256, 128), BF16),
        pltpu.VMEM((16, 128, 512), BF16),
        pltpu.VMEM((128, 256), BF16),
        pltpu.VMEM((2, 4, 2, 16, 1024), BF16),
        pltpu.VMEM((3, 2, 2, 16, 1024), BF16),
        pltpu.VMEM((4, 4, 16, 1024), BF16),
        pltpu.VMEM((3, 4, 16, 1024), BF16),
        pltpu.VMEM((4, 16, 1024), F32),
        pltpu.VMEM((3, 16, 1024), F32),
        pltpu.VMEM((4, 16, 1024), F32),
        pltpu.VMEM((3, 16, 1024), F32),
        pltpu.VMEM((16, 16, 128), F32),
        pltpu.VMEM((16, 16, 128), BF16),
        pltpu.VMEM((15, 16, 128), BF16),
        pltpu.VMEM((8, 128), F32),
        pltpu.VMEM((15, 8, 128), F32),
        pltpu.VMEM((8, 128), F32),
        pltpu.VMEM((3, 8, 128), F32),
        pltpu.VMEM((8, 128), F32),
        pltpu.VMEM((3, 8, 128), F32),
        pltpu.VMEM((16, 128), F32),
        pltpu.VMEM((16, 128), F32),
        dma((5,)),
        pltpu.SemaphoreType.REGULAR((3,)),
        dma((22,)),
        dma((8, 4)),
        dma((4,)),
        dma((4,)),
        dma((9,)),
        dma((9,)),
        dma((6,)),
        dma((6,)),
        dma((15,)),
        dma((15,)),
        dma((21,)),
        dma((21,)),
    ]
    average, evidence = pl.pallas_call(
        kernel,
        out_shape=(jax.ShapeDtypeStruct((16, 128), F32), jax.ShapeDtypeStruct((1, 64), F32)),
        in_specs=[anywhere] * 5,
        out_specs=(vmem, vmem),
        scratch_shapes=scratch,
        compiler_params=pltpu.CompilerParams(
            collective_id=0, has_side_effects=True, vmem_limit_bytes=55200 * 1024
        ),
    )(images, references, precision.reshape(1, 64), candidates.T, table)
    return average, evidence.reshape(64)


def solution(mesh):
    in_specs = (P(("img", "blk"), None), P("blk", None), P(("img", "blk")), P(("img", "blk"), None))
    out_specs = (P("blk", "img"), P(("img", "blk")))
    return jax.shard_map(body, mesh=mesh, in_specs=in_specs, out_specs=out_specs, check_vma=False)
```

```python
import math

import jax
import jax.numpy as jnp
import ml_dtypes
import numpy as np
from jax import lax
from jax.experimental import pallas as pl
from jax.experimental.pallas import tpu as pltpu
from jax.sharding import PartitionSpec as P

CYCLES = 32
ORDERS = 64
TURNS = 36
FEATS = 4096
LANES = 128
MESH = pl.DeviceIdType.MESH
F32 = jnp.float32
BF16 = jnp.bfloat16


def factor_table():
    turns = np.arange(TURNS)
    angle = 2.0 * math.pi / TURNS * ((np.arange(ORDERS)[:, None] * turns[None, :]) % TURNS)
    values = np.stack([np.cos(angle), -np.sin(angle)], axis=1).reshape(2 * ORDERS, TURNS).astype(np.float32)
    high = values.astype(ml_dtypes.bfloat16).astype(np.float32)
    out = np.zeros((128, 128), np.float32)
    out[:, 0:36] = high
    out[:, 40:76] = high
    out[:, 80:116] = values - high
    return out.astype(ml_dtypes.bfloat16)


def weighted(pairs):
    total = None
    for coef, value in pairs:
        if abs(coef) < 1e-12:
            continue
        if abs(coef - 1.0) < 1e-12:
            term = value
        elif abs(coef + 1.0) < 1e-12:
            term = -value
        else:
            term = value * np.float32(coef)
        total = term if total is None else total + term
    return total


def turns_of(a, b):
    def cos(k, s):
        return math.cos(2.0 * math.pi * (k * s % 36) / 36.0)

    def sin(k, s):
        return math.sin(2.0 * math.pi * (k * s % 36) / 36.0)

    even_c, odd_c, even_s, odd_s = {}, {}, {}, {}
    for s in range(5):
        p = weighted([(cos(k, s), a[k]) for k in range(0, 19, 4)])
        q = weighted([(cos(k, s), a[k]) for k in range(2, 19, 4)])
        even_c[s], even_c[9 - s] = p + q, p - q
    for s in range(9):
        odd_c[s] = weighted([(cos(k, s), a[k]) for k in range(1, 18, 2)])
    for s in range(1, 5):
        p = weighted([(sin(k, s), b[k]) for k in range(4, 17, 4)])
        q = weighted([(sin(k, s), b[k]) for k in range(2, 17, 4)])
        even_s[s], even_s[9 - s] = p + q, q - p
    for s in range(1, 10):
        odd_s[s] = weighted([(sin(k, s), b[k]) for k in range(1, 18, 2)])
    x = [None] * 36
    for s in range(10):
        if s < 9:
            c_lo, c_hi = even_c[s] + odd_c[s], even_c[s] - odd_c[s]
        else:
            c_lo = c_hi = even_c[9]
        if s == 0:
            x[0], x[18] = c_lo, c_hi
        elif s == 9:
            x[9], x[27] = c_lo - odd_s[9], c_lo + odd_s[9]
        else:
            s_lo, s_hi = even_s[s] + odd_s[s], odd_s[s] - even_s[s]
            x[s], x[36 - s] = c_lo - s_lo, c_lo + s_lo
            x[18 - s], x[18 + s] = c_hi - s_hi, c_hi + s_hi
    return x


def tree(op, values):
    values = list(values)
    while len(values) > 1:
        nxt = [op(values[i], values[i + 1]) for i in range(0, len(values) - 1, 2)]
        if len(values) % 2:
            nxt.append(values[-1])
        values = nxt
    return values[0]


def add(p, q):
    return p + q


def dot_nt(a, b, **kw):
    return lax.dot_general(a, b, (((1,), (1,)), ((), ())), preferred_element_type=F32, **kw)


def dot_nn(a, b):
    return jnp.dot(a, b, preferred_element_type=F32)


def kernel(
    images, refs, prec, cand, table, avg_out, evid_out,
    G, IM, FI, F, PIN, CIN, AUX, AUXS, CHX, CHS, PT, H, TE, OH, SA, RA, SB, RB, TA, R2A, TB, R2B,
    UZ, SZ, RZ, W0, RW0, W1, RW1, W2, RW2, LS, LR,
    loc, tok, ags, agr, sibs, sibr, s1s, s1r, s2s, s2r, zs, zr, ws, wr,
):
    img, blk = lax.axis_index("img"), lax.axis_index("blk")
    z, x_lo = img % 16, img // 16
    core, y, x_hi = blk % 2, (blk // 2) % 4, blk // 8
    x = x_hi * 2 + x_lo
    q_me = x_hi * 4 + y

    def dev(x_, y_, z_, c_):
        return ((x_ % 2) * 16 + z_, (x_ // 2) * 8 + y_ * 2 + c_)

    sib = dev(x, y, z, 1 - core)
    x_opp, x_same = 3 - x, x_hi * 2 + 1 - x_lo
    zb = z % 2
    z_pair, z_other = (z + 1 - 2 * zb) % 16, (z + 15 + 2 * zb) % 16
    same, pair, other_z = dev(x_same, y, z, core), dev(x, y, z_pair, core), dev(x, y, z_other, core)
    diagonal = dev(x_same, y, z_pair, core)

    def at_y(d):
        return dev(x, (y + d) % 4, z, core)

    def at_x(d):
        return dev((x + d) % 4, y, z, core)

    def at_z(d):
        return dev(x, y, (z + d) % 16, core)

    sent = []
    far_first = sorted(range(1, 16), key=lambda d: -min(d, 16 - d))

    def send(src, dst, ssem, rsem, to):
        copy = pltpu.make_async_remote_copy(
            src_ref=src, dst_ref=dst, send_sem=ssem, recv_sem=rsem, device_id=to, device_id_type=MESH
        )
        copy.start()
        sent.append(copy)

    def arrived(dst, rsem):
        pltpu.make_async_copy(dst, dst, rsem).wait()

    mine_rows = pl.ds(pl.multiple_of(core * 64, 64), 64)
    own_p = pltpu.make_async_copy(prec, PIN, loc.at[3])
    own_p.start()
    own_c = pltpu.make_async_copy(cand, CIN, loc.at[4])
    own_c.start()
    own_g = pltpu.make_async_copy(refs, G.at[pl.ds(pl.multiple_of(q_me * 16, 16), 16)], loc.at[1])
    own_g.start()
    own_im = pltpu.make_async_copy(images, IM.at[mine_rows], loc.at[0])
    own_im.start()
    own_t = pltpu.make_async_copy(table, TE, loc.at[2])
    own_t.start()

    barrier = pltpu.get_barrier_semaphore()
    partners = [dev(x_opp, (y + d) % 4, z, core) for d in range(1, 4)]
    partners += [at_y(d) for d in range(1, 4)] + [at_x(d) for d in range(1, 4)]
    partners += [diagonal, pair, other_z, sib]
    for to in partners:
        pl.semaphore_signal(barrier, inc=1, device_id=to, device_id_type=MESH)
    own_p.wait()
    own_c.wait()
    mine = jnp.concatenate([PIN[...], CIN[...].astype(F32)], axis=0)
    AUX[0:3, :] = jnp.concatenate([mine, mine], axis=1)
    AUX[3:8, :] = jnp.zeros((5, 128), F32)
    pl.semaphore_wait(barrier, len(partners))

    def token(n):
        for d in (1 << n, 16 - (1 << n)):
            pl.semaphore_signal(tok.at[n], inc=1, device_id=at_z(d), device_id_type=MESH)

    def rows_at(q):
        return pl.ds(pl.multiple_of(q * 16, 16), 16)

    def half(q, n):
        return G.at[rows_at(q), pl.ds(pl.multiple_of(n * 2048, 2048), 2048)]

    def quarter(q, n):
        return G.at[rows_at(q), pl.ds(pl.multiple_of(n * 1024, 1024), 1024)]

    mine_f, same_f = 2 * x_lo + zb, 2 * (1 - x_lo) + zb
    pair_f, diagonal_f = 2 * x_lo + 1 - zb, 2 * (1 - x_lo) + 1 - zb
    col, far = x_hi * 4, (1 - x_hi) * 4
    order = (0, 1, 3, 2)

    def near_q(d):
        return col + (y + d) % 4

    def far_q(d):
        return far + (y + d) % 4

    send(AUX, AUXS, sibs.at[1], sibr.at[1], sib)
    send(images, IM.at[mine_rows], sibs.at[0], sibr.at[0], sib)
    opp_quarter = refs.at[:, pl.ds(pl.multiple_of(same_f * 1024, 1024), 1024)]
    own_half = refs.at[:, pl.ds(pl.multiple_of(zb * 2048, 2048), 2048)]
    for n, d in enumerate(order):
        to = dev(x_opp, (y + d) % 4, z, core)
        send(opp_quarter, quarter(q_me, same_f), ags.at[n], agr.at[q_me, same_f], to)
    for n, d in enumerate((1, 3, 2)):
        send(own_half, half(q_me, zb), ags.at[4 + n], agr.at[q_me, zb], at_y(d))
    token(0)
    own_im.wait()
    arrived(IM.at[pl.ds(pl.multiple_of((1 - core) * 64, 64), 64)], sibr.at[0])
    arrived(AUXS, sibr.at[1])

    row = lax.broadcasted_iota(jnp.int32, (128, 128), 0)
    lane = lax.broadcasted_iota(jnp.int32, (128, 128), 1)

    def swap(src, dst):
        first = dst % 64 < 32
        return jnp.where(first & (src == dst + 32), 1.0, jnp.where((~first) & (src == dst - 32), -1.0, 0.0))

    eye = jnp.where(row == lane, 1.0, 0.0)
    rows_of = jnp.concatenate([eye, swap(lane, row)], axis=0).astype(BF16)

    def prepare(first, count, half):
        def step(n, carry):
            t = first + n
            block = IM[:, pl.ds(pl.multiple_of(t * 128, 128), 128)]
            both = dot_nt(rows_of, block)
            j = t - 18 * half
            sign = jnp.where(j < 9, 1.0, -1.0).astype(F32)
            FI[j, half * 128 : half * 128 + 128, 0:128] = both[0:128].astype(BF16)
            FI[j, half * 128 : half * 128 + 128, 128:256] = (both[128:256] * sign).astype(BF16)
            return carry

        lax.fori_loop(0, count, step, 0, unroll=2)

    def hand_far(n):
        q = far_q(order[n])
        part, sem = quarter(q, mine_f), agr.at[q, mine_f]
        arrived(part, sem)
        for m, to in enumerate((diagonal, same, pair)):
            send(part, part, ags.at[10 + 3 * n + m], sem, to)

    def hand_near(n):
        q = near_q((1, 3, 2)[n])
        part, sem = half(q, zb), agr.at[q, zb]
        arrived(part, sem)
        send(part, part, ags.at[7 + n], sem, other_z)

    prepare(0, 4, 0)
    hand_far(0)
    prepare(4, 2, 0)
    hand_far(1)
    hand_far(2)
    hand_near(0)
    hand_near(1)
    prepare(6, 2, 0)
    hand_far(3)
    hand_near(2)
    pl.semaphore_wait(tok.at[0], 2)
    token(1)
    prepare(8, 10, 0)
    prepare(18, 14, 1)

    right = lax.broadcasted_iota(jnp.int32, (8, 128), 1) >= 64
    auxc = jnp.where(right == (core == 1), AUX[...], AUXS[...])
    precision = auxc[0:1, :]
    class_id = ((row // 16) * 32 + core * 16 + row % 16).astype(F32)
    picks = [auxc[1:2, :] == class_id, auxc[2:3, :] == class_id]
    for k in range(2):
        OH[:, k * 128 : k * 128 + 128] = jnp.where(picks[k], 1.0, 0.0).astype(BF16)
    PT[...] = jnp.zeros_like(PT)

    own_g.wait()
    for d in (1, 3, 2):
        q = near_q(d)
        arrived(half(q, 1 - zb), agr.at[q, 1 - zb])

    low = (lax.broadcasted_iota(jnp.int32, (64, 256), 1) % 128) < 64

    def harmonics(first):
        rows = pl.ds(pl.multiple_of(first * 16, 64), 64)
        for j in range(18):
            left = G[rows, j * 128 : j * 128 + 128]
            if j < 14:
                tile = jnp.concatenate([left, G[rows, (18 + j) * 128 : (18 + j) * 128 + 128]], axis=1)
                keep, right_side = low, FI[j]
            else:
                tile, keep, right_side = left, low[:, 0:128], FI[j, 0:128, :]
            zero = jnp.zeros_like(tile)
            stacked = jnp.concatenate([jnp.where(keep, tile, zero), jnp.where(keep, zero, tile)], axis=0)
            out = dot_nn(stacked, right_side)
            even, odd = out[0:64], out[64:128]
            k_even, k_odd = (2 * j if j <= 9 else 36 - 2 * j), (2 * j + 1 if j <= 8 else 35 - 2 * j)
            if j <= 9:
                F[k_even, rows, :] = even[:, 0:128]
            else:
                F[k_even, rows, :] += even[:, 0:128]
            if 0 < k_even < 18:
                if j <= 9:
                    F[18 + k_even, rows, :] = even[:, 128:256]
                else:
                    F[18 + k_even, rows, :] += even[:, 128:256]
            if j <= 8:
                F[k_odd, rows, :] = odd[:, 0:128]
                F[18 + k_odd, rows, :] = odd[:, 128:256]
            else:
                F[k_odd, rows, :] += odd[:, 0:128]
                F[18 + k_odd, rows, :] += odd[:, 128:256]
        square = jnp.zeros((64, 128), F32)
        for t in range(32):
            value = G[rows, t * 128 : t * 128 + 128].astype(F32)
            square = square + value * value
        F[36, rows, :] = jnp.broadcast_to(0.5 * jnp.sum(square, axis=1, keepdims=True), (64, 128))

    even_row = lax.broadcasted_iota(jnp.int32, (8, 128), 0) % 2 == 0

    def choose(first, more):
        rows = pl.ds(pl.multiple_of(first * 16, 64), 64)
        ids = (((row[0:64] // 16) + first) * 32 + core * 16 + row[0:64] % 16).astype(F32)
        keep = [auxc[k : k + 1, :] == ids for k in (1, 2)]

        def step(kk, carry):
            f = F[kk, rows, :]
            parts = []
            for k in range(2):
                kept = jnp.where(keep[k], f, 0.0)
                total = tree(add, [kept[n * 8 : n * 8 + 8] for n in range(8)])
                parts.append(total + pltpu.roll(total, 1, 0))
            both = jnp.where(even_row, parts[0], parts[1])
            both = both + pltpu.roll(both, 2, 0)
            both = both + pltpu.roll(both, 4, 0)
            CHX[kk] = CHX[kk] + both if more else both
            return carry

        lax.fori_loop(0, 36, step, 0, unroll=4)
        step(36, 0)

    harmonics(col)
    choose(col, False)
    pl.semaphore_wait(tok.at[1], 2)
    token(2)
    for d in order:
        for f in (same_f, pair_f, diagonal_f):
            arrived(quarter(far_q(d), f), agr.at[far_q(d), f])
    harmonics(far)
    choose(far, True)
    send(CHX, CHS, sibs.at[2], sibr.at[2], sib)
    arrived(CHS, sibr.at[2])

    coefs = [CHX[k] + CHS[k] for k in range(37)]
    turned = turns_of(coefs[0:19], [None] + coefs[19:36])
    scores = [precision * (v - coefs[36]) for v in turned]
    peak = tree(jnp.maximum, scores)
    peak = jnp.maximum(peak, jnp.where(even_row, pltpu.roll(peak, 7, 0), pltpu.roll(peak, 1, 0)))
    exps = [jnp.exp(v - peak) for v in scores]
    total = tree(add, exps)
    total = total + jnp.where(even_row, pltpu.roll(total, 7, 0), pltpu.roll(total, 1, 0))
    posterior = [v / total for v in exps]
    share = tree(add, posterior)
    for s in range(TURNS):
        high = posterior[s].astype(BF16).astype(F32)
        rest = posterior[s] - high
        for k in range(2):
            PT[k, s : s + 1, :] = high[k : k + 1]
            PT[k, 40 + s : 41 + s, :] = rest[k : k + 1]
            PT[k, 80 + s : 81 + s, :] = high[k : k + 1]
    own_t.wait()
    for k in range(2):
        H[k] = dot_nn(TE[...], PT[k].astype(BF16))

    onehot = OH[...]

    def sums(x_half, second):
        def step(v, carry):
            u = x_half * 8 + second * 4 + v
            out_lanes = pl.ds(pl.multiple_of(v * 256, 256), 256)
            upper = u // 9
            factors = [H[k, pl.ds(pl.multiple_of(u * 8, 8), 8), :] for k in range(2)]
            columns = [[], []]
            for part in range(2):
                rows = pl.ds(pl.multiple_of(upper * 128, 128), 128)
                tile = FI[2 * u + part - 18 * upper, rows, 0:128].astype(F32)
                for m in range(2):
                    real, imag = tile[m * 64 : m * 64 + 32], tile[m * 64 + 32 : m * 64 + 64]
                    for k in range(2):
                        at = (part * 2 + m) * 2
                        f_real, f_imag = factors[k][at : at + 1], factors[k][at + 1 : at + 2]
                        columns[k].append((real * f_real - imag * f_imag).astype(BF16))
                        columns[k].append((real * f_imag + imag * f_real).astype(BF16))
            rows_in = jnp.concatenate([jnp.concatenate(c, axis=0) for c in columns], axis=1)
            out = dot_nt(onehot, rows_in).astype(BF16)
            for q in range(8):
                block = out[q * 16 : q * 16 + 16]
                if second:
                    SB[(q // 4) * 2 + x_half, q % 4, :, out_lanes] = block
                else:
                    SA[x_half, q % 4, q // 4, :, out_lanes] = block
            return carry

        lax.fori_loop(0, 4, step, 0, unroll=True)

    other = 1 - x_lo
    for pos, x_half in enumerate((other, x_lo)):
        sums(x_half, 0)
        for d in (2, 1, 3):
            n = pos * 3 + d - 1
            send(SA.at[x_half, (y + d) % 4], RA.at[d - 1, x_half], s1s.at[n], s1r.at[n], at_y(d))
        sums(x_half, 1)
        for d in ((1, 3), (2,))[pos]:
            send(SB.at[(x + d) % 4], RB.at[d - 1], s1s.at[5 + d], s1r.at[5 + d], at_x(d))
    shares = jnp.concatenate(
        [jnp.broadcast_to(share[0:1], (8, 128)), jnp.broadcast_to(share[1:2], (8, 128))], axis=1
    )
    W0[...] = dot_nt(shares, onehot.astype(F32), precision=lax.Precision.HIGHEST)
    pl.semaphore_wait(tok.at[2], 2)
    for d in far_first:
        send(W0, RW0.at[d - 1], ws.at[d - 1], wr.at[d - 1], at_z(d))

    def block_scores(n, carry):
        run_peak, run_total = carry
        rows = pl.ds(pl.multiple_of(n * 8, 8), 8)
        f = [F[k, rows, :] for k in range(37)]
        turned = turns_of(f[0:19], [None] + f[19:36])
        scores = [precision * (v - f[36]) for v in turned]
        new_peak = jnp.maximum(run_peak, tree(jnp.maximum, scores))
        total = tree(add, [jnp.exp(v - new_peak) for v in scores])
        return new_peak, run_total * jnp.exp(run_peak - new_peak) + total

    start = (jnp.full((8, 128), -jnp.inf, F32), jnp.zeros((8, 128), F32))
    run_peak, run_total = lax.fori_loop(0, 16, block_scores, start)
    peak = jnp.max(run_peak, axis=0, keepdims=True)
    total = jnp.sum(run_total * jnp.exp(run_peak - peak), axis=0, keepdims=True)
    LS[0:8] = jnp.broadcast_to(peak, (8, 128))
    LS[8:16] = jnp.broadcast_to(total, (8, 128))
    send(LS, LR, sibs.at[3], sibr.at[3], sib)

    for pos, x_half in enumerate((other, x_lo)):
        for d in range(1, 4):
            arrived(RA.at[d - 1, x_half], s1r.at[pos * 3 + d - 1])
    for x_half in range(2):
        for x_top in range(2):
            total = SA[x_half, y, x_top].astype(F32)
            for d in range(3):
                total = total + RA[d, x_half, x_top].astype(F32)
            TA[x_top * 2 + x_half] = total
    for d in range(1, 4):
        send(TA.at[(x + d) % 4], R2A.at[d - 1], s2s.at[d - 1], s2r.at[d - 1], at_x(d))
    for d in range(1, 4):
        arrived(RB.at[d - 1], s1r.at[5 + d])
    for y_to in range(4):
        total = SB[x, y_to].astype(F32)
        for d in range(3):
            total = total + RB[d, y_to].astype(F32)
        TB[y_to] = total
    for d in range(1, 4):
        send(TB.at[(y + d) % 4], R2B.at[d - 1], s2s.at[2 + d], s2r.at[2 + d], at_y(d))

    arrived(LR, sibr.at[3])
    peak = jnp.maximum(LS[0:8], LR[0:8])
    total = LS[8:16] * jnp.exp(LS[0:8] - peak) + LR[8:16] * jnp.exp(LR[0:8] - peak)
    evidence = peak + jnp.log(total)
    evid_out[...] = jnp.where(core == 0, evidence[0:1, 0:64], evidence[0:1, 64:128])

    for d in range(1, 16):
        arrived(RW0.at[d - 1], wr.at[d - 1])
    W1[...] = tree(add, [W0[...]] + [RW0[d] for d in range(15)])
    for d in range(1, 4):
        send(W1, RW1.at[d - 1], ws.at[14 + d], wr.at[14 + d], at_y(d))

    for d in range(1, 4):
        arrived(R2A.at[d - 1], s2r.at[d - 1])
    total = TA[x] + R2A[0] + R2A[1] + R2A[2]
    for n in range(8):
        UZ[n] = total[:, n * 128 : n * 128 + 128]
    for d in range(1, 4):
        arrived(R2B.at[d - 1], s2r.at[2 + d])
    total = TB[y] + R2B[0] + R2B[1] + R2B[2]
    for n in range(8):
        UZ[8 + n] = total[:, n * 128 : n * 128 + 128]
    SZ[...] = UZ[...].astype(BF16)
    for d in far_first:
        send(SZ.at[(z + d) % 16], RZ.at[d - 1], zs.at[d - 1], zr.at[d - 1], at_z(d))

    for d in range(1, 4):
        arrived(RW1.at[d - 1], wr.at[14 + d])
    W2[...] = tree(add, [W1[...]] + [RW1[d] for d in range(3)])
    for d in range(1, 4):
        send(W2, RW2.at[d - 1], ws.at[17 + d], wr.at[17 + d], at_x(d))

    for d in range(1, 4):
        arrived(RW2.at[d - 1], wr.at[17 + d])
    weight = tree(add, [W2[...]] + [RW2[d] for d in range(3)])
    pick = lane[0:16] == row[0:16] + q_me * 16
    weight = jnp.sum(jnp.where(pick, jnp.broadcast_to(weight[0:1], (16, 128)), 0.0), axis=1, keepdims=True)
    for copy in sent:
        copy.wait_send()
    for d in range(1, 16):
        arrived(RZ.at[d - 1], zr.at[d - 1])
    total = tree(add, [UZ[z]] + [RZ[d].astype(F32) for d in range(15)])
    avg_out[...] = total / (1.0 + weight)


def body(images, references, precision, candidates):
    table = jnp.asarray(factor_table())
    anywhere = pl.BlockSpec(memory_space=pltpu.HBM)
    vmem = pl.BlockSpec(memory_space=pltpu.VMEM)
    dma = pltpu.SemaphoreType.DMA
    scratch = [
        pltpu.VMEM((128, 4096), BF16),
        pltpu.VMEM((128, 4096), BF16),
        pltpu.VMEM((18, 256, 256), BF16),
        pltpu.VMEM((37, 128, 128), F32),
        pltpu.VMEM((1, 64), F32),
        pltpu.VMEM((2, 64), jnp.int32),
        pltpu.VMEM((8, 128), F32),
        pltpu.VMEM((8, 128), F32),
        pltpu.VMEM((37, 8, 128), F32),
        pltpu.VMEM((37, 8, 128), F32),
        pltpu.VMEM((2, 128, 128), F32),
        pltpu.VMEM((2, 128, 128), F32),
        pltpu.VMEM((128, 128), BF16),
        pltpu.VMEM((128, 256), BF16),
        pltpu.VMEM((2, 4, 2, 16, 1024), BF16),
        pltpu.VMEM((3, 2, 2, 16, 1024), BF16),
        pltpu.VMEM((4, 4, 16, 1024), BF16),
        pltpu.VMEM((3, 4, 16, 1024), BF16),
        pltpu.VMEM((4, 16, 1024), F32),
        pltpu.VMEM((3, 16, 1024), F32),
        pltpu.VMEM((4, 16, 1024), F32),
        pltpu.VMEM((3, 16, 1024), F32),
        pltpu.VMEM((16, 16, 128), F32),
        pltpu.VMEM((16, 16, 128), BF16),
        pltpu.VMEM((15, 16, 128), BF16),
        pltpu.VMEM((8, 128), F32),
        pltpu.VMEM((15, 8, 128), F32),
        pltpu.VMEM((8, 128), F32),
        pltpu.VMEM((3, 8, 128), F32),
        pltpu.VMEM((8, 128), F32),
        pltpu.VMEM((3, 8, 128), F32),
        pltpu.VMEM((16, 128), F32),
        pltpu.VMEM((16, 128), F32),
        dma((5,)),
        pltpu.SemaphoreType.REGULAR((3,)),
        dma((22,)),
        dma((8, 4)),
        dma((4,)),
        dma((4,)),
        dma((9,)),
        dma((9,)),
        dma((6,)),
        dma((6,)),
        dma((15,)),
        dma((15,)),
        dma((21,)),
        dma((21,)),
    ]
    average, evidence = pl.pallas_call(
        kernel,
        out_shape=(jax.ShapeDtypeStruct((16, 128), F32), jax.ShapeDtypeStruct((1, 64), F32)),
        in_specs=[anywhere] * 5,
        out_specs=(vmem, vmem),
        scratch_shapes=scratch,
        compiler_params=pltpu.CompilerParams(
            collective_id=0, has_side_effects=True, vmem_limit_bytes=55200 * 1024
        ),
    )(images, references, precision.reshape(1, 64), candidates.T, table)
    return average, evidence.reshape(64)


def solution(mesh):
    in_specs = (P(("img", "blk"), None), P("blk", None), P(("img", "blk")), P(("img", "blk"), None))
    out_specs = (P("blk", "img"), P(("img", "blk")))
    return jax.shard_map(body, mesh=mesh, in_specs=in_specs, out_specs=out_specs, check_vma=False)
```

```python
import math

import jax
import jax.numpy as jnp
import ml_dtypes
import numpy as np
from jax import lax
from jax.experimental import pallas as pl
from jax.experimental.pallas import tpu as pltpu
from jax.sharding import PartitionSpec as P

CYCLES = 32
ORDERS = 64
TURNS = 36
FEATS = 4096
LANES = 128
MESH = pl.DeviceIdType.MESH
F32 = jnp.float32
BF16 = jnp.bfloat16


def factor_table():
    turns = np.arange(TURNS)
    angle = 2.0 * math.pi / TURNS * ((np.arange(ORDERS)[:, None] * turns[None, :]) % TURNS)
    values = np.stack([np.cos(angle), -np.sin(angle)], axis=1).reshape(2 * ORDERS, TURNS).astype(np.float32)
    high = values.astype(ml_dtypes.bfloat16).astype(np.float32)
    out = np.zeros((128, 128), np.float32)
    out[:, 0:36] = high
    out[:, 40:76] = high
    out[:, 80:116] = values - high
    return out.astype(ml_dtypes.bfloat16)


def weighted(pairs):
    total = None
    for coef, value in pairs:
        if abs(coef) < 1e-12:
            continue
        if abs(coef - 1.0) < 1e-12:
            term = value
        elif abs(coef + 1.0) < 1e-12:
            term = -value
        else:
            term = value * np.float32(coef)
        total = term if total is None else total + term
    return total


def turns_of(a, b):
    def cos(k, s):
        return math.cos(2.0 * math.pi * (k * s % 36) / 36.0)

    def sin(k, s):
        return math.sin(2.0 * math.pi * (k * s % 36) / 36.0)

    even_c, odd_c, even_s, odd_s = {}, {}, {}, {}
    for s in range(5):
        p = weighted([(cos(k, s), a[k]) for k in range(0, 19, 4)])
        q = weighted([(cos(k, s), a[k]) for k in range(2, 19, 4)])
        even_c[s], even_c[9 - s] = p + q, p - q
    for s in range(9):
        odd_c[s] = weighted([(cos(k, s), a[k]) for k in range(1, 18, 2)])
    for s in range(1, 5):
        p = weighted([(sin(k, s), b[k]) for k in range(4, 17, 4)])
        q = weighted([(sin(k, s), b[k]) for k in range(2, 17, 4)])
        even_s[s], even_s[9 - s] = p + q, q - p
    for s in range(1, 10):
        odd_s[s] = weighted([(sin(k, s), b[k]) for k in range(1, 18, 2)])
    x = [None] * 36
    for s in range(10):
        if s < 9:
            c_lo, c_hi = even_c[s] + odd_c[s], even_c[s] - odd_c[s]
        else:
            c_lo = c_hi = even_c[9]
        if s == 0:
            x[0], x[18] = c_lo, c_hi
        elif s == 9:
            x[9], x[27] = c_lo - odd_s[9], c_lo + odd_s[9]
        else:
            s_lo, s_hi = even_s[s] + odd_s[s], odd_s[s] - even_s[s]
            x[s], x[36 - s] = c_lo - s_lo, c_lo + s_lo
            x[18 - s], x[18 + s] = c_hi - s_hi, c_hi + s_hi
    return x


def tree(op, values):
    values = list(values)
    while len(values) > 1:
        nxt = [op(values[i], values[i + 1]) for i in range(0, len(values) - 1, 2)]
        if len(values) % 2:
            nxt.append(values[-1])
        values = nxt
    return values[0]


def add(p, q):
    return p + q


def dot_nt(a, b, **kw):
    return lax.dot_general(a, b, (((1,), (1,)), ((), ())), preferred_element_type=F32, **kw)


def dot_nn(a, b):
    return jnp.dot(a, b, preferred_element_type=F32)


def kernel(
    images, refs, prec, cand, table, avg_out, evid_out,
    G, IM, FI, F, PIN, CIN, AUX, AUXS, CHX, PS, PR, PT, H, TE, OH, SA, RA, SB, RB, TA, R2A, TB, R2B,
    UZ, SZ, RZ, W0, RW0, W1, RW1, W2, RW2, LS, LR,
    loc, tok, ags, agr, sibs, sibr, s1s, s1r, s2s, s2r, zs, zr, ws, wr,
):
    img, blk = lax.axis_index("img"), lax.axis_index("blk")
    z, x_lo = img % 16, img // 16
    core, y, x_hi = blk % 2, (blk // 2) % 4, blk // 8
    x = x_hi * 2 + x_lo
    q_me = x_hi * 4 + y

    def dev(x_, y_, z_, c_):
        return ((x_ % 2) * 16 + z_, (x_ // 2) * 8 + y_ * 2 + c_)

    sib = dev(x, y, z, 1 - core)
    x_opp, x_same = 3 - x, x_hi * 2 + 1 - x_lo
    zb = z % 2

    def at_z_of(d):
        return dev(x, y, (z + d) % 16, core)

    same, z_up, z_dn = dev(x_same, y, z, core), at_z_of(1), at_z_of(15)

    def at_y(d):
        return dev(x, (y + d) % 4, z, core)

    def at_x(d):
        return dev((x + d) % 4, y, z, core)

    def at_z(d):
        return dev(x, y, (z + d) % 16, core)

    sent = []
    far_first = sorted(range(1, 16), key=lambda d: -min(d, 16 - d))

    def send(src, dst, ssem, rsem, to):
        copy = pltpu.make_async_remote_copy(
            src_ref=src, dst_ref=dst, send_sem=ssem, recv_sem=rsem, device_id=to, device_id_type=MESH
        )
        copy.start()
        sent.append(copy)

    def arrived(dst, rsem):
        pltpu.make_async_copy(dst, dst, rsem).wait()

    mine_rows = pl.ds(pl.multiple_of(core * 64, 64), 64)
    own_p = pltpu.make_async_copy(prec, PIN, loc.at[3])
    own_p.start()
    own_c = pltpu.make_async_copy(cand, CIN, loc.at[4])
    own_c.start()
    own_g = pltpu.make_async_copy(refs, G.at[pl.ds(pl.multiple_of(q_me * 16, 16), 16)], loc.at[1])
    own_g.start()
    own_im = pltpu.make_async_copy(images, IM.at[mine_rows], loc.at[0])
    own_im.start()
    own_t = pltpu.make_async_copy(table, TE, loc.at[2])
    own_t.start()

    barrier = pltpu.get_barrier_semaphore()
    partners = [dev(x_opp, (y + d) % 4, z, core) for d in range(1, 4)]
    partners += [at_y(d) for d in range(1, 4)] + [at_x(d) for d in range(1, 4)]
    partners += [z_up, z_dn, sib]
    for to in partners:
        pl.semaphore_signal(barrier, inc=1, device_id=to, device_id_type=MESH)
    own_p.wait()
    own_c.wait()
    mine = jnp.concatenate([PIN[...], CIN[...].astype(F32)], axis=0)
    AUX[0:3, :] = jnp.concatenate([mine, mine], axis=1)
    AUX[3:8, :] = jnp.zeros((5, 128), F32)
    pl.semaphore_wait(barrier, len(partners))

    def token(n):
        for d in (1 << n, 16 - (1 << n)):
            pl.semaphore_signal(tok.at[n], inc=1, device_id=at_z(d), device_id_type=MESH)

    def rows_at(q):
        return pl.ds(pl.multiple_of(q * 16, 16), 16)

    def half(q, n):
        return G.at[rows_at(q), pl.ds(pl.multiple_of(n * 2048, 2048), 2048)]

    def quarter(q, n):
        return G.at[rows_at(q), pl.ds(pl.multiple_of(n * 1024, 1024), 1024)]

    mine_f = (z + 2 * x_lo) % 4
    same_f, up_f, dn_f = (mine_f + 2) % 4, (mine_f + 1) % 4, (mine_f + 3) % 4
    col, far = x_hi * 4, (1 - x_hi) * 4
    order = (0, 1, 3, 2)

    def near_q(d):
        return col + (y + d) % 4

    def far_q(d):
        return far + (y + d) % 4

    send(AUX, AUXS, sibs.at[1], sibr.at[1], sib)
    send(images, IM.at[mine_rows], sibs.at[0], sibr.at[0], sib)
    opp_quarter = refs.at[:, pl.ds(pl.multiple_of(same_f * 1024, 1024), 1024)]
    own_half = refs.at[:, pl.ds(pl.multiple_of(zb * 2048, 2048), 2048)]
    for n, d in enumerate(order):
        to = dev(x_opp, (y + d) % 4, z, core)
        send(opp_quarter, quarter(q_me, same_f), ags.at[n], agr.at[q_me, same_f], to)
    for n, d in enumerate((1, 3, 2)):
        send(own_half, half(q_me, zb), ags.at[4 + n], agr.at[q_me, 2 * zb], at_y(d))
    token(0)
    own_im.wait()
    arrived(IM.at[pl.ds(pl.multiple_of((1 - core) * 64, 64), 64)], sibr.at[0])
    arrived(AUXS, sibr.at[1])

    row = lax.broadcasted_iota(jnp.int32, (128, 128), 0)
    lane = lax.broadcasted_iota(jnp.int32, (128, 128), 1)

    def swap(src, dst):
        first = dst % 64 < 32
        return jnp.where(first & (src == dst + 32), 1.0, jnp.where((~first) & (src == dst - 32), -1.0, 0.0))

    eye = jnp.where(row == lane, 1.0, 0.0)
    rows_of = jnp.concatenate([eye, swap(lane, row)], axis=0).astype(BF16)

    def prepare(first, count, half):
        def step(n, carry):
            t = first + n
            block = IM[:, pl.ds(pl.multiple_of(t * 128, 128), 128)]
            both = dot_nt(rows_of, block)
            j = t - 18 * half
            sign = jnp.where(j < 9, 1.0, -1.0).astype(F32)
            FI[j, half * 128 : half * 128 + 128, 0:128] = both[0:128].astype(BF16)
            FI[j, half * 128 : half * 128 + 128, 128:256] = (both[128:256] * sign).astype(BF16)
            return carry

        lax.fori_loop(0, count, step, 0, unroll=2)

    def hand_far(n):
        q = far_q(order[n])
        part, sem = quarter(q, mine_f), agr.at[q, mine_f]
        arrived(part, sem)
        for m, to in enumerate((same, z_up, z_dn)):
            send(part, part, ags.at[13 + 3 * n + m], sem, to)

    def hand_near(n):
        q = near_q((1, 3, 2)[n])
        arrived(half(q, zb), agr.at[q, 2 * zb])
        for m, to in enumerate((z_up, z_dn)):
            part = quarter(q, 2 * zb + m)
            send(part, part, ags.at[7 + 2 * n + m], agr.at[q, 2 * zb + m], to)

    prepare(0, 4, 0)
    hand_far(0)
    prepare(4, 2, 0)
    hand_far(1)
    hand_far(2)
    hand_near(0)
    hand_near(1)
    prepare(6, 2, 0)
    hand_far(3)
    hand_near(2)
    pl.semaphore_wait(tok.at[0], 2)
    token(1)
    prepare(8, 10, 0)
    prepare(18, 14, 1)

    right = lax.broadcasted_iota(jnp.int32, (8, 128), 1) >= 64
    auxc = jnp.where(right == (core == 1), AUX[...], AUXS[...])
    precision = auxc[0:1, :]
    class_id = ((row // 16) * 32 + core * 16 + row % 16).astype(F32)
    picks = [auxc[1:2, :] == class_id, auxc[2:3, :] == class_id]
    for k in range(2):
        OH[:, k * 128 : k * 128 + 128] = jnp.where(picks[k], 1.0, 0.0).astype(BF16)
    PT[...] = jnp.zeros_like(PT)

    own_g.wait()
    for d in (1, 3, 2):
        q = near_q(d)
        for m in range(2):
            arrived(quarter(q, 2 * (1 - zb) + m), agr.at[q, 2 * (1 - zb) + m])

    low = (lax.broadcasted_iota(jnp.int32, (64, 256), 1) % 128) < 64

    def harmonics(first):
        rows = pl.ds(pl.multiple_of(first * 16, 64), 64)
        for j in range(18):
            left = G[rows, j * 128 : j * 128 + 128]
            if j < 14:
                tile = jnp.concatenate([left, G[rows, (18 + j) * 128 : (18 + j) * 128 + 128]], axis=1)
                keep, right_side = low, FI[j]
            else:
                tile, keep, right_side = left, low[:, 0:128], FI[j, 0:128, :]
            zero = jnp.zeros_like(tile)
            stacked = jnp.concatenate([jnp.where(keep, tile, zero), jnp.where(keep, zero, tile)], axis=0)
            out = dot_nn(stacked, right_side)
            even, odd = out[0:64], out[64:128]
            k_even, k_odd = (2 * j if j <= 9 else 36 - 2 * j), (2 * j + 1 if j <= 8 else 35 - 2 * j)
            if j <= 9:
                F[k_even, rows, :] = even[:, 0:128]
            else:
                F[k_even, rows, :] += even[:, 0:128]
            if 0 < k_even < 18:
                if j <= 9:
                    F[18 + k_even, rows, :] = even[:, 128:256]
                else:
                    F[18 + k_even, rows, :] += even[:, 128:256]
            if j <= 8:
                F[k_odd, rows, :] = odd[:, 0:128]
                F[18 + k_odd, rows, :] = odd[:, 128:256]
            else:
                F[k_odd, rows, :] += odd[:, 0:128]
                F[18 + k_odd, rows, :] += odd[:, 128:256]
        square = jnp.zeros((64, 128), F32)
        for t in range(32):
            value = G[rows, t * 128 : t * 128 + 128].astype(F32)
            square = square + value * value
        F[36, rows, :] = jnp.broadcast_to(0.5 * jnp.sum(square, axis=1, keepdims=True), (64, 128))

    even_row = lax.broadcasted_iota(jnp.int32, (8, 128), 0) % 2 == 0

    def choose(first, more):
        rows = pl.ds(pl.multiple_of(first * 16, 64), 64)
        ids = (((row[0:64] // 16) + first) * 32 + core * 16 + row[0:64] % 16).astype(F32)
        keep = [auxc[k : k + 1, :] == ids for k in (1, 2)]

        def step(kk, carry):
            f = F[kk, rows, :]
            parts = []
            for k in range(2):
                kept = jnp.where(keep[k], f, 0.0)
                total = tree(add, [kept[n * 8 : n * 8 + 8] for n in range(8)])
                parts.append(total + pltpu.roll(total, 1, 0))
            both = jnp.where(even_row, parts[0], parts[1])
            both = both + pltpu.roll(both, 2, 0)
            both = both + pltpu.roll(both, 4, 0)
            CHX[kk] = CHX[kk] + both if more else both
            return carry

        lax.fori_loop(0, 36, step, 0, unroll=4)
        step(36, 0)

    harmonics(col)
    choose(col, False)
    pl.semaphore_wait(tok.at[1], 2)
    token(2)
    for d in order:
        for f in (same_f, up_f, dn_f):
            arrived(quarter(far_q(d), f), agr.at[far_q(d), f])
    harmonics(far)
    choose(far, True)
    names = jnp.where(even_row, auxc[1:2, :], auxc[2:3, :]).astype(jnp.int32)
    held = (names // 16) % 2 == core

    def both_picks(op, v):
        return op(v, jnp.where(even_row, pltpu.roll(v, 7, 0), pltpu.roll(v, 1, 0)))

    coefs = [CHX[k] for k in range(37)]
    turned = turns_of(coefs[0:19], [None] + coefs[19:36])
    scores = [precision * (v - coefs[36]) for v in turned]
    own_peak = both_picks(jnp.maximum, jnp.where(held, tree(jnp.maximum, scores), -1e30))
    weights = [jnp.where(held, jnp.exp(v - own_peak), 0.0) for v in scores]
    share = tree(add, weights)
    own_total = both_picks(add, share)
    PS[0:8] = own_peak
    PS[8:16] = own_total
    send(PS, PR, sibs.at[2], sibr.at[2], sib)
    for s in range(TURNS):
        high = weights[s].astype(BF16).astype(F32)
        rest = weights[s] - high
        for k in range(2):
            PT[k, s : s + 1, :] = high[k : k + 1]
            PT[k, 40 + s : 41 + s, :] = rest[k : k + 1]
            PT[k, 80 + s : 81 + s, :] = high[k : k + 1]
    own_t.wait()
    spectra = [dot_nn(TE[...], PT[k].astype(BF16)) for k in range(2)]
    arrived(PR, sibr.at[2])
    peak = jnp.maximum(own_peak, PR[0:8])
    own_part = jnp.exp(own_peak - peak)
    scale = own_part / (own_part * own_total + jnp.exp(PR[0:8] - peak) * PR[8:16])
    share = share * scale
    for k in range(2):
        H[k] = spectra[k] * scale[0:1]

    onehot = OH[...]

    def sums(x_half, second):
        def step(v, carry):
            u = x_half * 8 + second * 4 + v
            out_lanes = pl.ds(pl.multiple_of(v * 256, 256), 256)
            upper = u // 9
            factors = [H[k, pl.ds(pl.multiple_of(u * 8, 8), 8), :] for k in range(2)]
            columns = [[], []]
            for part in range(2):
                rows = pl.ds(pl.multiple_of(upper * 128, 128), 128)
                tile = FI[2 * u + part - 18 * upper, rows, 0:128].astype(F32)
                for m in range(2):
                    real, imag = tile[m * 64 : m * 64 + 32], tile[m * 64 + 32 : m * 64 + 64]
                    for k in range(2):
                        at = (part * 2 + m) * 2
                        f_real, f_imag = factors[k][at : at + 1], factors[k][at + 1 : at + 2]
                        columns[k].append((real * f_real - imag * f_imag).astype(BF16))
                        columns[k].append((real * f_imag + imag * f_real).astype(BF16))
            rows_in = jnp.concatenate([jnp.concatenate(c, axis=0) for c in columns], axis=1)
            out = dot_nt(onehot, rows_in).astype(BF16)
            for q in range(8):
                block = out[q * 16 : q * 16 + 16]
                if second:
                    SB[(q // 4) * 2 + x_half, q % 4, :, out_lanes] = block
                else:
                    SA[x_half, q % 4, q // 4, :, out_lanes] = block
            return carry

        lax.fori_loop(0, 4, step, 0, unroll=True)

    other = 1 - x_lo
    for pos, x_half in enumerate((other, x_lo)):
        sums(x_half, 0)
        for d in (2, 1, 3):
            n = pos * 3 + d - 1
            send(SA.at[x_half, (y + d) % 4], RA.at[d - 1, x_half], s1s.at[n], s1r.at[n], at_y(d))
        sums(x_half, 1)
        for d in ((1, 3), (2,))[pos]:
            send(SB.at[(x + d) % 4], RB.at[d - 1], s1s.at[5 + d], s1r.at[5 + d], at_x(d))
    shares = jnp.concatenate(
        [jnp.broadcast_to(share[0:1], (8, 128)), jnp.broadcast_to(share[1:2], (8, 128))], axis=1
    )
    W0[...] = dot_nt(shares, onehot.astype(F32), precision=lax.Precision.HIGHEST)
    pl.semaphore_wait(tok.at[2], 2)
    for d in far_first:
        send(W0, RW0.at[d - 1], ws.at[d - 1], wr.at[d - 1], at_z(d))

    def block_scores(n, carry):
        run_peak, run_total = carry
        rows = pl.ds(pl.multiple_of(n * 8, 8), 8)
        f = [F[k, rows, :] for k in range(37)]
        turned = turns_of(f[0:19], [None] + f[19:36])
        scores = [precision * (v - f[36]) for v in turned]
        new_peak = jnp.maximum(run_peak, tree(jnp.maximum, scores))
        total = tree(add, [jnp.exp(v - new_peak) for v in scores])
        return new_peak, run_total * jnp.exp(run_peak - new_peak) + total

    start = (jnp.full((8, 128), -jnp.inf, F32), jnp.zeros((8, 128), F32))
    run_peak, run_total = lax.fori_loop(0, 16, block_scores, start)
    peak = jnp.max(run_peak, axis=0, keepdims=True)
    total = jnp.sum(run_total * jnp.exp(run_peak - peak), axis=0, keepdims=True)
    LS[0:8] = jnp.broadcast_to(peak, (8, 128))
    LS[8:16] = jnp.broadcast_to(total, (8, 128))
    send(LS, LR, sibs.at[3], sibr.at[3], sib)

    for pos, x_half in enumerate((other, x_lo)):
        for d in range(1, 4):
            arrived(RA.at[d - 1, x_half], s1r.at[pos * 3 + d - 1])
    for x_half in range(2):
        for x_top in range(2):
            total = SA[x_half, y, x_top].astype(F32)
            for d in range(3):
                total = total + RA[d, x_half, x_top].astype(F32)
            TA[x_top * 2 + x_half] = total
    for d in range(1, 4):
        send(TA.at[(x + d) % 4], R2A.at[d - 1], s2s.at[d - 1], s2r.at[d - 1], at_x(d))
    for d in range(1, 4):
        arrived(RB.at[d - 1], s1r.at[5 + d])
    for y_to in range(4):
        total = SB[x, y_to].astype(F32)
        for d in range(3):
            total = total + RB[d, y_to].astype(F32)
        TB[y_to] = total
    for d in range(1, 4):
        send(TB.at[(y + d) % 4], R2B.at[d - 1], s2s.at[2 + d], s2r.at[2 + d], at_y(d))

    arrived(LR, sibr.at[3])
    peak = jnp.maximum(LS[0:8], LR[0:8])
    total = LS[8:16] * jnp.exp(LS[0:8] - peak) + LR[8:16] * jnp.exp(LR[0:8] - peak)
    evidence = peak + jnp.log(total)
    evid_out[...] = jnp.where(core == 0, evidence[0:1, 0:64], evidence[0:1, 64:128])

    for d in range(1, 16):
        arrived(RW0.at[d - 1], wr.at[d - 1])
    W1[...] = tree(add, [W0[...]] + [RW0[d] for d in range(15)])
    for d in range(1, 4):
        send(W1, RW1.at[d - 1], ws.at[14 + d], wr.at[14 + d], at_y(d))

    for d in range(1, 4):
        arrived(R2A.at[d - 1], s2r.at[d - 1])
    total = TA[x] + R2A[0] + R2A[1] + R2A[2]
    for n in range(8):
        UZ[n] = total[:, n * 128 : n * 128 + 128]
    for d in range(1, 4):
        arrived(R2B.at[d - 1], s2r.at[2 + d])
    total = TB[y] + R2B[0] + R2B[1] + R2B[2]
    for n in range(8):
        UZ[8 + n] = total[:, n * 128 : n * 128 + 128]
    SZ[...] = UZ[...].astype(BF16)
    for d in far_first:
        send(SZ.at[(z + d) % 16], RZ.at[d - 1], zs.at[d - 1], zr.at[d - 1], at_z(d))

    for d in range(1, 4):
        arrived(RW1.at[d - 1], wr.at[14 + d])
    W2[...] = tree(add, [W1[...]] + [RW1[d] for d in range(3)])
    for d in range(1, 4):
        send(W2, RW2.at[d - 1], ws.at[17 + d], wr.at[17 + d], at_x(d))

    for d in range(1, 4):
        arrived(RW2.at[d - 1], wr.at[17 + d])
    weight = tree(add, [W2[...]] + [RW2[d] for d in range(3)])
    pick = lane[0:16] == row[0:16] + q_me * 16
    weight = jnp.sum(jnp.where(pick, jnp.broadcast_to(weight[0:1], (16, 128)), 0.0), axis=1, keepdims=True)
    for copy in sent:
        copy.wait_send()
    for d in range(1, 16):
        arrived(RZ.at[d - 1], zr.at[d - 1])
    total = tree(add, [UZ[z]] + [RZ[d].astype(F32) for d in range(15)])
    avg_out[...] = total / (1.0 + weight)


def body(images, references, precision, candidates):
    table = jnp.asarray(factor_table())
    anywhere = pl.BlockSpec(memory_space=pltpu.HBM)
    vmem = pl.BlockSpec(memory_space=pltpu.VMEM)
    dma = pltpu.SemaphoreType.DMA
    scratch = [
        pltpu.VMEM((128, 4096), BF16),
        pltpu.VMEM((128, 4096), BF16),
        pltpu.VMEM((18, 256, 256), BF16),
        pltpu.VMEM((37, 128, 128), F32),
        pltpu.VMEM((1, 64), F32),
        pltpu.VMEM((2, 64), jnp.int32),
        pltpu.VMEM((8, 128), F32),
        pltpu.VMEM((8, 128), F32),
        pltpu.VMEM((37, 8, 128), F32),
        pltpu.VMEM((16, 128), F32),
        pltpu.VMEM((16, 128), F32),
        pltpu.VMEM((2, 128, 128), F32),
        pltpu.VMEM((2, 128, 128), F32),
        pltpu.VMEM((128, 128), BF16),
        pltpu.VMEM((128, 256), BF16),
        pltpu.VMEM((2, 4, 2, 16, 1024), BF16),
        pltpu.VMEM((3, 2, 2, 16, 1024), BF16),
        pltpu.VMEM((4, 4, 16, 1024), BF16),
        pltpu.VMEM((3, 4, 16, 1024), BF16),
        pltpu.VMEM((4, 16, 1024), F32),
        pltpu.VMEM((3, 16, 1024), F32),
        pltpu.VMEM((4, 16, 1024), F32),
        pltpu.VMEM((3, 16, 1024), F32),
        pltpu.VMEM((16, 16, 128), F32),
        pltpu.VMEM((16, 16, 128), BF16),
        pltpu.VMEM((15, 16, 128), BF16),
        pltpu.VMEM((8, 128), F32),
        pltpu.VMEM((15, 8, 128), F32),
        pltpu.VMEM((8, 128), F32),
        pltpu.VMEM((3, 8, 128), F32),
        pltpu.VMEM((8, 128), F32),
        pltpu.VMEM((3, 8, 128), F32),
        pltpu.VMEM((16, 128), F32),
        pltpu.VMEM((16, 128), F32),
        dma((5,)),
        pltpu.SemaphoreType.REGULAR((3,)),
        dma((25,)),
        dma((8, 4)),
        dma((4,)),
        dma((4,)),
        dma((9,)),
        dma((9,)),
        dma((6,)),
        dma((6,)),
        dma((15,)),
        dma((15,)),
        dma((21,)),
        dma((21,)),
    ]
    average, evidence = pl.pallas_call(
        kernel,
        out_shape=(jax.ShapeDtypeStruct((16, 128), F32), jax.ShapeDtypeStruct((1, 64), F32)),
        in_specs=[anywhere] * 5,
        out_specs=(vmem, vmem),
        scratch_shapes=scratch,
        compiler_params=pltpu.CompilerParams(
            collective_id=0, has_side_effects=True, vmem_limit_bytes=55200 * 1024
        ),
    )(images, references, precision.reshape(1, 64), candidates.T, table)
    return average, evidence.reshape(64)


def solution(mesh):
    in_specs = (P(("img", "blk"), None), P("blk", None), P(("img", "blk")), P(("img", "blk"), None))
    out_specs = (P("blk", "img"), P(("img", "blk")))
    return jax.shard_map(body, mesh=mesh, in_specs=in_specs, out_specs=out_specs, check_vma=False)
```

```python
import math

import jax
import jax.numpy as jnp
import ml_dtypes
import numpy as np
from jax import lax
from jax.experimental import pallas as pl
from jax.experimental.pallas import tpu as pltpu
from jax.sharding import PartitionSpec as P

CYCLES = 32
ORDERS = 64
TURNS = 36
FEATS = 4096
LANES = 128
MESH = pl.DeviceIdType.MESH
F32 = jnp.float32
BF16 = jnp.bfloat16


def factor_table():
    turns = np.arange(TURNS)
    angle = 2.0 * math.pi / TURNS * ((np.arange(ORDERS)[:, None] * turns[None, :]) % TURNS)
    values = np.stack([np.cos(angle), -np.sin(angle)], axis=1).reshape(2 * ORDERS, TURNS).astype(np.float32)
    high = values.astype(ml_dtypes.bfloat16).astype(np.float32)
    out = np.zeros((128, 128), np.float32)
    out[:, 0:36] = high
    out[:, 40:76] = high
    out[:, 80:116] = values - high
    return out.astype(ml_dtypes.bfloat16)


def weighted(pairs):
    total = None
    for coef, value in pairs:
        if abs(coef) < 1e-12:
            continue
        if abs(coef - 1.0) < 1e-12:
            term = value
        elif abs(coef + 1.0) < 1e-12:
            term = -value
        else:
            term = value * np.float32(coef)
        total = term if total is None else total + term
    return total


def turns_of(a, b):
    def cos(k, s):
        return math.cos(2.0 * math.pi * (k * s % 36) / 36.0)

    def sin(k, s):
        return math.sin(2.0 * math.pi * (k * s % 36) / 36.0)

    even_c, odd_c, even_s, odd_s = {}, {}, {}, {}
    for s in range(5):
        p = weighted([(cos(k, s), a[k]) for k in range(0, 19, 4)])
        q = weighted([(cos(k, s), a[k]) for k in range(2, 19, 4)])
        even_c[s], even_c[9 - s] = p + q, p - q
    for s in range(9):
        odd_c[s] = weighted([(cos(k, s), a[k]) for k in range(1, 18, 2)])
    for s in range(1, 5):
        p = weighted([(sin(k, s), b[k]) for k in range(4, 17, 4)])
        q = weighted([(sin(k, s), b[k]) for k in range(2, 17, 4)])
        even_s[s], even_s[9 - s] = p + q, q - p
    for s in range(1, 10):
        odd_s[s] = weighted([(sin(k, s), b[k]) for k in range(1, 18, 2)])
    x = [None] * 36
    for s in range(10):
        if s < 9:
            c_lo, c_hi = even_c[s] + odd_c[s], even_c[s] - odd_c[s]
        else:
            c_lo = c_hi = even_c[9]
        if s == 0:
            x[0], x[18] = c_lo, c_hi
        elif s == 9:
            x[9], x[27] = c_lo - odd_s[9], c_lo + odd_s[9]
        else:
            s_lo, s_hi = even_s[s] + odd_s[s], odd_s[s] - even_s[s]
            x[s], x[36 - s] = c_lo - s_lo, c_lo + s_lo
            x[18 - s], x[18 + s] = c_hi - s_hi, c_hi + s_hi
    return x


def tree(op, values):
    values = list(values)
    while len(values) > 1:
        nxt = [op(values[i], values[i + 1]) for i in range(0, len(values) - 1, 2)]
        if len(values) % 2:
            nxt.append(values[-1])
        values = nxt
    return values[0]


def add(p, q):
    return p + q


def dot_nt(a, b, **kw):
    return lax.dot_general(a, b, (((1,), (1,)), ((), ())), preferred_element_type=F32, **kw)


def dot_nn(a, b):
    return jnp.dot(a, b, preferred_element_type=F32)


def kernel(
    images, refs, prec, cand, table, avg_out, evid_out,
    G, IM, FI, F, PIN, CIN, AUX, AUXS, CHX, PS, PR, PT, H, TE, OH, SA, RA, SB, RB, TA, TAB, R2A, TB, TBB, R2B,
    UZ, SZ, RZ, W0, RW0, W1, RW1, W2, RW2, LS, LR,
    loc, tok, ags, agr, sibs, sibr, s1s, s1r, s2s, s2r, zs, zr, ws, wr,
):
    img, blk = lax.axis_index("img"), lax.axis_index("blk")
    z, x_lo = img % 16, img // 16
    core, y, x_hi = blk % 2, (blk // 2) % 4, blk // 8
    x = x_hi * 2 + x_lo
    q_me = x_hi * 4 + y

    def dev(x_, y_, z_, c_):
        return ((x_ % 2) * 16 + z_, (x_ // 2) * 8 + y_ * 2 + c_)

    sib = dev(x, y, z, 1 - core)
    x_opp, x_same = 3 - x, x_hi * 2 + 1 - x_lo
    zb = z % 2

    def at_z_of(d):
        return dev(x, y, (z + d) % 16, core)

    same, z_up, z_dn = dev(x_same, y, z, core), at_z_of(1), at_z_of(15)

    def at_y(d):
        return dev(x, (y + d) % 4, z, core)

    def at_x(d):
        return dev((x + d) % 4, y, z, core)

    def at_z(d):
        return dev(x, y, (z + d) % 16, core)

    sent = []
    far_first = sorted(range(1, 16), key=lambda d: -min(d, 16 - d))

    def send(src, dst, ssem, rsem, to):
        copy = pltpu.make_async_remote_copy(
            src_ref=src, dst_ref=dst, send_sem=ssem, recv_sem=rsem, device_id=to, device_id_type=MESH
        )
        copy.start()
        sent.append(copy)

    def arrived(dst, rsem):
        pltpu.make_async_copy(dst, dst, rsem).wait()

    mine_rows = pl.ds(pl.multiple_of(core * 64, 64), 64)
    own_p = pltpu.make_async_copy(prec, PIN, loc.at[3])
    own_p.start()
    own_c = pltpu.make_async_copy(cand, CIN, loc.at[4])
    own_c.start()
    own_g = pltpu.make_async_copy(refs, G.at[pl.ds(pl.multiple_of(q_me * 16, 16), 16)], loc.at[1])
    own_g.start()
    own_im = pltpu.make_async_copy(images, IM.at[mine_rows], loc.at[0])
    own_im.start()
    own_t = pltpu.make_async_copy(table, TE, loc.at[2])
    own_t.start()

    barrier = pltpu.get_barrier_semaphore()
    partners = [dev(x_opp, (y + d) % 4, z, core) for d in range(1, 4)]
    partners += [at_y(d) for d in range(1, 4)] + [at_x(d) for d in range(1, 4)]
    partners += [z_up, z_dn, sib]
    for to in partners:
        pl.semaphore_signal(barrier, inc=1, device_id=to, device_id_type=MESH)
    own_p.wait()
    own_c.wait()
    mine = jnp.concatenate([PIN[...], CIN[...].astype(F32)], axis=0)
    AUX[0:3, :] = jnp.concatenate([mine, mine], axis=1)
    AUX[3:8, :] = jnp.zeros((5, 128), F32)
    pl.semaphore_wait(barrier, len(partners))

    def token(n):
        for d in (1 << n, 16 - (1 << n)):
            pl.semaphore_signal(tok.at[n], inc=1, device_id=at_z(d), device_id_type=MESH)

    def rows_at(q):
        return pl.ds(pl.multiple_of(q * 16, 16), 16)

    def half(q, n):
        return G.at[rows_at(q), pl.ds(pl.multiple_of(n * 2048, 2048), 2048)]

    def quarter(q, n):
        return G.at[rows_at(q), pl.ds(pl.multiple_of(n * 1024, 1024), 1024)]

    mine_f = (z + 2 * x_lo) % 4
    same_f, up_f, dn_f = (mine_f + 2) % 4, (mine_f + 1) % 4, (mine_f + 3) % 4
    col, far = x_hi * 4, (1 - x_hi) * 4
    order = (0, 1, 3, 2)

    def near_q(d):
        return col + (y + d) % 4

    def far_q(d):
        return far + (y + d) % 4

    send(AUX, AUXS, sibs.at[1], sibr.at[1], sib)
    send(images, IM.at[mine_rows], sibs.at[0], sibr.at[0], sib)
    opp_quarter = refs.at[:, pl.ds(pl.multiple_of(same_f * 1024, 1024), 1024)]
    own_half = refs.at[:, pl.ds(pl.multiple_of(zb * 2048, 2048), 2048)]
    for n, d in enumerate(order):
        to = dev(x_opp, (y + d) % 4, z, core)
        send(opp_quarter, quarter(q_me, same_f), ags.at[n], agr.at[q_me, same_f], to)
    for n, d in enumerate((1, 3, 2)):
        send(own_half, half(q_me, zb), ags.at[4 + n], agr.at[q_me, 2 * zb], at_y(d))
    token(0)
    own_im.wait()
    arrived(IM.at[pl.ds(pl.multiple_of((1 - core) * 64, 64), 64)], sibr.at[0])
    arrived(AUXS, sibr.at[1])

    row = lax.broadcasted_iota(jnp.int32, (128, 128), 0)
    lane = lax.broadcasted_iota(jnp.int32, (128, 128), 1)

    def swap(src, dst):
        first = dst % 64 < 32
        return jnp.where(first & (src == dst + 32), 1.0, jnp.where((~first) & (src == dst - 32), -1.0, 0.0))

    eye = jnp.where(row == lane, 1.0, 0.0)
    rows_of = jnp.concatenate([eye, swap(lane, row)], axis=0).astype(BF16)

    def prepare(first, count, half):
        def step(n, carry):
            t = first + n
            block = IM[:, pl.ds(pl.multiple_of(t * 128, 128), 128)]
            both = dot_nt(rows_of, block)
            j = t - 18 * half
            sign = jnp.where(j < 9, 1.0, -1.0).astype(F32)
            FI[j, half * 128 : half * 128 + 128, 0:128] = both[0:128].astype(BF16)
            FI[j, half * 128 : half * 128 + 128, 128:256] = (both[128:256] * sign).astype(BF16)
            return carry

        lax.fori_loop(0, count, step, 0, unroll=2)

    def hand_far(n):
        q = far_q(order[n])
        part, sem = quarter(q, mine_f), agr.at[q, mine_f]
        arrived(part, sem)
        for m, to in enumerate((same, z_up, z_dn)):
            send(part, part, ags.at[13 + 3 * n + m], sem, to)

    def hand_near(n):
        q = near_q((1, 3, 2)[n])
        arrived(half(q, zb), agr.at[q, 2 * zb])
        for m, to in enumerate((z_up, z_dn)):
            part = quarter(q, 2 * zb + m)
            send(part, part, ags.at[7 + 2 * n + m], agr.at[q, 2 * zb + m], to)

    prepare(0, 4, 0)
    hand_far(0)
    prepare(4, 2, 0)
    hand_far(1)
    hand_far(2)
    hand_near(0)
    hand_near(1)
    prepare(6, 2, 0)
    hand_far(3)
    hand_near(2)
    pl.semaphore_wait(tok.at[0], 2)
    token(1)
    prepare(8, 10, 0)
    prepare(18, 14, 1)

    right = lax.broadcasted_iota(jnp.int32, (8, 128), 1) >= 64
    auxc = jnp.where(right == (core == 1), AUX[...], AUXS[...])
    precision = auxc[0:1, :]
    class_id = ((row // 16) * 32 + core * 16 + row % 16).astype(F32)
    picks = [auxc[1:2, :] == class_id, auxc[2:3, :] == class_id]
    for k in range(2):
        OH[:, k * 128 : k * 128 + 128] = jnp.where(picks[k], 1.0, 0.0).astype(BF16)
    PT[...] = jnp.zeros_like(PT)

    own_g.wait()
    for d in (1, 3, 2):
        q = near_q(d)
        for m in range(2):
            arrived(quarter(q, 2 * (1 - zb) + m), agr.at[q, 2 * (1 - zb) + m])

    low = (lax.broadcasted_iota(jnp.int32, (64, 256), 1) % 128) < 64

    def harmonics(first):
        rows = pl.ds(pl.multiple_of(first * 16, 64), 64)
        for j in range(18):
            left = G[rows, j * 128 : j * 128 + 128]
            if j < 14:
                tile = jnp.concatenate([left, G[rows, (18 + j) * 128 : (18 + j) * 128 + 128]], axis=1)
                keep, right_side = low, FI[j]
            else:
                tile, keep, right_side = left, low[:, 0:128], FI[j, 0:128, :]
            zero = jnp.zeros_like(tile)
            stacked = jnp.concatenate([jnp.where(keep, tile, zero), jnp.where(keep, zero, tile)], axis=0)
            out = dot_nn(stacked, right_side)
            even, odd = out[0:64], out[64:128]
            k_even, k_odd = (2 * j if j <= 9 else 36 - 2 * j), (2 * j + 1 if j <= 8 else 35 - 2 * j)
            if j <= 9:
                F[k_even, rows, :] = even[:, 0:128]
            else:
                F[k_even, rows, :] += even[:, 0:128]
            if 0 < k_even < 18:
                if j <= 9:
                    F[18 + k_even, rows, :] = even[:, 128:256]
                else:
                    F[18 + k_even, rows, :] += even[:, 128:256]
            if j <= 8:
                F[k_odd, rows, :] = odd[:, 0:128]
                F[18 + k_odd, rows, :] = odd[:, 128:256]
            else:
                F[k_odd, rows, :] += odd[:, 0:128]
                F[18 + k_odd, rows, :] += odd[:, 128:256]
        square = jnp.zeros((64, 128), F32)
        for t in range(32):
            value = G[rows, t * 128 : t * 128 + 128].astype(F32)
            square = square + value * value
        F[36, rows, :] = jnp.broadcast_to(0.5 * jnp.sum(square, axis=1, keepdims=True), (64, 128))

    even_row = lax.broadcasted_iota(jnp.int32, (8, 128), 0) % 2 == 0

    def choose(first, more):
        rows = pl.ds(pl.multiple_of(first * 16, 64), 64)
        ids = (((row[0:64] // 16) + first) * 32 + core * 16 + row[0:64] % 16).astype(F32)
        keep = [auxc[k : k + 1, :] == ids for k in (1, 2)]

        def step(kk, carry):
            f = F[kk, rows, :]
            parts = []
            for k in range(2):
                kept = jnp.where(keep[k], f, 0.0)
                total = tree(add, [kept[n * 8 : n * 8 + 8] for n in range(8)])
                parts.append(total + pltpu.roll(total, 1, 0))
            both = jnp.where(even_row, parts[0], parts[1])
            both = both + pltpu.roll(both, 2, 0)
            both = both + pltpu.roll(both, 4, 0)
            CHX[kk] = CHX[kk] + both if more else both
            return carry

        lax.fori_loop(0, 36, step, 0, unroll=4)
        step(36, 0)

    harmonics(col)
    choose(col, False)
    pl.semaphore_wait(tok.at[1], 2)
    token(2)
    for d in order:
        for f in (same_f, up_f, dn_f):
            arrived(quarter(far_q(d), f), agr.at[far_q(d), f])
    harmonics(far)
    choose(far, True)
    names = jnp.where(even_row, auxc[1:2, :], auxc[2:3, :]).astype(jnp.int32)
    held = (names // 16) % 2 == core

    def both_picks(op, v):
        return op(v, jnp.where(even_row, pltpu.roll(v, 7, 0), pltpu.roll(v, 1, 0)))

    coefs = [CHX[k] for k in range(37)]
    turned = turns_of(coefs[0:19], [None] + coefs[19:36])
    scores = [precision * (v - coefs[36]) for v in turned]
    own_peak = both_picks(jnp.maximum, jnp.where(held, tree(jnp.maximum, scores), -1e30))
    weights = [jnp.where(held, jnp.exp(v - own_peak), 0.0) for v in scores]
    share = tree(add, weights)
    own_total = both_picks(add, share)
    PS[0:8] = own_peak
    PS[8:16] = own_total
    send(PS, PR, sibs.at[2], sibr.at[2], sib)
    for s in range(TURNS):
        high = weights[s].astype(BF16).astype(F32)
        rest = weights[s] - high
        for k in range(2):
            PT[k, s : s + 1, :] = high[k : k + 1]
            PT[k, 40 + s : 41 + s, :] = rest[k : k + 1]
            PT[k, 80 + s : 81 + s, :] = high[k : k + 1]
    own_t.wait()
    spectra = [dot_nn(TE[...], PT[k].astype(BF16)) for k in range(2)]
    arrived(PR, sibr.at[2])
    peak = jnp.maximum(own_peak, PR[0:8])
    own_part = jnp.exp(own_peak - peak)
    scale = own_part / (own_part * own_total + jnp.exp(PR[0:8] - peak) * PR[8:16])
    share = share * scale
    for k in range(2):
        H[k] = spectra[k] * scale[0:1]

    onehot = OH[...]

    def sums(x_half, second):
        def step(v, carry):
            u = x_half * 8 + second * 4 + v
            out_lanes = pl.ds(pl.multiple_of(v * 256, 256), 256)
            upper = u // 9
            factors = [H[k, pl.ds(pl.multiple_of(u * 8, 8), 8), :] for k in range(2)]
            columns = [[], []]
            for part in range(2):
                rows = pl.ds(pl.multiple_of(upper * 128, 128), 128)
                tile = FI[2 * u + part - 18 * upper, rows, 0:128].astype(F32)
                for m in range(2):
                    real, imag = tile[m * 64 : m * 64 + 32], tile[m * 64 + 32 : m * 64 + 64]
                    for k in range(2):
                        at = (part * 2 + m) * 2
                        f_real, f_imag = factors[k][at : at + 1], factors[k][at + 1 : at + 2]
                        columns[k].append((real * f_real - imag * f_imag).astype(BF16))
                        columns[k].append((real * f_imag + imag * f_real).astype(BF16))
            rows_in = jnp.concatenate([jnp.concatenate(c, axis=0) for c in columns], axis=1)
            out = dot_nt(onehot, rows_in).astype(BF16)
            for q in range(8):
                block = out[q * 16 : q * 16 + 16]
                if second:
                    SB[(q // 4) * 2 + x_half, q % 4, :, out_lanes] = block
                else:
                    SA[x_half, q % 4, q // 4, :, out_lanes] = block
            return carry

        lax.fori_loop(0, 4, step, 0, unroll=True)

    other = 1 - x_lo
    for pos, x_half in enumerate((other, x_lo)):
        sums(x_half, 0)
        for d in (2, 1, 3):
            n = pos * 3 + d - 1
            send(SA.at[x_half, (y + d) % 4], RA.at[d - 1, x_half], s1s.at[n], s1r.at[n], at_y(d))
        sums(x_half, 1)
        for d in ((1, 3), (2,))[pos]:
            send(SB.at[(x + d) % 4], RB.at[d - 1], s1s.at[5 + d], s1r.at[5 + d], at_x(d))
    shares = jnp.concatenate(
        [jnp.broadcast_to(share[0:1], (8, 128)), jnp.broadcast_to(share[1:2], (8, 128))], axis=1
    )
    W0[...] = dot_nt(shares, onehot.astype(F32), precision=lax.Precision.HIGHEST)
    pl.semaphore_wait(tok.at[2], 2)
    for d in far_first:
        send(W0, RW0.at[d - 1], ws.at[d - 1], wr.at[d - 1], at_z(d))

    def block_scores(n, carry):
        run_peak, run_total = carry
        rows = pl.ds(pl.multiple_of(n * 8, 8), 8)
        f = [F[k, rows, :] for k in range(37)]
        turned = turns_of(f[0:19], [None] + f[19:36])
        scores = [precision * (v - f[36]) for v in turned]
        new_peak = jnp.maximum(run_peak, tree(jnp.maximum, scores))
        total = tree(add, [jnp.exp(v - new_peak) for v in scores])
        return new_peak, run_total * jnp.exp(run_peak - new_peak) + total

    start = (jnp.full((8, 128), -jnp.inf, F32), jnp.zeros((8, 128), F32))
    run_peak, run_total = lax.fori_loop(0, 16, block_scores, start)
    peak = jnp.max(run_peak, axis=0, keepdims=True)
    total = jnp.sum(run_total * jnp.exp(run_peak - peak), axis=0, keepdims=True)
    LS[0:8] = jnp.broadcast_to(peak, (8, 128))
    LS[8:16] = jnp.broadcast_to(total, (8, 128))
    send(LS, LR, sibs.at[3], sibr.at[3], sib)

    for pos, x_half in enumerate((other, x_lo)):
        for d in range(1, 4):
            arrived(RA.at[d - 1, x_half], s1r.at[pos * 3 + d - 1])
    for x_half in range(2):
        for x_top in range(2):
            total = SA[x_half, y, x_top].astype(F32)
            for d in range(3):
                total = total + RA[d, x_half, x_top].astype(F32)
            TA[x_top * 2 + x_half] = total
            TAB[x_top * 2 + x_half] = total.astype(BF16)
    for d in range(1, 4):
        send(TAB.at[(x + d) % 4], R2A.at[d - 1], s2s.at[d - 1], s2r.at[d - 1], at_x(d))
    for d in range(1, 4):
        arrived(RB.at[d - 1], s1r.at[5 + d])
    for y_to in range(4):
        total = SB[x, y_to].astype(F32)
        for d in range(3):
            total = total + RB[d, y_to].astype(F32)
        TB[y_to] = total
        TBB[y_to] = total.astype(BF16)
    for d in range(1, 4):
        send(TBB.at[(y + d) % 4], R2B.at[d - 1], s2s.at[2 + d], s2r.at[2 + d], at_y(d))

    arrived(LR, sibr.at[3])
    peak = jnp.maximum(LS[0:8], LR[0:8])
    total = LS[8:16] * jnp.exp(LS[0:8] - peak) + LR[8:16] * jnp.exp(LR[0:8] - peak)
    evidence = peak + jnp.log(total)
    evid_out[...] = jnp.where(core == 0, evidence[0:1, 0:64], evidence[0:1, 64:128])

    for d in range(1, 16):
        arrived(RW0.at[d - 1], wr.at[d - 1])
    W1[...] = tree(add, [W0[...]] + [RW0[d] for d in range(15)])
    for d in range(1, 4):
        send(W1, RW1.at[d - 1], ws.at[14 + d], wr.at[14 + d], at_y(d))

    for d in range(1, 4):
        arrived(R2A.at[d - 1], s2r.at[d - 1])
    total = TA[x] + R2A[0].astype(F32) + R2A[1].astype(F32) + R2A[2].astype(F32)
    for n in range(8):
        UZ[n] = total[:, n * 128 : n * 128 + 128]
    for d in range(1, 4):
        arrived(R2B.at[d - 1], s2r.at[2 + d])
    total = TB[y] + R2B[0].astype(F32) + R2B[1].astype(F32) + R2B[2].astype(F32)
    for n in range(8):
        UZ[8 + n] = total[:, n * 128 : n * 128 + 128]
    SZ[...] = UZ[...].astype(BF16)
    for d in far_first:
        send(SZ.at[(z + d) % 16], RZ.at[d - 1], zs.at[d - 1], zr.at[d - 1], at_z(d))

    for d in range(1, 4):
        arrived(RW1.at[d - 1], wr.at[14 + d])
    W2[...] = tree(add, [W1[...]] + [RW1[d] for d in range(3)])
    for d in range(1, 4):
        send(W2, RW2.at[d - 1], ws.at[17 + d], wr.at[17 + d], at_x(d))

    for d in range(1, 4):
        arrived(RW2.at[d - 1], wr.at[17 + d])
    weight = tree(add, [W2[...]] + [RW2[d] for d in range(3)])
    pick = lane[0:16] == row[0:16] + q_me * 16
    weight = jnp.sum(jnp.where(pick, jnp.broadcast_to(weight[0:1], (16, 128)), 0.0), axis=1, keepdims=True)
    for copy in sent:
        copy.wait_send()
    for d in range(1, 16):
        arrived(RZ.at[d - 1], zr.at[d - 1])
    total = tree(add, [UZ[z]] + [RZ[d].astype(F32) for d in range(15)])
    avg_out[...] = total / (1.0 + weight)


def body(images, references, precision, candidates):
    table = jnp.asarray(factor_table())
    anywhere = pl.BlockSpec(memory_space=pltpu.HBM)
    vmem = pl.BlockSpec(memory_space=pltpu.VMEM)
    dma = pltpu.SemaphoreType.DMA
    scratch = [
        pltpu.VMEM((128, 4096), BF16),
        pltpu.VMEM((128, 4096), BF16),
        pltpu.VMEM((18, 256, 256), BF16),
        pltpu.VMEM((37, 128, 128), F32),
        pltpu.VMEM((1, 64), F32),
        pltpu.VMEM((2, 64), jnp.int32),
        pltpu.VMEM((8, 128), F32),
        pltpu.VMEM((8, 128), F32),
        pltpu.VMEM((37, 8, 128), F32),
        pltpu.VMEM((16, 128), F32),
        pltpu.VMEM((16, 128), F32),
        pltpu.VMEM((2, 128, 128), F32),
        pltpu.VMEM((2, 128, 128), F32),
        pltpu.VMEM((128, 128), BF16),
        pltpu.VMEM((128, 256), BF16),
        pltpu.VMEM((2, 4, 2, 16, 1024), BF16),
        pltpu.VMEM((3, 2, 2, 16, 1024), BF16),
        pltpu.VMEM((4, 4, 16, 1024), BF16),
        pltpu.VMEM((3, 4, 16, 1024), BF16),
        pltpu.VMEM((4, 16, 1024), F32),
        pltpu.VMEM((4, 16, 1024), BF16),
        pltpu.VMEM((3, 16, 1024), BF16),
        pltpu.VMEM((4, 16, 1024), F32),
        pltpu.VMEM((4, 16, 1024), BF16),
        pltpu.VMEM((3, 16, 1024), BF16),
        pltpu.VMEM((16, 16, 128), F32),
        pltpu.VMEM((16, 16, 128), BF16),
        pltpu.VMEM((15, 16, 128), BF16),
        pltpu.VMEM((8, 128), F32),
        pltpu.VMEM((15, 8, 128), F32),
        pltpu.VMEM((8, 128), F32),
        pltpu.VMEM((3, 8, 128), F32),
        pltpu.VMEM((8, 128), F32),
        pltpu.VMEM((3, 8, 128), F32),
        pltpu.VMEM((16, 128), F32),
        pltpu.VMEM((16, 128), F32),
        dma((5,)),
        pltpu.SemaphoreType.REGULAR((3,)),
        dma((25,)),
        dma((8, 4)),
        dma((4,)),
        dma((4,)),
        dma((9,)),
        dma((9,)),
        dma((6,)),
        dma((6,)),
        dma((15,)),
        dma((15,)),
        dma((21,)),
        dma((21,)),
    ]
    average, evidence = pl.pallas_call(
        kernel,
        out_shape=(jax.ShapeDtypeStruct((16, 128), F32), jax.ShapeDtypeStruct((1, 64), F32)),
        in_specs=[anywhere] * 5,
        out_specs=(vmem, vmem),
        scratch_shapes=scratch,
        compiler_params=pltpu.CompilerParams(
            collective_id=0, has_side_effects=True, vmem_limit_bytes=55200 * 1024
        ),
    )(images, references, precision.reshape(1, 64), candidates.T, table)
    return average, evidence.reshape(64)


def solution(mesh):
    in_specs = (P(("img", "blk"), None), P("blk", None), P(("img", "blk")), P(("img", "blk"), None))
    out_specs = (P("blk", "img"), P(("img", "blk")))
    return jax.shard_map(body, mesh=mesh, in_specs=in_specs, out_specs=out_specs, check_vma=False)
```

```python
import math

import jax
import jax.numpy as jnp
import ml_dtypes
import numpy as np
from jax import lax
from jax.experimental import pallas as pl
from jax.experimental.pallas import tpu as pltpu
from jax.sharding import PartitionSpec as P

CYCLES = 32
ORDERS = 64
TURNS = 36
FEATS = 4096
LANES = 128
MESH = pl.DeviceIdType.MESH
F32 = jnp.float32
BF16 = jnp.bfloat16


def factor_table():
    turns = np.arange(TURNS)
    angle = 2.0 * math.pi / TURNS * ((np.arange(ORDERS)[:, None] * turns[None, :]) % TURNS)
    values = np.stack([np.cos(angle), -np.sin(angle)], axis=1).reshape(2 * ORDERS, TURNS).astype(np.float32)
    high = values.astype(ml_dtypes.bfloat16).astype(np.float32)
    out = np.zeros((128, 128), np.float32)
    out[:, 0:36] = high
    out[:, 40:76] = high
    out[:, 80:116] = values - high
    return out.astype(ml_dtypes.bfloat16)


def weighted(pairs):
    total = None
    for coef, value in pairs:
        if abs(coef) < 1e-12:
            continue
        if abs(coef - 1.0) < 1e-12:
            term = value
        elif abs(coef + 1.0) < 1e-12:
            term = -value
        else:
            term = value * np.float32(coef)
        total = term if total is None else total + term
    return total


def turns_of(a, b):
    def cos(k, s):
        return math.cos(2.0 * math.pi * (k * s % 36) / 36.0)

    def sin(k, s):
        return math.sin(2.0 * math.pi * (k * s % 36) / 36.0)

    even_c, odd_c, even_s, odd_s = {}, {}, {}, {}
    for s in range(5):
        p = weighted([(cos(k, s), a[k]) for k in range(0, 19, 4)])
        q = weighted([(cos(k, s), a[k]) for k in range(2, 19, 4)])
        even_c[s], even_c[9 - s] = p + q, p - q
    for s in range(9):
        odd_c[s] = weighted([(cos(k, s), a[k]) for k in range(1, 18, 2)])
    for s in range(1, 5):
        p = weighted([(sin(k, s), b[k]) for k in range(4, 17, 4)])
        q = weighted([(sin(k, s), b[k]) for k in range(2, 17, 4)])
        even_s[s], even_s[9 - s] = p + q, q - p
    for s in range(1, 10):
        odd_s[s] = weighted([(sin(k, s), b[k]) for k in range(1, 18, 2)])
    x = [None] * 36
    for s in range(10):
        if s < 9:
            c_lo, c_hi = even_c[s] + odd_c[s], even_c[s] - odd_c[s]
        else:
            c_lo = c_hi = even_c[9]
        if s == 0:
            x[0], x[18] = c_lo, c_hi
        elif s == 9:
            x[9], x[27] = c_lo - odd_s[9], c_lo + odd_s[9]
        else:
            s_lo, s_hi = even_s[s] + odd_s[s], odd_s[s] - even_s[s]
            x[s], x[36 - s] = c_lo - s_lo, c_lo + s_lo
            x[18 - s], x[18 + s] = c_hi - s_hi, c_hi + s_hi
    return x


def tree(op, values):
    values = list(values)
    while len(values) > 1:
        nxt = [op(values[i], values[i + 1]) for i in range(0, len(values) - 1, 2)]
        if len(values) % 2:
            nxt.append(values[-1])
        values = nxt
    return values[0]


def add(p, q):
    return p + q


def dot_nt(a, b, **kw):
    return lax.dot_general(a, b, (((1,), (1,)), ((), ())), preferred_element_type=F32, **kw)


def dot_nn(a, b):
    return jnp.dot(a, b, preferred_element_type=F32)


def kernel(
    images, refs, prec, cand, table, avg_out, evid_out,
    G, IM, FI, F, PIN, CIN, AUX, AUXS, CHX, PS, PR, PT, H, TE, OH, SA, RA, SB, RB, TA, TAB, R2A, TB, TBB, R2B,
    OA, OB, UZ, SZ, RZ, W0, RW0, W1, RW1, W2, RW2, LS, LR,
    loc, tok, ags, agr, sibs, sibr, s1s, s1r, s2s, s2r, zs, zr, ws, wr,
):
    img, blk = lax.axis_index("img"), lax.axis_index("blk")
    z, x_lo = img % 16, img // 16
    core, y, x_hi = blk % 2, (blk // 2) % 4, blk // 8
    x = x_hi * 2 + x_lo
    q_me = x_hi * 4 + y

    def dev(x_, y_, z_, c_):
        return ((x_ % 2) * 16 + z_, (x_ // 2) * 8 + y_ * 2 + c_)

    sib = dev(x, y, z, 1 - core)
    x_opp, x_same = 3 - x, x_hi * 2 + 1 - x_lo
    zb = z % 2

    def at_z_of(d):
        return dev(x, y, (z + d) % 16, core)

    same, z_up, z_dn = dev(x_same, y, z, core), at_z_of(1), at_z_of(15)

    def at_y(d):
        return dev(x, (y + d) % 4, z, core)

    def at_x(d):
        return dev((x + d) % 4, y, z, core)

    def at_z(d):
        return dev(x, y, (z + d) % 16, core)

    sent = []
    far_first = sorted(range(1, 16), key=lambda d: -min(d, 16 - d))

    def send(src, dst, ssem, rsem, to):
        copy = pltpu.make_async_remote_copy(
            src_ref=src, dst_ref=dst, send_sem=ssem, recv_sem=rsem, device_id=to, device_id_type=MESH
        )
        copy.start()
        sent.append(copy)

    def arrived(dst, rsem):
        pltpu.make_async_copy(dst, dst, rsem).wait()

    mine_rows = pl.ds(pl.multiple_of(core * 64, 64), 64)
    own_p = pltpu.make_async_copy(prec, PIN, loc.at[3])
    own_p.start()
    own_c = pltpu.make_async_copy(cand, CIN, loc.at[4])
    own_c.start()
    own_g = pltpu.make_async_copy(refs, G.at[pl.ds(pl.multiple_of(q_me * 16, 16), 16)], loc.at[1])
    own_g.start()
    own_im = pltpu.make_async_copy(images, IM.at[mine_rows], loc.at[0])
    own_im.start()
    own_t = pltpu.make_async_copy(table, TE, loc.at[2])
    own_t.start()

    barrier = pltpu.get_barrier_semaphore()
    partners = [dev(x_opp, (y + d) % 4, z, core) for d in range(1, 4)]
    partners += [at_y(d) for d in range(1, 4)] + [at_x(d) for d in range(1, 4)]
    partners += [z_up, z_dn, sib]
    for to in partners:
        pl.semaphore_signal(barrier, inc=1, device_id=to, device_id_type=MESH)
    own_p.wait()
    own_c.wait()
    mine = jnp.concatenate([PIN[...], CIN[...].astype(F32)], axis=0)
    AUX[0:3, :] = jnp.concatenate([mine, mine], axis=1)
    AUX[3:8, :] = jnp.zeros((5, 128), F32)
    pl.semaphore_wait(barrier, len(partners))

    def token(n):
        for d in (1 << n, 16 - (1 << n)):
            pl.semaphore_signal(tok.at[n], inc=1, device_id=at_z(d), device_id_type=MESH)

    def rows_at(q):
        return pl.ds(pl.multiple_of(q * 16, 16), 16)

    def half(q, n):
        return G.at[rows_at(q), pl.ds(pl.multiple_of(n * 2048, 2048), 2048)]

    def quarter(q, n):
        return G.at[rows_at(q), pl.ds(pl.multiple_of(n * 1024, 1024), 1024)]

    mine_f = (z + 2 * x_lo) % 4
    same_f, up_f, dn_f = (mine_f + 2) % 4, (mine_f + 1) % 4, (mine_f + 3) % 4
    col, far = x_hi * 4, (1 - x_hi) * 4
    order = (0, 1, 3, 2)

    def near_q(d):
        return col + (y + d) % 4

    def far_q(d):
        return far + (y + d) % 4

    send(AUX, AUXS, sibs.at[1], sibr.at[1], sib)
    send(images, IM.at[mine_rows], sibs.at[0], sibr.at[0], sib)
    opp_quarter = refs.at[:, pl.ds(pl.multiple_of(same_f * 1024, 1024), 1024)]
    own_half = refs.at[:, pl.ds(pl.multiple_of(zb * 2048, 2048), 2048)]
    for n, d in enumerate(order):
        to = dev(x_opp, (y + d) % 4, z, core)
        send(opp_quarter, quarter(q_me, same_f), ags.at[n], agr.at[q_me, same_f], to)
    for n, d in enumerate((1, 3, 2)):
        send(own_half, half(q_me, zb), ags.at[4 + n], agr.at[q_me, 2 * zb], at_y(d))
    token(0)
    own_im.wait()
    arrived(IM.at[pl.ds(pl.multiple_of((1 - core) * 64, 64), 64)], sibr.at[0])
    arrived(AUXS, sibr.at[1])

    row = lax.broadcasted_iota(jnp.int32, (128, 128), 0)
    lane = lax.broadcasted_iota(jnp.int32, (128, 128), 1)

    def swap(src, dst):
        first = dst % 64 < 32
        return jnp.where(first & (src == dst + 32), 1.0, jnp.where((~first) & (src == dst - 32), -1.0, 0.0))

    eye = jnp.where(row == lane, 1.0, 0.0)
    rows_of = jnp.concatenate([eye, swap(lane, row)], axis=0).astype(BF16)

    def prepare(first, count, half):
        def step(n, carry):
            t = first + n
            block = IM[:, pl.ds(pl.multiple_of(t * 128, 128), 128)]
            both = dot_nt(rows_of, block)
            j = t - 18 * half
            sign = jnp.where(j < 9, 1.0, -1.0).astype(F32)
            FI[j, half * 128 : half * 128 + 128, 0:128] = both[0:128].astype(BF16)
            FI[j, half * 128 : half * 128 + 128, 128:256] = (both[128:256] * sign).astype(BF16)
            return carry

        lax.fori_loop(0, count, step, 0, unroll=2)

    def hand_far(n):
        q = far_q(order[n])
        part, sem = quarter(q, mine_f), agr.at[q, mine_f]
        arrived(part, sem)
        for m, to in enumerate((same, z_up, z_dn)):
            send(part, part, ags.at[13 + 3 * n + m], sem, to)

    def hand_near(n):
        q = near_q((1, 3, 2)[n])
        arrived(half(q, zb), agr.at[q, 2 * zb])
        for m, to in enumerate((z_up, z_dn)):
            part = quarter(q, 2 * zb + m)
            send(part, part, ags.at[7 + 2 * n + m], agr.at[q, 2 * zb + m], to)

    prepare(0, 4, 0)
    hand_far(0)
    prepare(4, 2, 0)
    hand_far(1)
    hand_far(2)
    hand_near(0)
    hand_near(1)
    prepare(6, 2, 0)
    hand_far(3)
    hand_near(2)
    pl.semaphore_wait(tok.at[0], 2)
    token(1)
    prepare(8, 10, 0)
    prepare(18, 14, 1)

    right = lax.broadcasted_iota(jnp.int32, (8, 128), 1) >= 64
    auxc = jnp.where(right == (core == 1), AUX[...], AUXS[...])
    precision = auxc[0:1, :]
    class_id = ((row // 16) * 32 + core * 16 + row % 16).astype(F32)
    picks = [auxc[1:2, :] == class_id, auxc[2:3, :] == class_id]
    for k in range(2):
        OH[:, k * 128 : k * 128 + 128] = jnp.where(picks[k], 1.0, 0.0).astype(BF16)
    PT[...] = jnp.zeros_like(PT)

    own_g.wait()
    for d in (1, 3, 2):
        q = near_q(d)
        for m in range(2):
            arrived(quarter(q, 2 * (1 - zb) + m), agr.at[q, 2 * (1 - zb) + m])

    low = (lax.broadcasted_iota(jnp.int32, (64, 256), 1) % 128) < 64

    def harmonics(first):
        rows = pl.ds(pl.multiple_of(first * 16, 64), 64)
        for j in range(18):
            left = G[rows, j * 128 : j * 128 + 128]
            if j < 14:
                tile = jnp.concatenate([left, G[rows, (18 + j) * 128 : (18 + j) * 128 + 128]], axis=1)
                keep, right_side = low, FI[j]
            else:
                tile, keep, right_side = left, low[:, 0:128], FI[j, 0:128, :]
            zero = jnp.zeros_like(tile)
            stacked = jnp.concatenate([jnp.where(keep, tile, zero), jnp.where(keep, zero, tile)], axis=0)
            out = dot_nn(stacked, right_side)
            even, odd = out[0:64], out[64:128]
            k_even, k_odd = (2 * j if j <= 9 else 36 - 2 * j), (2 * j + 1 if j <= 8 else 35 - 2 * j)
            if j <= 9:
                F[k_even, rows, :] = even[:, 0:128]
            else:
                F[k_even, rows, :] += even[:, 0:128]
            if 0 < k_even < 18:
                if j <= 9:
                    F[18 + k_even, rows, :] = even[:, 128:256]
                else:
                    F[18 + k_even, rows, :] += even[:, 128:256]
            if j <= 8:
                F[k_odd, rows, :] = odd[:, 0:128]
                F[18 + k_odd, rows, :] = odd[:, 128:256]
            else:
                F[k_odd, rows, :] += odd[:, 0:128]
                F[18 + k_odd, rows, :] += odd[:, 128:256]
        square = jnp.zeros((64, 128), F32)
        for t in range(32):
            value = G[rows, t * 128 : t * 128 + 128].astype(F32)
            square = square + value * value
        F[36, rows, :] = jnp.broadcast_to(0.5 * jnp.sum(square, axis=1, keepdims=True), (64, 128))

    even_row = lax.broadcasted_iota(jnp.int32, (8, 128), 0) % 2 == 0

    def choose(first, more):
        rows = pl.ds(pl.multiple_of(first * 16, 64), 64)
        ids = (((row[0:64] // 16) + first) * 32 + core * 16 + row[0:64] % 16).astype(F32)
        keep = [auxc[k : k + 1, :] == ids for k in (1, 2)]

        def step(kk, carry):
            f = F[kk, rows, :]
            parts = []
            for k in range(2):
                kept = jnp.where(keep[k], f, 0.0)
                total = tree(add, [kept[n * 8 : n * 8 + 8] for n in range(8)])
                parts.append(total + pltpu.roll(total, 1, 0))
            both = jnp.where(even_row, parts[0], parts[1])
            both = both + pltpu.roll(both, 2, 0)
            both = both + pltpu.roll(both, 4, 0)
            CHX[kk] = CHX[kk] + both if more else both
            return carry

        lax.fori_loop(0, 36, step, 0, unroll=4)
        step(36, 0)

    harmonics(col)
    choose(col, False)
    pl.semaphore_wait(tok.at[1], 2)
    token(2)
    for d in order:
        for f in (same_f, up_f, dn_f):
            arrived(quarter(far_q(d), f), agr.at[far_q(d), f])
    harmonics(far)
    choose(far, True)
    names = jnp.where(even_row, auxc[1:2, :], auxc[2:3, :]).astype(jnp.int32)
    held = (names // 16) % 2 == core

    def both_picks(op, v):
        return op(v, jnp.where(even_row, pltpu.roll(v, 7, 0), pltpu.roll(v, 1, 0)))

    coefs = [CHX[k] for k in range(37)]
    turned = turns_of(coefs[0:19], [None] + coefs[19:36])
    scores = [precision * (v - coefs[36]) for v in turned]
    own_peak = both_picks(jnp.maximum, jnp.where(held, tree(jnp.maximum, scores), -1e30))
    weights = [jnp.where(held, jnp.exp(v - own_peak), 0.0) for v in scores]
    share = tree(add, weights)
    own_total = both_picks(add, share)
    PS[0:8] = own_peak
    PS[8:16] = own_total
    send(PS, PR, sibs.at[2], sibr.at[2], sib)
    for s in range(TURNS):
        high = weights[s].astype(BF16).astype(F32)
        rest = weights[s] - high
        for k in range(2):
            PT[k, s : s + 1, :] = high[k : k + 1]
            PT[k, 40 + s : 41 + s, :] = rest[k : k + 1]
            PT[k, 80 + s : 81 + s, :] = high[k : k + 1]
    own_t.wait()
    spectra = [dot_nn(TE[...], PT[k].astype(BF16)) for k in range(2)]
    arrived(PR, sibr.at[2])
    peak = jnp.maximum(own_peak, PR[0:8])
    own_part = jnp.exp(own_peak - peak)
    scale = own_part / (own_part * own_total + jnp.exp(PR[0:8] - peak) * PR[8:16])
    share = share * scale
    for k in range(2):
        H[k] = spectra[k] * scale[0:1]

    onehot = OH[...]

    def sums(x_half, second, mine):
        def step(v, carry):
            u = x_half * 8 + second * 4 + v
            out_lanes = pl.ds(pl.multiple_of(v * 256, 256), 256)
            upper = u // 9
            factors = [H[k, pl.ds(pl.multiple_of(u * 8, 8), 8), :] for k in range(2)]
            columns = [[], []]
            for part in range(2):
                rows = pl.ds(pl.multiple_of(upper * 128, 128), 128)
                tile = FI[2 * u + part - 18 * upper, rows, 0:128].astype(F32)
                for m in range(2):
                    real, imag = tile[m * 64 : m * 64 + 32], tile[m * 64 + 32 : m * 64 + 64]
                    for k in range(2):
                        at = (part * 2 + m) * 2
                        f_real, f_imag = factors[k][at : at + 1], factors[k][at + 1 : at + 2]
                        columns[k].append((real * f_real - imag * f_imag).astype(BF16))
                        columns[k].append((real * f_imag + imag * f_real).astype(BF16))
            rows_in = jnp.concatenate([jnp.concatenate(c, axis=0) for c in columns], axis=1)
            exact = dot_nt(onehot, rows_in)
            out = exact.astype(BF16)
            parts = [exact[q * 16 : q * 16 + 16] for q in range(8)]
            if second and mine:
                for n in range(4):
                    OB[n, :, out_lanes] = jnp.where(x_hi == 0, parts[n], parts[4 + n])
            if not second:
                for n in range(2):
                    four = parts[n * 4 : n * 4 + 4]
                    lower, upper_two = jnp.where(y == 0, four[0], four[1]), jnp.where(y == 2, four[2], four[3])
                    OA[n * 2 + x_half, :, out_lanes] = jnp.where(y < 2, lower, upper_two)
            for q in range(8):
                block = out[q * 16 : q * 16 + 16]
                if second:
                    SB[(q // 4) * 2 + x_half, q % 4, :, out_lanes] = block
                else:
                    SA[x_half, q % 4, q // 4, :, out_lanes] = block
            return carry

        lax.fori_loop(0, 4, step, 0, unroll=True)

    other = 1 - x_lo
    for pos, x_half in enumerate((x_lo, other)):
        sums(x_half, 1, pos == 0)
        for d in ((2,), (1, 3))[pos]:
            send(SB.at[(x + d) % 4], RB.at[d - 1], s1s.at[5 + d], s1r.at[5 + d], at_x(d))
        sums(x_half, 0, pos == 0)
        for d in (2, 1, 3):
            n = (1 - pos) * 3 + d - 1
            send(SA.at[x_half, (y + d) % 4], RA.at[d - 1, x_half], s1s.at[n], s1r.at[n], at_y(d))
    shares = jnp.concatenate(
        [jnp.broadcast_to(share[0:1], (8, 128)), jnp.broadcast_to(share[1:2], (8, 128))], axis=1
    )
    W0[...] = dot_nt(shares, onehot.astype(F32), precision=lax.Precision.HIGHEST)
    pl.semaphore_wait(tok.at[2], 2)
    for d in far_first:
        send(W0, RW0.at[d - 1], ws.at[d - 1], wr.at[d - 1], at_z(d))

    def block_scores(n, carry):
        run_peak, run_total = carry
        rows = pl.ds(pl.multiple_of(n * 8, 8), 8)
        f = [F[k, rows, :] for k in range(37)]
        turned = turns_of(f[0:19], [None] + f[19:36])
        scores = [precision * (v - f[36]) for v in turned]
        new_peak = jnp.maximum(run_peak, tree(jnp.maximum, scores))
        total = tree(add, [jnp.exp(v - new_peak) for v in scores])
        return new_peak, run_total * jnp.exp(run_peak - new_peak) + total

    start = (jnp.full((8, 128), -jnp.inf, F32), jnp.zeros((8, 128), F32))
    run_peak, run_total = lax.fori_loop(0, 16, block_scores, start)
    peak = jnp.max(run_peak, axis=0, keepdims=True)
    total = jnp.sum(run_total * jnp.exp(run_peak - peak), axis=0, keepdims=True)
    LS[0:8] = jnp.broadcast_to(peak, (8, 128))
    LS[8:16] = jnp.broadcast_to(total, (8, 128))
    send(LS, LR, sibs.at[3], sibr.at[3], sib)

    for pos, x_half in enumerate((other, x_lo)):
        for d in range(1, 4):
            arrived(RA.at[d - 1, x_half], s1r.at[pos * 3 + d - 1])
    for d in (2, 1, 3, 0):
        x_to = (x + d) % 4
        total = OA[x_to]
        for n in range(3):
            total = total + RA[n, x_to % 2, x_to // 2].astype(F32)
        if d:
            TAB[d - 1] = total.astype(BF16)
            send(TAB.at[d - 1], R2A.at[d - 1], s2s.at[d - 1], s2r.at[d - 1], at_x(d))
        else:
            TA[...] = total
    for d in range(1, 4):
        arrived(RB.at[d - 1], s1r.at[5 + d])
    for d in (2, 1, 3, 0):
        y_to = (y + d) % 4
        total = OB[y_to]
        for n in range(3):
            total = total + RB[n, y_to].astype(F32)
        if d:
            TBB[d - 1] = total.astype(BF16)
            send(TBB.at[d - 1], R2B.at[d - 1], s2s.at[2 + d], s2r.at[2 + d], at_y(d))
        else:
            TB[...] = total

    arrived(LR, sibr.at[3])
    peak = jnp.maximum(LS[0:8], LR[0:8])
    total = LS[8:16] * jnp.exp(LS[0:8] - peak) + LR[8:16] * jnp.exp(LR[0:8] - peak)
    evidence = peak + jnp.log(total)
    evid_out[...] = jnp.where(core == 0, evidence[0:1, 0:64], evidence[0:1, 64:128])

    for d in range(1, 16):
        arrived(RW0.at[d - 1], wr.at[d - 1])
    W1[...] = tree(add, [W0[...]] + [RW0[d] for d in range(15)])
    for d in range(1, 4):
        send(W1, RW1.at[d - 1], ws.at[14 + d], wr.at[14 + d], at_y(d))

    for d in range(1, 4):
        arrived(R2A.at[d - 1], s2r.at[d - 1])
    total = TA[...] + R2A[0].astype(F32) + R2A[1].astype(F32) + R2A[2].astype(F32)
    for n in range(8):
        UZ[n] = total[:, n * 128 : n * 128 + 128]
    for d in range(1, 4):
        arrived(R2B.at[d - 1], s2r.at[2 + d])
    total = TB[...] + R2B[0].astype(F32) + R2B[1].astype(F32) + R2B[2].astype(F32)
    for n in range(8):
        UZ[8 + n] = total[:, n * 128 : n * 128 + 128]
    SZ[...] = UZ[...].astype(BF16)
    for d in far_first:
        send(SZ.at[(z + d) % 16], RZ.at[d - 1], zs.at[d - 1], zr.at[d - 1], at_z(d))

    for d in range(1, 4):
        arrived(RW1.at[d - 1], wr.at[14 + d])
    W2[...] = tree(add, [W1[...]] + [RW1[d] for d in range(3)])
    for d in range(1, 4):
        send(W2, RW2.at[d - 1], ws.at[17 + d], wr.at[17 + d], at_x(d))

    for d in range(1, 4):
        arrived(RW2.at[d - 1], wr.at[17 + d])
    weight = tree(add, [W2[...]] + [RW2[d] for d in range(3)])
    pick = lane[0:16] == row[0:16] + q_me * 16
    weight = jnp.sum(jnp.where(pick, jnp.broadcast_to(weight[0:1], (16, 128)), 0.0), axis=1, keepdims=True)
    for copy in sent:
        copy.wait_send()
    for d in range(1, 16):
        arrived(RZ.at[d - 1], zr.at[d - 1])
    total = tree(add, [UZ[z]] + [RZ[d].astype(F32) for d in range(15)])
    avg_out[...] = total / (1.0 + weight)


def body(images, references, precision, candidates):
    table = jnp.asarray(factor_table())
    anywhere = pl.BlockSpec(memory_space=pltpu.HBM)
    vmem = pl.BlockSpec(memory_space=pltpu.VMEM)
    dma = pltpu.SemaphoreType.DMA
    scratch = [
        pltpu.VMEM((128, 4096), BF16),
        pltpu.VMEM((128, 4096), BF16),
        pltpu.VMEM((18, 256, 256), BF16),
        pltpu.VMEM((37, 128, 128), F32),
        pltpu.VMEM((1, 64), F32),
        pltpu.VMEM((2, 64), jnp.int32),
        pltpu.VMEM((8, 128), F32),
        pltpu.VMEM((8, 128), F32),
        pltpu.VMEM((37, 8, 128), F32),
        pltpu.VMEM((16, 128), F32),
        pltpu.VMEM((16, 128), F32),
        pltpu.VMEM((2, 128, 128), F32),
        pltpu.VMEM((2, 128, 128), F32),
        pltpu.VMEM((128, 128), BF16),
        pltpu.VMEM((128, 256), BF16),
        pltpu.VMEM((2, 4, 2, 16, 1024), BF16),
        pltpu.VMEM((3, 2, 2, 16, 1024), BF16),
        pltpu.VMEM((4, 4, 16, 1024), BF16),
        pltpu.VMEM((3, 4, 16, 1024), BF16),
        pltpu.VMEM((16, 1024), F32),
        pltpu.VMEM((3, 16, 1024), BF16),
        pltpu.VMEM((3, 16, 1024), BF16),
        pltpu.VMEM((16, 1024), F32),
        pltpu.VMEM((3, 16, 1024), BF16),
        pltpu.VMEM((3, 16, 1024), BF16),
        pltpu.VMEM((4, 16, 1024), F32),
        pltpu.VMEM((4, 16, 1024), F32),
        pltpu.VMEM((16, 16, 128), F32),
        pltpu.VMEM((16, 16, 128), BF16),
        pltpu.VMEM((15, 16, 128), BF16),
        pltpu.VMEM((8, 128), F32),
        pltpu.VMEM((15, 8, 128), F32),
        pltpu.VMEM((8, 128), F32),
        pltpu.VMEM((3, 8, 128), F32),
        pltpu.VMEM((8, 128), F32),
        pltpu.VMEM((3, 8, 128), F32),
        pltpu.VMEM((16, 128), F32),
        pltpu.VMEM((16, 128), F32),
        dma((5,)),
        pltpu.SemaphoreType.REGULAR((3,)),
        dma((25,)),
        dma((8, 4)),
        dma((4,)),
        dma((4,)),
        dma((9,)),
        dma((9,)),
        dma((6,)),
        dma((6,)),
        dma((15,)),
        dma((15,)),
        dma((21,)),
        dma((21,)),
    ]
    average, evidence = pl.pallas_call(
        kernel,
        out_shape=(jax.ShapeDtypeStruct((16, 128), F32), jax.ShapeDtypeStruct((1, 64), F32)),
        in_specs=[anywhere] * 5,
        out_specs=(vmem, vmem),
        scratch_shapes=scratch,
        compiler_params=pltpu.CompilerParams(
            collective_id=0, has_side_effects=True, vmem_limit_bytes=55200 * 1024
        ),
    )(images, references, precision.reshape(1, 64), candidates.T, table)
    return average, evidence.reshape(64)


def solution(mesh):
    in_specs = (P(("img", "blk"), None), P("blk", None), P(("img", "blk")), P(("img", "blk"), None))
    out_specs = (P("blk", "img"), P(("img", "blk")))
    return jax.shard_map(body, mesh=mesh, in_specs=in_specs, out_specs=out_specs, check_vma=False)
```

```python
import math

import jax
import jax.numpy as jnp
import ml_dtypes
import numpy as np
from jax import lax
from jax.experimental import pallas as pl
from jax.experimental.pallas import tpu as pltpu
from jax.sharding import PartitionSpec as P

CYCLES = 32
ORDERS = 64
TURNS = 36
FEATS = 4096
LANES = 128
MESH = pl.DeviceIdType.MESH
F32 = jnp.float32
BF16 = jnp.bfloat16


def factor_table():
    turns = np.arange(TURNS)
    angle = 2.0 * math.pi / TURNS * ((np.arange(ORDERS)[:, None] * turns[None, :]) % TURNS)
    values = np.stack([np.cos(angle), -np.sin(angle)], axis=1).reshape(2 * ORDERS, TURNS).astype(np.float32)
    high = values.astype(ml_dtypes.bfloat16).astype(np.float32)
    out = np.zeros((128, 128), np.float32)
    out[:, 0:36] = high
    out[:, 40:76] = high
    out[:, 80:116] = values - high
    return out.astype(ml_dtypes.bfloat16)


def weighted(pairs):
    total = None
    for coef, value in pairs:
        if abs(coef) < 1e-12:
            continue
        if abs(coef - 1.0) < 1e-12:
            term = value
        elif abs(coef + 1.0) < 1e-12:
            term = -value
        else:
            term = value * np.float32(coef)
        total = term if total is None else total + term
    return total


def turns_of(a, b):
    def cos(k, s):
        return math.cos(2.0 * math.pi * (k * s % 36) / 36.0)

    def sin(k, s):
        return math.sin(2.0 * math.pi * (k * s % 36) / 36.0)

    even_c, odd_c, even_s, odd_s = {}, {}, {}, {}
    for s in range(5):
        p = weighted([(cos(k, s), a[k]) for k in range(0, 19, 4)])
        q = weighted([(cos(k, s), a[k]) for k in range(2, 19, 4)])
        even_c[s], even_c[9 - s] = p + q, p - q
    for s in range(9):
        odd_c[s] = weighted([(cos(k, s), a[k]) for k in range(1, 18, 2)])
    for s in range(1, 5):
        p = weighted([(sin(k, s), b[k]) for k in range(4, 17, 4)])
        q = weighted([(sin(k, s), b[k]) for k in range(2, 17, 4)])
        even_s[s], even_s[9 - s] = p + q, q - p
    for s in range(1, 10):
        odd_s[s] = weighted([(sin(k, s), b[k]) for k in range(1, 18, 2)])
    x = [None] * 36
    for s in range(10):
        if s < 9:
            c_lo, c_hi = even_c[s] + odd_c[s], even_c[s] - odd_c[s]
        else:
            c_lo = c_hi = even_c[9]
        if s == 0:
            x[0], x[18] = c_lo, c_hi
        elif s == 9:
            x[9], x[27] = c_lo - odd_s[9], c_lo + odd_s[9]
        else:
            s_lo, s_hi = even_s[s] + odd_s[s], odd_s[s] - even_s[s]
            x[s], x[36 - s] = c_lo - s_lo, c_lo + s_lo
            x[18 - s], x[18 + s] = c_hi - s_hi, c_hi + s_hi
    return x


def tree(op, values):
    values = list(values)
    while len(values) > 1:
        nxt = [op(values[i], values[i + 1]) for i in range(0, len(values) - 1, 2)]
        if len(values) % 2:
            nxt.append(values[-1])
        values = nxt
    return values[0]


def add(p, q):
    return p + q


def dot_nt(a, b, **kw):
    return lax.dot_general(a, b, (((1,), (1,)), ((), ())), preferred_element_type=F32, **kw)


def dot_nn(a, b):
    return jnp.dot(a, b, preferred_element_type=F32)


def kernel(
    images, refs, prec, cand, table, avg_out, evid_out,
    G, IM, FI, F, PIN, CIN, AUX, AUXS, CHX, PS, PR, PT, H, TE, OH, SA, RA, SB, RB, TA, TAB, R2A, TB, TBB, R2B,
    OA, OB, UZ, SZ, RZ, W0, RW0, W1, RW1, W2, RW2, LS, LR,
    loc, tok, ags, agr, sibs, sibr, s1s, s1r, s2s, s2r, zs, zr, ws, wr,
):
    img, blk = lax.axis_index("img"), lax.axis_index("blk")
    z, x_lo = img % 16, img // 16
    core, y, x_hi = blk % 2, (blk // 2) % 4, blk // 8
    x = x_hi * 2 + x_lo
    q_me = x_hi * 4 + y

    def dev(x_, y_, z_, c_):
        return ((x_ % 2) * 16 + z_, (x_ // 2) * 8 + y_ * 2 + c_)

    sib = dev(x, y, z, 1 - core)
    x_opp, x_same = 3 - x, x_hi * 2 + 1 - x_lo
    def at_z_of(d):
        return dev(x, y, (z + d) % 16, core)

    same, z_up, z_dn = dev(x_same, y, z, core), at_z_of(1), at_z_of(15)

    def at_y(d):
        return dev(x, (y + d) % 4, z, core)

    def at_x(d):
        return dev((x + d) % 4, y, z, core)

    def at_z(d):
        return dev(x, y, (z + d) % 16, core)

    sent = []
    far_first = sorted(range(1, 16), key=lambda d: -min(d, 16 - d))

    def send(src, dst, ssem, rsem, to):
        copy = pltpu.make_async_remote_copy(
            src_ref=src, dst_ref=dst, send_sem=ssem, recv_sem=rsem, device_id=to, device_id_type=MESH
        )
        copy.start()
        sent.append(copy)

    def arrived(dst, rsem):
        pltpu.make_async_copy(dst, dst, rsem).wait()

    mine_rows = pl.ds(pl.multiple_of(core * 64, 64), 64)
    own_p = pltpu.make_async_copy(prec, PIN, loc.at[3])
    own_p.start()
    own_c = pltpu.make_async_copy(cand, CIN, loc.at[4])
    own_c.start()
    own_g = pltpu.make_async_copy(refs, G.at[pl.ds(pl.multiple_of(q_me * 16, 16), 16)], loc.at[1])
    own_g.start()
    own_im = pltpu.make_async_copy(images, IM.at[mine_rows], loc.at[0])
    own_im.start()
    own_t = pltpu.make_async_copy(table, TE, loc.at[2])
    own_t.start()

    barrier = pltpu.get_barrier_semaphore()
    partners = [dev(x_opp, (y + d) % 4, z, core) for d in range(1, 4)]
    partners += [at_y(d) for d in range(1, 4)] + [at_x(d) for d in range(1, 4)]
    partners += [z_up, z_dn, sib]
    for to in partners:
        pl.semaphore_signal(barrier, inc=1, device_id=to, device_id_type=MESH)
    own_p.wait()
    own_c.wait()
    mine = jnp.concatenate([PIN[...], CIN[...].astype(F32)], axis=0)
    AUX[0:3, :] = jnp.concatenate([mine, mine], axis=1)
    AUX[3:8, :] = jnp.zeros((5, 128), F32)
    pl.semaphore_wait(barrier, len(partners))

    def token(n):
        for d in (1 << n, 16 - (1 << n)):
            pl.semaphore_signal(tok.at[n], inc=1, device_id=at_z(d), device_id_type=MESH)

    def rows_at(q):
        return pl.ds(pl.multiple_of(q * 16, 16), 16)

    def quarter(q, n):
        return G.at[rows_at(q), pl.ds(pl.multiple_of(n * 1024, 1024), 1024)]

    mine_f = (z + 2 * x_lo) % 4
    same_f, up_f, dn_f = (mine_f + 2) % 4, (mine_f + 1) % 4, (mine_f + 3) % 4
    col, far = x_hi * 4, (1 - x_hi) * 4
    order = (0, 1, 3, 2)

    def near_q(d):
        return col + (y + d) % 4

    def far_q(d):
        return far + (y + d) % 4

    send(AUX, AUXS, sibs.at[1], sibr.at[1], sib)
    send(images, IM.at[mine_rows], sibs.at[0], sibr.at[0], sib)
    opp_quarter = refs.at[:, pl.ds(pl.multiple_of(same_f * 1024, 1024), 1024)]
    for n, d in enumerate(order):
        to = dev(x_opp, (y + d) % 4, z, core)
        send(opp_quarter, quarter(q_me, same_f), ags.at[n], agr.at[q_me, same_f], to)
    for n, d in enumerate((1, 3, 2)):
        send(refs, G.at[rows_at(q_me)], ags.at[4 + n], agr.at[q_me, 0], at_y(d))
    token(0)
    own_im.wait()
    arrived(IM.at[pl.ds(pl.multiple_of((1 - core) * 64, 64), 64)], sibr.at[0])
    arrived(AUXS, sibr.at[1])

    row = lax.broadcasted_iota(jnp.int32, (128, 128), 0)
    lane = lax.broadcasted_iota(jnp.int32, (128, 128), 1)

    def swap(src, dst):
        first = dst % 64 < 32
        return jnp.where(first & (src == dst + 32), 1.0, jnp.where((~first) & (src == dst - 32), -1.0, 0.0))

    eye = jnp.where(row == lane, 1.0, 0.0)
    rows_of = jnp.concatenate([eye, swap(lane, row)], axis=0).astype(BF16)

    def prepare(first, count, half):
        def step(n, carry):
            t = first + n
            block = IM[:, pl.ds(pl.multiple_of(t * 128, 128), 128)]
            both = dot_nt(rows_of, block)
            j = t - 18 * half
            sign = jnp.where(j < 9, 1.0, -1.0).astype(F32)
            FI[j, half * 128 : half * 128 + 128, 0:128] = both[0:128].astype(BF16)
            FI[j, half * 128 : half * 128 + 128, 128:256] = (both[128:256] * sign).astype(BF16)
            return carry

        lax.fori_loop(0, count, step, 0, unroll=2)

    def hand_far(n):
        q = far_q(order[n])
        part, sem = quarter(q, mine_f), agr.at[q, mine_f]
        arrived(part, sem)
        for m, to in enumerate((same, z_up, z_dn)):
            send(part, part, ags.at[13 + 3 * n + m], sem, to)

    prepare(0, 4, 0)
    hand_far(0)
    prepare(4, 2, 0)
    hand_far(1)
    hand_far(2)
    prepare(6, 2, 0)
    hand_far(3)
    pl.semaphore_wait(tok.at[0], 2)
    token(1)
    prepare(8, 10, 0)
    prepare(18, 14, 1)

    right = lax.broadcasted_iota(jnp.int32, (8, 128), 1) >= 64
    auxc = jnp.where(right == (core == 1), AUX[...], AUXS[...])
    precision = auxc[0:1, :]
    class_id = ((row // 16) * 32 + core * 16 + row % 16).astype(F32)
    picks = [auxc[1:2, :] == class_id, auxc[2:3, :] == class_id]
    for k in range(2):
        OH[:, k * 128 : k * 128 + 128] = jnp.where(picks[k], 1.0, 0.0).astype(BF16)
    PT[...] = jnp.zeros_like(PT)

    own_g.wait()
    for d in (1, 3, 2):
        q = near_q(d)
        arrived(G.at[rows_at(q)], agr.at[q, 0])

    low = (lax.broadcasted_iota(jnp.int32, (64, 256), 1) % 128) < 64

    def harmonics(first):
        rows = pl.ds(pl.multiple_of(first * 16, 64), 64)
        for j in range(18):
            left = G[rows, j * 128 : j * 128 + 128]
            if j < 14:
                tile = jnp.concatenate([left, G[rows, (18 + j) * 128 : (18 + j) * 128 + 128]], axis=1)
                keep, right_side = low, FI[j]
            else:
                tile, keep, right_side = left, low[:, 0:128], FI[j, 0:128, :]
            zero = jnp.zeros_like(tile)
            stacked = jnp.concatenate([jnp.where(keep, tile, zero), jnp.where(keep, zero, tile)], axis=0)
            out = dot_nn(stacked, right_side)
            even, odd = out[0:64], out[64:128]
            k_even, k_odd = (2 * j if j <= 9 else 36 - 2 * j), (2 * j + 1 if j <= 8 else 35 - 2 * j)
            if j <= 9:
                F[k_even, rows, :] = even[:, 0:128]
            else:
                F[k_even, rows, :] += even[:, 0:128]
            if 0 < k_even < 18:
                if j <= 9:
                    F[18 + k_even, rows, :] = even[:, 128:256]
                else:
                    F[18 + k_even, rows, :] += even[:, 128:256]
            if j <= 8:
                F[k_odd, rows, :] = odd[:, 0:128]
                F[18 + k_odd, rows, :] = odd[:, 128:256]
            else:
                F[k_odd, rows, :] += odd[:, 0:128]
                F[18 + k_odd, rows, :] += odd[:, 128:256]
        square = jnp.zeros((64, 128), F32)
        for t in range(32):
            value = G[rows, t * 128 : t * 128 + 128].astype(F32)
            square = square + value * value
        F[36, rows, :] = jnp.broadcast_to(0.5 * jnp.sum(square, axis=1, keepdims=True), (64, 128))

    even_row = lax.broadcasted_iota(jnp.int32, (8, 128), 0) % 2 == 0

    def choose(first, more):
        rows = pl.ds(pl.multiple_of(first * 16, 64), 64)
        ids = (((row[0:64] // 16) + first) * 32 + core * 16 + row[0:64] % 16).astype(F32)
        keep = [auxc[k : k + 1, :] == ids for k in (1, 2)]

        def step(kk, carry):
            f = F[kk, rows, :]
            parts = []
            for k in range(2):
                kept = jnp.where(keep[k], f, 0.0)
                total = tree(add, [kept[n * 8 : n * 8 + 8] for n in range(8)])
                parts.append(total + pltpu.roll(total, 1, 0))
            both = jnp.where(even_row, parts[0], parts[1])
            both = both + pltpu.roll(both, 2, 0)
            both = both + pltpu.roll(both, 4, 0)
            CHX[kk] = CHX[kk] + both if more else both
            return carry

        lax.fori_loop(0, 36, step, 0, unroll=4)
        step(36, 0)

    harmonics(col)
    choose(col, False)
    pl.semaphore_wait(tok.at[1], 2)
    token(2)
    for d in order:
        for f in (same_f, up_f, dn_f):
            arrived(quarter(far_q(d), f), agr.at[far_q(d), f])
    harmonics(far)
    choose(far, True)
    names = jnp.where(even_row, auxc[1:2, :], auxc[2:3, :]).astype(jnp.int32)
    held = (names // 16) % 2 == core

    def both_picks(op, v):
        return op(v, jnp.where(even_row, pltpu.roll(v, 7, 0), pltpu.roll(v, 1, 0)))

    coefs = [CHX[k] for k in range(37)]
    turned = turns_of(coefs[0:19], [None] + coefs[19:36])
    scores = [precision * (v - coefs[36]) for v in turned]
    own_peak = both_picks(jnp.maximum, jnp.where(held, tree(jnp.maximum, scores), -1e30))
    weights = [jnp.where(held, jnp.exp(v - own_peak), 0.0) for v in scores]
    share = tree(add, weights)
    own_total = both_picks(add, share)
    PS[0:8] = own_peak
    PS[8:16] = own_total
    send(PS, PR, sibs.at[2], sibr.at[2], sib)
    for s in range(TURNS):
        high = weights[s].astype(BF16).astype(F32)
        rest = weights[s] - high
        for k in range(2):
            PT[k, s : s + 1, :] = high[k : k + 1]
            PT[k, 40 + s : 41 + s, :] = rest[k : k + 1]
            PT[k, 80 + s : 81 + s, :] = high[k : k + 1]
    own_t.wait()
    spectra = [dot_nn(TE[...], PT[k].astype(BF16)) for k in range(2)]
    arrived(PR, sibr.at[2])
    peak = jnp.maximum(own_peak, PR[0:8])
    own_part = jnp.exp(own_peak - peak)
    scale = own_part / (own_part * own_total + jnp.exp(PR[0:8] - peak) * PR[8:16])
    share = share * scale
    for k in range(2):
        H[k] = spectra[k] * scale[0:1]

    onehot = OH[...]

    def sums(x_half, second, mine):
        def step(v, carry):
            u = x_half * 8 + second * 4 + v
            out_lanes = pl.ds(pl.multiple_of(v * 256, 256), 256)
            upper = u // 9
            factors = [H[k, pl.ds(pl.multiple_of(u * 8, 8), 8), :] for k in range(2)]
            columns = [[], []]
            for part in range(2):
                rows = pl.ds(pl.multiple_of(upper * 128, 128), 128)
                tile = FI[2 * u + part - 18 * upper, rows, 0:128].astype(F32)
                for m in range(2):
                    real, imag = tile[m * 64 : m * 64 + 32], tile[m * 64 + 32 : m * 64 + 64]
                    for k in range(2):
                        at = (part * 2 + m) * 2
                        f_real, f_imag = factors[k][at : at + 1], factors[k][at + 1 : at + 2]
                        columns[k].append((real * f_real - imag * f_imag).astype(BF16))
                        columns[k].append((real * f_imag + imag * f_real).astype(BF16))
            rows_in = jnp.concatenate([jnp.concatenate(c, axis=0) for c in columns], axis=1)
            exact = dot_nt(onehot, rows_in)
            out = exact.astype(BF16)
            parts = [exact[q * 16 : q * 16 + 16] for q in range(8)]
            if second and mine:
                for n in range(4):
                    OB[n, :, out_lanes] = jnp.where(x_hi == 0, parts[n], parts[4 + n])
            if not second:
                for n in range(2):
                    four = parts[n * 4 : n * 4 + 4]
                    lower, upper_two = jnp.where(y == 0, four[0], four[1]), jnp.where(y == 2, four[2], four[3])
                    OA[n * 2 + x_half, :, out_lanes] = jnp.where(y < 2, lower, upper_two)
            for q in range(8):
                block = out[q * 16 : q * 16 + 16]
                if second:
                    SB[(q // 4) * 2 + x_half, q % 4, :, out_lanes] = block
                else:
                    SA[x_half, q % 4, q // 4, :, out_lanes] = block
            return carry

        lax.fori_loop(0, 4, step, 0, unroll=True)

    other = 1 - x_lo
    for pos, x_half in enumerate((x_lo, other)):
        sums(x_half, 1, pos == 0)
        for d in ((2,), (1, 3))[pos]:
            send(SB.at[(x + d) % 4], RB.at[d - 1], s1s.at[5 + d], s1r.at[5 + d], at_x(d))
        sums(x_half, 0, pos == 0)
        for d in (2, 1, 3):
            n = (1 - pos) * 3 + d - 1
            send(SA.at[x_half, (y + d) % 4], RA.at[d - 1, x_half], s1s.at[n], s1r.at[n], at_y(d))
    shares = jnp.concatenate(
        [jnp.broadcast_to(share[0:1], (8, 128)), jnp.broadcast_to(share[1:2], (8, 128))], axis=1
    )
    W0[...] = dot_nt(shares, onehot.astype(F32), precision=lax.Precision.HIGHEST)
    pl.semaphore_wait(tok.at[2], 2)
    for d in far_first:
        send(W0, RW0.at[d - 1], ws.at[d - 1], wr.at[d - 1], at_z(d))

    def block_scores(n, carry):
        run_peak, run_total = carry
        rows = pl.ds(pl.multiple_of(n * 8, 8), 8)
        f = [F[k, rows, :] for k in range(37)]
        turned = turns_of(f[0:19], [None] + f[19:36])
        scores = [precision * (v - f[36]) for v in turned]
        new_peak = jnp.maximum(run_peak, tree(jnp.maximum, scores))
        total = tree(add, [jnp.exp(v - new_peak) for v in scores])
        return new_peak, run_total * jnp.exp(run_peak - new_peak) + total

    start = (jnp.full((8, 128), -jnp.inf, F32), jnp.zeros((8, 128), F32))
    run_peak, run_total = lax.fori_loop(0, 16, block_scores, start)
    peak = jnp.max(run_peak, axis=0, keepdims=True)
    total = jnp.sum(run_total * jnp.exp(run_peak - peak), axis=0, keepdims=True)
    LS[0:8] = jnp.broadcast_to(peak, (8, 128))
    LS[8:16] = jnp.broadcast_to(total, (8, 128))
    send(LS, LR, sibs.at[3], sibr.at[3], sib)

    for pos, x_half in enumerate((other, x_lo)):
        for d in range(1, 4):
            arrived(RA.at[d - 1, x_half], s1r.at[pos * 3 + d - 1])
    for d in (2, 1, 3, 0):
        x_to = (x + d) % 4
        total = OA[x_to]
        for n in range(3):
            total = total + RA[n, x_to % 2, x_to // 2].astype(F32)
        if d:
            TAB[d - 1] = total.astype(BF16)
            send(TAB.at[d - 1], R2A.at[d - 1], s2s.at[d - 1], s2r.at[d - 1], at_x(d))
        else:
            TA[...] = total
    for d in range(1, 4):
        arrived(RB.at[d - 1], s1r.at[5 + d])
    for d in (2, 1, 3, 0):
        y_to = (y + d) % 4
        total = OB[y_to]
        for n in range(3):
            total = total + RB[n, y_to].astype(F32)
        if d:
            TBB[d - 1] = total.astype(BF16)
            send(TBB.at[d - 1], R2B.at[d - 1], s2s.at[2 + d], s2r.at[2 + d], at_y(d))
        else:
            TB[...] = total

    arrived(LR, sibr.at[3])
    peak = jnp.maximum(LS[0:8], LR[0:8])
    total = LS[8:16] * jnp.exp(LS[0:8] - peak) + LR[8:16] * jnp.exp(LR[0:8] - peak)
    evidence = peak + jnp.log(total)
    evid_out[...] = jnp.where(core == 0, evidence[0:1, 0:64], evidence[0:1, 64:128])

    for d in range(1, 16):
        arrived(RW0.at[d - 1], wr.at[d - 1])
    W1[...] = tree(add, [W0[...]] + [RW0[d] for d in range(15)])
    for d in range(1, 4):
        send(W1, RW1.at[d - 1], ws.at[14 + d], wr.at[14 + d], at_y(d))

    for d in range(1, 4):
        arrived(R2A.at[d - 1], s2r.at[d - 1])
    total = TA[...] + R2A[0].astype(F32) + R2A[1].astype(F32) + R2A[2].astype(F32)
    for n in range(8):
        UZ[n] = total[:, n * 128 : n * 128 + 128]
    for d in range(1, 4):
        arrived(R2B.at[d - 1], s2r.at[2 + d])
    total = TB[...] + R2B[0].astype(F32) + R2B[1].astype(F32) + R2B[2].astype(F32)
    for n in range(8):
        UZ[8 + n] = total[:, n * 128 : n * 128 + 128]
    SZ[...] = UZ[...].astype(BF16)
    for d in far_first:
        send(SZ.at[(z + d) % 16], RZ.at[d - 1], zs.at[d - 1], zr.at[d - 1], at_z(d))

    for d in range(1, 4):
        arrived(RW1.at[d - 1], wr.at[14 + d])
    W2[...] = tree(add, [W1[...]] + [RW1[d] for d in range(3)])
    for d in range(1, 4):
        send(W2, RW2.at[d - 1], ws.at[17 + d], wr.at[17 + d], at_x(d))

    for d in range(1, 4):
        arrived(RW2.at[d - 1], wr.at[17 + d])
    weight = tree(add, [W2[...]] + [RW2[d] for d in range(3)])
    pick = lane[0:16] == row[0:16] + q_me * 16
    weight = jnp.sum(jnp.where(pick, jnp.broadcast_to(weight[0:1], (16, 128)), 0.0), axis=1, keepdims=True)
    for copy in sent:
        copy.wait_send()
    for d in range(1, 16):
        arrived(RZ.at[d - 1], zr.at[d - 1])
    total = tree(add, [UZ[z]] + [RZ[d].astype(F32) for d in range(15)])
    avg_out[...] = total / (1.0 + weight)


def body(images, references, precision, candidates):
    table = jnp.asarray(factor_table())
    anywhere = pl.BlockSpec(memory_space=pltpu.HBM)
    vmem = pl.BlockSpec(memory_space=pltpu.VMEM)
    dma = pltpu.SemaphoreType.DMA
    scratch = [
        pltpu.VMEM((128, 4096), BF16),
        pltpu.VMEM((128, 4096), BF16),
        pltpu.VMEM((18, 256, 256), BF16),
        pltpu.VMEM((37, 128, 128), F32),
        pltpu.VMEM((1, 64), F32),
        pltpu.VMEM((2, 64), jnp.int32),
        pltpu.VMEM((8, 128), F32),
        pltpu.VMEM((8, 128), F32),
        pltpu.VMEM((37, 8, 128), F32),
        pltpu.VMEM((16, 128), F32),
        pltpu.VMEM((16, 128), F32),
        pltpu.VMEM((2, 128, 128), F32),
        pltpu.VMEM((2, 128, 128), F32),
        pltpu.VMEM((128, 128), BF16),
        pltpu.VMEM((128, 256), BF16),
        pltpu.VMEM((2, 4, 2, 16, 1024), BF16),
        pltpu.VMEM((3, 2, 2, 16, 1024), BF16),
        pltpu.VMEM((4, 4, 16, 1024), BF16),
        pltpu.VMEM((3, 4, 16, 1024), BF16),
        pltpu.VMEM((16, 1024), F32),
        pltpu.VMEM((3, 16, 1024), BF16),
        pltpu.VMEM((3, 16, 1024), BF16),
        pltpu.VMEM((16, 1024), F32),
        pltpu.VMEM((3, 16, 1024), BF16),
        pltpu.VMEM((3, 16, 1024), BF16),
        pltpu.VMEM((4, 16, 1024), F32),
        pltpu.VMEM((4, 16, 1024), F32),
        pltpu.VMEM((16, 16, 128), F32),
        pltpu.VMEM((16, 16, 128), BF16),
        pltpu.VMEM((15, 16, 128), BF16),
        pltpu.VMEM((8, 128), F32),
        pltpu.VMEM((15, 8, 128), F32),
        pltpu.VMEM((8, 128), F32),
        pltpu.VMEM((3, 8, 128), F32),
        pltpu.VMEM((8, 128), F32),
        pltpu.VMEM((3, 8, 128), F32),
        pltpu.VMEM((16, 128), F32),
        pltpu.VMEM((16, 128), F32),
        dma((5,)),
        pltpu.SemaphoreType.REGULAR((3,)),
        dma((25,)),
        dma((8, 4)),
        dma((4,)),
        dma((4,)),
        dma((9,)),
        dma((9,)),
        dma((6,)),
        dma((6,)),
        dma((15,)),
        dma((15,)),
        dma((21,)),
        dma((21,)),
    ]
    average, evidence = pl.pallas_call(
        kernel,
        out_shape=(jax.ShapeDtypeStruct((16, 128), F32), jax.ShapeDtypeStruct((1, 64), F32)),
        in_specs=[anywhere] * 5,
        out_specs=(vmem, vmem),
        scratch_shapes=scratch,
        compiler_params=pltpu.CompilerParams(
            collective_id=0, has_side_effects=True, vmem_limit_bytes=55200 * 1024
        ),
    )(images, references, precision.reshape(1, 64), candidates.T, table)
    return average, evidence.reshape(64)


def solution(mesh):
    in_specs = (P(("img", "blk"), None), P("blk", None), P(("img", "blk")), P(("img", "blk"), None))
    out_specs = (P("blk", "img"), P(("img", "blk")))
    return jax.shard_map(body, mesh=mesh, in_specs=in_specs, out_specs=out_specs, check_vma=False)
```

```python
import math

import jax
import jax.numpy as jnp
import ml_dtypes
import numpy as np
from jax import lax
from jax.experimental import pallas as pl
from jax.experimental.pallas import tpu as pltpu
from jax.sharding import PartitionSpec as P

CYCLES = 32
ORDERS = 64
TURNS = 36
FEATS = 4096
LANES = 128
MESH = pl.DeviceIdType.MESH
F32 = jnp.float32
BF16 = jnp.bfloat16


def factor_table():
    turns = np.arange(TURNS)
    angle = 2.0 * math.pi / TURNS * ((np.arange(ORDERS)[:, None] * turns[None, :]) % TURNS)
    values = np.stack([np.cos(angle), -np.sin(angle)], axis=1).reshape(2 * ORDERS, TURNS).astype(np.float32)
    high = values.astype(ml_dtypes.bfloat16).astype(np.float32)
    out = np.zeros((128, 128), np.float32)
    out[:, 0:36] = high
    out[:, 40:76] = high
    out[:, 80:116] = values - high
    return out.astype(ml_dtypes.bfloat16)


def weighted(pairs):
    total = None
    for coef, value in pairs:
        if abs(coef) < 1e-12:
            continue
        if abs(coef - 1.0) < 1e-12:
            term = value
        elif abs(coef + 1.0) < 1e-12:
            term = -value
        else:
            term = value * np.float32(coef)
        total = term if total is None else total + term
    return total


def turns_of(a, b):
    def cos(k, s):
        return math.cos(2.0 * math.pi * (k * s % 36) / 36.0)

    def sin(k, s):
        return math.sin(2.0 * math.pi * (k * s % 36) / 36.0)

    even_c, odd_c, even_s, odd_s = {}, {}, {}, {}
    for s in range(5):
        p = weighted([(cos(k, s), a[k]) for k in range(0, 19, 4)])
        q = weighted([(cos(k, s), a[k]) for k in range(2, 19, 4)])
        even_c[s], even_c[9 - s] = p + q, p - q
    for s in range(9):
        odd_c[s] = weighted([(cos(k, s), a[k]) for k in range(1, 18, 2)])
    for s in range(1, 5):
        p = weighted([(sin(k, s), b[k]) for k in range(4, 17, 4)])
        q = weighted([(sin(k, s), b[k]) for k in range(2, 17, 4)])
        even_s[s], even_s[9 - s] = p + q, q - p
    for s in range(1, 10):
        odd_s[s] = weighted([(sin(k, s), b[k]) for k in range(1, 18, 2)])
    x = [None] * 36
    for s in range(10):
        if s < 9:
            c_lo, c_hi = even_c[s] + odd_c[s], even_c[s] - odd_c[s]
        else:
            c_lo = c_hi = even_c[9]
        if s == 0:
            x[0], x[18] = c_lo, c_hi
        elif s == 9:
            x[9], x[27] = c_lo - odd_s[9], c_lo + odd_s[9]
        else:
            s_lo, s_hi = even_s[s] + odd_s[s], odd_s[s] - even_s[s]
            x[s], x[36 - s] = c_lo - s_lo, c_lo + s_lo
            x[18 - s], x[18 + s] = c_hi - s_hi, c_hi + s_hi
    return x


def tree(op, values):
    values = list(values)
    while len(values) > 1:
        nxt = [op(values[i], values[i + 1]) for i in range(0, len(values) - 1, 2)]
        if len(values) % 2:
            nxt.append(values[-1])
        values = nxt
    return values[0]


def add(p, q):
    return p + q


def dot_nt(a, b, **kw):
    return lax.dot_general(a, b, (((1,), (1,)), ((), ())), preferred_element_type=F32, **kw)


def dot_nn(a, b):
    return jnp.dot(a, b, preferred_element_type=F32)


def kernel(
    images, refs, prec, cand, table, avg_out, evid_out,
    G, IM, FI, F, PIN, CIN, AUX, AUXS, CHX, PS, PR, PT, H, TE, OH, SA, RA, SB, RB, TA, TAB, R2A, TB, TBB, R2B,
    OA, OB, UZ, SZ, RZ, W0, RW0, W1, RW1, W2, RW2, LS, LR,
    loc, tok, ags, agr, sibs, sibr, s1s, s1r, s2s, s2r, zs, zr, ws, wr,
):
    img, blk = lax.axis_index("img"), lax.axis_index("blk")
    z, x_lo = img % 16, img // 16
    core, y, x_hi = blk % 2, (blk // 2) % 4, blk // 8
    x = x_hi * 2 + x_lo
    q_me = x_hi * 4 + y

    def dev(x_, y_, z_, c_):
        return ((x_ % 2) * 16 + z_, (x_ // 2) * 8 + y_ * 2 + c_)

    sib = dev(x, y, z, 1 - core)
    x_opp, x_same = 3 - x, x_hi * 2 + 1 - x_lo
    def at_z_of(d):
        return dev(x, y, (z + d) % 16, core)

    same, z_up, z_dn = dev(x_same, y, z, core), at_z_of(1), at_z_of(15)

    def at_y(d):
        return dev(x, (y + d) % 4, z, core)

    def at_x(d):
        return dev((x + d) % 4, y, z, core)

    def at_z(d):
        return dev(x, y, (z + d) % 16, core)

    sent = []
    far_first = sorted(range(1, 16), key=lambda d: -min(d, 16 - d))

    def send(src, dst, ssem, rsem, to):
        copy = pltpu.make_async_remote_copy(
            src_ref=src, dst_ref=dst, send_sem=ssem, recv_sem=rsem, device_id=to, device_id_type=MESH
        )
        copy.start()
        sent.append(copy)

    def arrived(dst, rsem):
        pltpu.make_async_copy(dst, dst, rsem).wait()

    mine_rows = pl.ds(pl.multiple_of(core * 64, 64), 64)
    own_p = pltpu.make_async_copy(prec, PIN, loc.at[3])
    own_p.start()
    own_c = pltpu.make_async_copy(cand, CIN, loc.at[4])
    own_c.start()
    own_g = pltpu.make_async_copy(refs, G.at[pl.ds(pl.multiple_of(q_me * 16, 16), 16)], loc.at[1])
    own_g.start()
    own_im = pltpu.make_async_copy(images, IM.at[mine_rows], loc.at[0])
    own_im.start()
    own_t = pltpu.make_async_copy(table, TE, loc.at[2])
    own_t.start()

    barrier = pltpu.get_barrier_semaphore()
    partners = [dev(x_opp, (y + d) % 4, z, core) for d in range(1, 4)]
    partners += [at_y(d) for d in range(1, 4)] + [at_x(d) for d in range(1, 4)]
    partners += [z_up, z_dn, sib]
    for to in partners:
        pl.semaphore_signal(barrier, inc=1, device_id=to, device_id_type=MESH)
    own_p.wait()
    own_c.wait()
    mine = jnp.concatenate([PIN[...], CIN[...].astype(F32)], axis=0)
    AUX[0:3, :] = jnp.concatenate([mine, mine], axis=1)
    AUX[3:8, :] = jnp.zeros((5, 128), F32)
    pl.semaphore_wait(barrier, len(partners))

    def token(n):
        for d in (1 << n, 16 - (1 << n)):
            pl.semaphore_signal(tok.at[n], inc=1, device_id=at_z(d), device_id_type=MESH)

    def rows_at(q):
        return pl.ds(pl.multiple_of(q * 16, 16), 16)

    def quarter(q, n):
        return G.at[rows_at(q), pl.ds(pl.multiple_of(n * 1024, 1024), 1024)]

    mine_f = (z + 2 * x_lo) % 4
    same_f, up_f, dn_f = (mine_f + 2) % 4, (mine_f + 1) % 4, (mine_f + 3) % 4
    col, far = x_hi * 4, (1 - x_hi) * 4
    order = (0, 1, 3, 2)

    def near_q(d):
        return col + (y + d) % 4

    def far_q(d):
        return far + (y + d) % 4

    send(AUX, AUXS, sibs.at[1], sibr.at[1], sib)
    opp_quarter = refs.at[:, pl.ds(pl.multiple_of(same_f * 1024, 1024), 1024)]
    for n, d in enumerate(order):
        to = dev(x_opp, (y + d) % 4, z, core)
        send(opp_quarter, quarter(q_me, same_f), ags.at[n], agr.at[q_me, same_f], to)
    for n, d in enumerate((1, 3, 2)):
        send(refs, G.at[rows_at(q_me)], ags.at[4 + n], agr.at[q_me, 0], at_y(d))
    send(images, IM.at[mine_rows], sibs.at[0], sibr.at[0], sib)
    token(0)
    own_im.wait()
    arrived(IM.at[pl.ds(pl.multiple_of((1 - core) * 64, 64), 64)], sibr.at[0])
    arrived(AUXS, sibr.at[1])

    row = lax.broadcasted_iota(jnp.int32, (128, 128), 0)
    lane = lax.broadcasted_iota(jnp.int32, (128, 128), 1)

    def swap(src, dst):
        first = dst % 64 < 32
        return jnp.where(first & (src == dst + 32), 1.0, jnp.where((~first) & (src == dst - 32), -1.0, 0.0))

    eye = jnp.where(row == lane, 1.0, 0.0)
    rows_of = jnp.concatenate([eye, swap(lane, row)], axis=0).astype(BF16)

    def prepare(first, count, half):
        def step(n, carry):
            t = first + n
            block = IM[:, pl.ds(pl.multiple_of(t * 128, 128), 128)]
            both = dot_nt(rows_of, block)
            j = t - 18 * half
            sign = jnp.where(j < 9, 1.0, -1.0).astype(F32)
            FI[j, half * 128 : half * 128 + 128, 0:128] = both[0:128].astype(BF16)
            FI[j, half * 128 : half * 128 + 128, 128:256] = (both[128:256] * sign).astype(BF16)
            return carry

        lax.fori_loop(0, count, step, 0, unroll=2)

    def hand_far(n):
        q = far_q(order[n])
        part, sem = quarter(q, mine_f), agr.at[q, mine_f]
        arrived(part, sem)
        for m, to in enumerate((same, z_up, z_dn)):
            send(part, part, ags.at[13 + 3 * n + m], sem, to)

    prepare(0, 4, 0)
    hand_far(0)
    prepare(4, 2, 0)
    hand_far(1)
    hand_far(2)
    prepare(6, 2, 0)
    hand_far(3)
    pl.semaphore_wait(tok.at[0], 2)
    token(1)
    prepare(8, 10, 0)
    prepare(18, 14, 1)

    right = lax.broadcasted_iota(jnp.int32, (8, 128), 1) >= 64
    auxc = jnp.where(right == (core == 1), AUX[...], AUXS[...])
    precision = auxc[0:1, :]
    class_id = ((row // 16) * 32 + core * 16 + row % 16).astype(F32)
    picks = [auxc[1:2, :] == class_id, auxc[2:3, :] == class_id]
    for k in range(2):
        OH[:, k * 128 : k * 128 + 128] = jnp.where(picks[k], 1.0, 0.0).astype(BF16)
    PT[...] = jnp.zeros_like(PT)

    own_g.wait()
    for d in (1, 3, 2):
        q = near_q(d)
        arrived(G.at[rows_at(q)], agr.at[q, 0])

    low = (lax.broadcasted_iota(jnp.int32, (64, 256), 1) % 128) < 64

    def harmonics(first):
        rows = pl.ds(pl.multiple_of(first * 16, 64), 64)
        for j in range(18):
            left = G[rows, j * 128 : j * 128 + 128]
            if j < 14:
                tile = jnp.concatenate([left, G[rows, (18 + j) * 128 : (18 + j) * 128 + 128]], axis=1)
                keep, right_side = low, FI[j]
            else:
                tile, keep, right_side = left, low[:, 0:128], FI[j, 0:128, :]
            zero = jnp.zeros_like(tile)
            stacked = jnp.concatenate([jnp.where(keep, tile, zero), jnp.where(keep, zero, tile)], axis=0)
            out = dot_nn(stacked, right_side)
            even, odd = out[0:64], out[64:128]
            k_even, k_odd = (2 * j if j <= 9 else 36 - 2 * j), (2 * j + 1 if j <= 8 else 35 - 2 * j)
            if j <= 9:
                F[k_even, rows, :] = even[:, 0:128]
            else:
                F[k_even, rows, :] += even[:, 0:128]
            if 0 < k_even < 18:
                if j <= 9:
                    F[18 + k_even, rows, :] = even[:, 128:256]
                else:
                    F[18 + k_even, rows, :] += even[:, 128:256]
            if j <= 8:
                F[k_odd, rows, :] = odd[:, 0:128]
                F[18 + k_odd, rows, :] = odd[:, 128:256]
            else:
                F[k_odd, rows, :] += odd[:, 0:128]
                F[18 + k_odd, rows, :] += odd[:, 128:256]
        square = jnp.zeros((64, 128), F32)
        for t in range(32):
            value = G[rows, t * 128 : t * 128 + 128].astype(F32)
            square = square + value * value
        F[36, rows, :] = jnp.broadcast_to(0.5 * jnp.sum(square, axis=1, keepdims=True), (64, 128))

    even_row = lax.broadcasted_iota(jnp.int32, (8, 128), 0) % 2 == 0

    def choose(first, more):
        rows = pl.ds(pl.multiple_of(first * 16, 64), 64)
        ids = (((row[0:64] // 16) + first) * 32 + core * 16 + row[0:64] % 16).astype(F32)
        keep = [auxc[k : k + 1, :] == ids for k in (1, 2)]

        def step(kk, carry):
            f = F[kk, rows, :]
            parts = []
            for k in range(2):
                kept = jnp.where(keep[k], f, 0.0)
                total = tree(add, [kept[n * 8 : n * 8 + 8] for n in range(8)])
                parts.append(total + pltpu.roll(total, 1, 0))
            both = jnp.where(even_row, parts[0], parts[1])
            both = both + pltpu.roll(both, 2, 0)
            both = both + pltpu.roll(both, 4, 0)
            CHX[kk] = CHX[kk] + both if more else both
            return carry

        lax.fori_loop(0, 36, step, 0, unroll=4)
        step(36, 0)

    harmonics(col)
    choose(col, False)
    pl.semaphore_wait(tok.at[1], 2)
    token(2)
    for d in order:
        for f in (same_f, up_f, dn_f):
            arrived(quarter(far_q(d), f), agr.at[far_q(d), f])
    harmonics(far)
    choose(far, True)
    names = jnp.where(even_row, auxc[1:2, :], auxc[2:3, :]).astype(jnp.int32)
    held = (names // 16) % 2 == core

    def both_picks(op, v):
        return op(v, jnp.where(even_row, pltpu.roll(v, 7, 0), pltpu.roll(v, 1, 0)))

    coefs = [CHX[k] for k in range(37)]
    turned = turns_of(coefs[0:19], [None] + coefs[19:36])
    scores = [precision * (v - coefs[36]) for v in turned]
    own_peak = both_picks(jnp.maximum, jnp.where(held, tree(jnp.maximum, scores), -1e30))
    weights = [jnp.where(held, jnp.exp(v - own_peak), 0.0) for v in scores]
    share = tree(add, weights)
    own_total = both_picks(add, share)
    PS[0:8] = own_peak
    PS[8:16] = own_total
    send(PS, PR, sibs.at[2], sibr.at[2], sib)
    for s in range(TURNS):
        high = weights[s].astype(BF16).astype(F32)
        rest = weights[s] - high
        for k in range(2):
            PT[k, s : s + 1, :] = high[k : k + 1]
            PT[k, 40 + s : 41 + s, :] = rest[k : k + 1]
            PT[k, 80 + s : 81 + s, :] = high[k : k + 1]
    own_t.wait()
    spectra = [dot_nn(TE[...], PT[k].astype(BF16)) for k in range(2)]
    arrived(PR, sibr.at[2])
    peak = jnp.maximum(own_peak, PR[0:8])
    own_part = jnp.exp(own_peak - peak)
    scale = own_part / (own_part * own_total + jnp.exp(PR[0:8] - peak) * PR[8:16])
    share = share * scale
    for k in range(2):
        H[k] = spectra[k] * scale[0:1]

    onehot = OH[...]

    def sums(x_half, second, mine):
        def step(v, carry):
            u = x_half * 8 + second * 4 + v
            out_lanes = pl.ds(pl.multiple_of(v * 256, 256), 256)
            upper = u // 9
            factors = [H[k, pl.ds(pl.multiple_of(u * 8, 8), 8), :] for k in range(2)]
            columns = [[], []]
            for part in range(2):
                rows = pl.ds(pl.multiple_of(upper * 128, 128), 128)
                tile = FI[2 * u + part - 18 * upper, rows, 0:128].astype(F32)
                for m in range(2):
                    real, imag = tile[m * 64 : m * 64 + 32], tile[m * 64 + 32 : m * 64 + 64]
                    for k in range(2):
                        at = (part * 2 + m) * 2
                        f_real, f_imag = factors[k][at : at + 1], factors[k][at + 1 : at + 2]
                        columns[k].append((real * f_real - imag * f_imag).astype(BF16))
                        columns[k].append((real * f_imag + imag * f_real).astype(BF16))
            rows_in = jnp.concatenate([jnp.concatenate(c, axis=0) for c in columns], axis=1)
            exact = dot_nt(onehot, rows_in)
            out = exact.astype(BF16)
            parts = [exact[q * 16 : q * 16 + 16] for q in range(8)]
            if second and mine:
                for n in range(4):
                    OB[n, :, out_lanes] = jnp.where(x_hi == 0, parts[n], parts[4 + n])
            if not second:
                for n in range(2):
                    four = parts[n * 4 : n * 4 + 4]
                    lower, upper_two = jnp.where(y == 0, four[0], four[1]), jnp.where(y == 2, four[2], four[3])
                    OA[n * 2 + x_half, :, out_lanes] = jnp.where(y < 2, lower, upper_two)
            for q in range(8):
                block = out[q * 16 : q * 16 + 16]
                if second:
                    SB[(q // 4) * 2 + x_half, q % 4, :, out_lanes] = block
                else:
                    SA[x_half, q % 4, q // 4, :, out_lanes] = block
            return carry

        lax.fori_loop(0, 4, step, 0, unroll=True)

    other = 1 - x_lo
    for pos, x_half in enumerate((x_lo, other)):
        sums(x_half, 1, pos == 0)
        for d in ((2,), (1, 3))[pos]:
            send(SB.at[(x + d) % 4], RB.at[d - 1], s1s.at[5 + d], s1r.at[5 + d], at_x(d))
        sums(x_half, 0, pos == 0)
        for d in (2, 1, 3):
            n = (1 - pos) * 3 + d - 1
            send(SA.at[x_half, (y + d) % 4], RA.at[d - 1, x_half], s1s.at[n], s1r.at[n], at_y(d))
    shares = jnp.concatenate(
        [jnp.broadcast_to(share[0:1], (8, 128)), jnp.broadcast_to(share[1:2], (8, 128))], axis=1
    )
    W0[...] = dot_nt(shares, onehot.astype(F32), precision=lax.Precision.HIGHEST)
    pl.semaphore_wait(tok.at[2], 2)
    for d in far_first:
        send(W0, RW0.at[d - 1], ws.at[d - 1], wr.at[d - 1], at_z(d))

    def block_scores(n, carry):
        run_peak, run_total = carry
        rows = pl.ds(pl.multiple_of(n * 8, 8), 8)
        f = [F[k, rows, :] for k in range(37)]
        turned = turns_of(f[0:19], [None] + f[19:36])
        scores = [precision * (v - f[36]) for v in turned]
        new_peak = jnp.maximum(run_peak, tree(jnp.maximum, scores))
        total = tree(add, [jnp.exp(v - new_peak) for v in scores])
        return new_peak, run_total * jnp.exp(run_peak - new_peak) + total

    start = (jnp.full((8, 128), -jnp.inf, F32), jnp.zeros((8, 128), F32))
    run_peak, run_total = lax.fori_loop(0, 16, block_scores, start)
    peak = jnp.max(run_peak, axis=0, keepdims=True)
    total = jnp.sum(run_total * jnp.exp(run_peak - peak), axis=0, keepdims=True)
    LS[0:8] = jnp.broadcast_to(peak, (8, 128))
    LS[8:16] = jnp.broadcast_to(total, (8, 128))
    send(LS, LR, sibs.at[3], sibr.at[3], sib)

    for pos, x_half in enumerate((other, x_lo)):
        for d in range(1, 4):
            arrived(RA.at[d - 1, x_half], s1r.at[pos * 3 + d - 1])
    for d in (2, 1, 3, 0):
        x_to = (x + d) % 4
        total = OA[x_to]
        for n in range(3):
            total = total + RA[n, x_to % 2, x_to // 2].astype(F32)
        if d:
            TAB[d - 1] = total.astype(BF16)
            send(TAB.at[d - 1], R2A.at[d - 1], s2s.at[d - 1], s2r.at[d - 1], at_x(d))
        else:
            TA[...] = total
    for d in range(1, 4):
        arrived(RB.at[d - 1], s1r.at[5 + d])
    for d in (2, 1, 3, 0):
        y_to = (y + d) % 4
        total = OB[y_to]
        for n in range(3):
            total = total + RB[n, y_to].astype(F32)
        if d:
            TBB[d - 1] = total.astype(BF16)
            send(TBB.at[d - 1], R2B.at[d - 1], s2s.at[2 + d], s2r.at[2 + d], at_y(d))
        else:
            TB[...] = total

    arrived(LR, sibr.at[3])
    peak = jnp.maximum(LS[0:8], LR[0:8])
    total = LS[8:16] * jnp.exp(LS[0:8] - peak) + LR[8:16] * jnp.exp(LR[0:8] - peak)
    evidence = peak + jnp.log(total)
    evid_out[...] = jnp.where(core == 0, evidence[0:1, 0:64], evidence[0:1, 64:128])

    for d in range(1, 16):
        arrived(RW0.at[d - 1], wr.at[d - 1])
    W1[...] = tree(add, [W0[...]] + [RW0[d] for d in range(15)])
    for d in range(1, 4):
        send(W1, RW1.at[d - 1], ws.at[14 + d], wr.at[14 + d], at_y(d))

    for d in range(1, 4):
        arrived(R2A.at[d - 1], s2r.at[d - 1])
    total = TA[...] + R2A[0].astype(F32) + R2A[1].astype(F32) + R2A[2].astype(F32)
    for n in range(8):
        UZ[n] = total[:, n * 128 : n * 128 + 128]
    for d in range(1, 4):
        arrived(R2B.at[d - 1], s2r.at[2 + d])
    total = TB[...] + R2B[0].astype(F32) + R2B[1].astype(F32) + R2B[2].astype(F32)
    for n in range(8):
        UZ[8 + n] = total[:, n * 128 : n * 128 + 128]
    SZ[...] = UZ[...].astype(BF16)
    for d in far_first:
        send(SZ.at[(z + d) % 16], RZ.at[d - 1], zs.at[d - 1], zr.at[d - 1], at_z(d))

    for d in range(1, 4):
        arrived(RW1.at[d - 1], wr.at[14 + d])
    W2[...] = tree(add, [W1[...]] + [RW1[d] for d in range(3)])
    for d in range(1, 4):
        send(W2, RW2.at[d - 1], ws.at[17 + d], wr.at[17 + d], at_x(d))

    for d in range(1, 4):
        arrived(RW2.at[d - 1], wr.at[17 + d])
    weight = tree(add, [W2[...]] + [RW2[d] for d in range(3)])
    pick = lane[0:16] == row[0:16] + q_me * 16
    weight = jnp.sum(jnp.where(pick, jnp.broadcast_to(weight[0:1], (16, 128)), 0.0), axis=1, keepdims=True)
    for copy in sent:
        copy.wait_send()
    for d in range(1, 16):
        arrived(RZ.at[d - 1], zr.at[d - 1])
    total = tree(add, [UZ[z]] + [RZ[d].astype(F32) for d in range(15)])
    avg_out[...] = total / (1.0 + weight)


def body(images, references, precision, candidates):
    table = jnp.asarray(factor_table())
    anywhere = pl.BlockSpec(memory_space=pltpu.HBM)
    vmem = pl.BlockSpec(memory_space=pltpu.VMEM)
    dma = pltpu.SemaphoreType.DMA
    scratch = [
        pltpu.VMEM((128, 4096), BF16),
        pltpu.VMEM((128, 4096), BF16),
        pltpu.VMEM((18, 256, 256), BF16),
        pltpu.VMEM((37, 128, 128), F32),
        pltpu.VMEM((1, 64), F32),
        pltpu.VMEM((2, 64), jnp.int32),
        pltpu.VMEM((8, 128), F32),
        pltpu.VMEM((8, 128), F32),
        pltpu.VMEM((37, 8, 128), F32),
        pltpu.VMEM((16, 128), F32),
        pltpu.VMEM((16, 128), F32),
        pltpu.VMEM((2, 128, 128), F32),
        pltpu.VMEM((2, 128, 128), F32),
        pltpu.VMEM((128, 128), BF16),
        pltpu.VMEM((128, 256), BF16),
        pltpu.VMEM((2, 4, 2, 16, 1024), BF16),
        pltpu.VMEM((3, 2, 2, 16, 1024), BF16),
        pltpu.VMEM((4, 4, 16, 1024), BF16),
        pltpu.VMEM((3, 4, 16, 1024), BF16),
        pltpu.VMEM((16, 1024), F32),
        pltpu.VMEM((3, 16, 1024), BF16),
        pltpu.VMEM((3, 16, 1024), BF16),
        pltpu.VMEM((16, 1024), F32),
        pltpu.VMEM((3, 16, 1024), BF16),
        pltpu.VMEM((3, 16, 1024), BF16),
        pltpu.VMEM((4, 16, 1024), F32),
        pltpu.VMEM((4, 16, 1024), F32),
        pltpu.VMEM((16, 16, 128), F32),
        pltpu.VMEM((16, 16, 128), BF16),
        pltpu.VMEM((15, 16, 128), BF16),
        pltpu.VMEM((8, 128), F32),
        pltpu.VMEM((15, 8, 128), F32),
        pltpu.VMEM((8, 128), F32),
        pltpu.VMEM((3, 8, 128), F32),
        pltpu.VMEM((8, 128), F32),
        pltpu.VMEM((3, 8, 128), F32),
        pltpu.VMEM((16, 128), F32),
        pltpu.VMEM((16, 128), F32),
        dma((5,)),
        pltpu.SemaphoreType.REGULAR((3,)),
        dma((25,)),
        dma((8, 4)),
        dma((4,)),
        dma((4,)),
        dma((9,)),
        dma((9,)),
        dma((6,)),
        dma((6,)),
        dma((15,)),
        dma((15,)),
        dma((21,)),
        dma((21,)),
    ]
    average, evidence = pl.pallas_call(
        kernel,
        out_shape=(jax.ShapeDtypeStruct((16, 128), F32), jax.ShapeDtypeStruct((1, 64), F32)),
        in_specs=[anywhere] * 5,
        out_specs=(vmem, vmem),
        scratch_shapes=scratch,
        compiler_params=pltpu.CompilerParams(
            collective_id=0, has_side_effects=True, vmem_limit_bytes=55200 * 1024
        ),
    )(images, references, precision.reshape(1, 64), candidates.T, table)
    return average, evidence.reshape(64)


def solution(mesh):
    in_specs = (P(("img", "blk"), None), P("blk", None), P(("img", "blk")), P(("img", "blk"), None))
    out_specs = (P("blk", "img"), P(("img", "blk")))
    return jax.shard_map(body, mesh=mesh, in_specs=in_specs, out_specs=out_specs, check_vma=False)
```
